256 devices in a mesh: dp: 8 (over z), cent: 32 (over y, x, core).
Axes of the slice: x: 4, y: 4, z: 8, core: 2. Of those that a mesh axis runs over, the one named last changes fastest.
Arguments:
- embeddings: bfloat16 [16384, 768], P(('dp', 'cent')), may hold values from -8 to 8
- centroids: bfloat16 [65536, 768], P('cent'), may hold values from -3 to 3
Outputs:
- new_centroids: bfloat16 [65536, 768], P('cent')
The draws below stay inside these ranges and needn't reach their ends.
All inputs are finite; a program needn't handle non-finite values.
Results may differ from the reference program's by a relative error of at most 0.0038.
Values may be sent and summed in bfloat16 or wider, within the bound.
No kernel may reach another device: no remote copies, remote signals or barrier semaphores. Data moves between devices by JAX's collectives and lax.ppermute only.
A program may use at most 128 MiB of HBM per device.

```python
import math
import jax
import jax.numpy as jnp
from jax import lax

D = 768
K_DEV = 2048
ITERS = 2
NDOC = 16384
NCENT = 65536


def draw_embeddings(key, part):
    values = jnp.clip(jax.random.normal(jax.random.fold_in(key, 1), (NDOC, D)), -6.0, 6.0)
    return values.astype(jnp.bfloat16)


def draw_centroids(key, part):
    width_scale = D ** (-0.5)
    values = jnp.clip(jax.random.normal(jax.random.fold_in(key, 11), (NCENT, D)), -6.0, 6.0) * width_scale
    return values.astype(jnp.bfloat16)


def setup_inputs(seed: int = 0) -> dict:
    streams_of = jax.random.split(jax.random.key(seed), 3)
    embeddings = draw_embeddings(jax.random.fold_in(streams_of[2], 71), 0)
    centroids = draw_centroids(jax.random.fold_in(streams_of[2], 71), 0)
    return {"embeddings": embeddings, "centroids": centroids}


def block_logits(embeddings, block):
    return 3.0 * jnp.dot(embeddings, block.T, preferred_element_type=jnp.float32)


def reference(embeddings, centroids):
    blocks = centroids.reshape(NCENT // K_DEV, K_DEV, D)
    log_ratio = math.log(NDOC / NCENT)
    row_pot = jnp.zeros((NDOC,), jnp.float32)
    col_pot = jnp.zeros((NCENT // K_DEV, K_DEV), jnp.float32)
    for repeat in range(ITERS):
        def sweep(carry, block):
            peak, total = carry
            logits = block_logits(embeddings, block)
            shifted = logits + row_pot[:, None]
            col_peak = jnp.max(shifted, axis=0)
            col_here = log_ratio - (col_peak + jnp.log(jnp.sum(jnp.exp(shifted - col_peak[None, :]), axis=0)))
            moved = logits + col_here[None, :]
            block_peak = jnp.max(moved, axis=1)
            new_peak = jnp.maximum(peak, block_peak)
            total = total * jnp.exp(peak - new_peak) + jnp.sum(jnp.exp(moved - new_peak[:, None]), axis=1)
            return (new_peak, total), col_here

        start = (jnp.full((NDOC,), -jnp.inf, jnp.float32), jnp.zeros((NDOC,), jnp.float32))
        (peak, total), col_pot = lax.scan(sweep, start, blocks)
        row_pot = -(peak + jnp.log(total))

    def finish(carry, inputs):
        block, col_here = inputs
        logits = block_logits(embeddings, block)
        plan = jnp.exp(logits + row_pot[:, None] + col_here[None, :]).astype(jnp.bfloat16)
        sums = jnp.dot(plan.T, embeddings, preferred_element_type=jnp.float32)
        mass = jnp.sum(plan.astype(jnp.float32), axis=0)
        return carry, (sums / mass[:, None]).astype(jnp.bfloat16)

    unused, updated = lax.scan(finish, jnp.zeros((), jnp.float32), (blocks, col_pot))
    return updated.reshape(NCENT, D)
```

```python
import functools
import math

import jax
import jax.numpy as jnp
from jax import lax
from jax.experimental import pallas as pl
from jax.experimental.pallas import tpu as pltpu
from jax.sharding import PartitionSpec as P

f32 = jnp.float32
bf16 = jnp.bfloat16
LANES = 128
BLOCK = 256
CHUNK = 16
SCALE = 3.0
SMALL_SUM = 1e-20
LARGE_POT = 46.0
NT = (((1,), (1,)), ((), ()))


def eye():
    rows = lax.broadcasted_iota(jnp.int32, (LANES, LANES), 0)
    cols = lax.broadcasted_iota(jnp.int32, (LANES, LANES), 1)
    return rows == cols


def to_row(column):
    return jnp.sum(jnp.where(eye(), column, 0.0), axis=0, keepdims=True)


def to_column(row):
    return jnp.sum(jnp.where(eye(), row, 0.0), axis=1, keepdims=True)


def fold(x, op):
    out = x[:, :LANES]
    for at in range(LANES, x.shape[1], LANES):
        out = op(out, x[:, at : at + LANES])
    return out


def merge(parts):
    peak = jnp.max(parts, axis=0)
    return peak + jnp.log(jnp.sum(jnp.exp(parts - peak[None]), axis=0))


def logits_block(cents, docs_ref, out_ref, rows):
    width = 512
    for at in range(0, docs_ref.shape[0], width):
        out_ref[rows, at : at + width] = lax.dot_general(
            cents, docs_ref[at : at + width, :], NT, preferred_element_type=f32
        )


def first_kernel(docs_ref, cents_ref, t_ref, peak_ref, lse_ref, wide_peak, wide_lse):
    n_cent = cents_ref.shape[0]

    def block(t, _):
        start = pl.multiple_of(t * BLOCK, BLOCK)
        rows = pl.ds(start, BLOCK)
        logits_block(cents_ref[rows, :], docs_ref, t_ref, rows)
        for c in range(BLOCK // CHUNK):
            at = pl.ds(start + c * CHUNK, CHUNK)
            x = t_ref[at, :]
            peak = jnp.max(fold(x, jnp.maximum), axis=1, keepdims=True)
            e = jnp.exp((x - peak) * SCALE)
            t_ref[at, :] = e
            total = jnp.sum(fold(e, jnp.add), axis=1, keepdims=True)
            peak = jnp.broadcast_to(peak * SCALE, (CHUNK, LANES))
            wide_peak[at, :] = peak
            wide_lse[at, :] = peak + jnp.log(jnp.broadcast_to(total, (CHUNK, LANES)))
        return 0

    lax.fori_loop(0, n_cent // BLOCK, block, 0)
    for b in range(n_cent // LANES):
        at = slice(b * LANES, (b + 1) * LANES)
        peak_ref[b : b + 1, :] = to_row(wide_peak[at, :])
        lse_ref[:, b, :] = jnp.broadcast_to(to_row(wide_lse[at, :]), (lse_ref.shape[0], LANES))


def load_all(docs_hbm, cents_hbm, docs, cents):
    pltpu.sync_copy(docs_hbm, docs)
    pltpu.sync_copy(cents_hbm, cents)


def row_slow(docs_hbm, cents_hbm, col_wide, lse_ref):
    n_doc, n_cent = docs_hbm.shape[0], cents_hbm.shape[0]

    def body(docs, cents, x_ref, peak, total):
        load_all(docs_hbm, cents_hbm, docs, cents)
        peak[...] = jnp.full(peak.shape, -jnp.inf, f32)
        total[...] = jnp.zeros(total.shape, f32)

        def sweep(last):
            def block(t, _):
                start = pl.multiple_of(t * BLOCK, BLOCK)
                rows = pl.ds(start, BLOCK)
                logits_block(cents[rows, :], docs, x_ref, pl.ds(0, BLOCK))
                for at in range(0, n_doc, LANES):
                    y = x_ref[:, at : at + LANES] * SCALE + col_wide[rows, :]
                    here = peak[:, at : at + LANES]
                    if last:
                        total[:, at : at + LANES] += jnp.sum(jnp.exp(y - here), axis=0, keepdims=True)
                    else:
                        peak[:, at : at + LANES] = jnp.maximum(here, jnp.max(y, axis=0, keepdims=True))
                return 0

            lax.fori_loop(0, n_cent // BLOCK, block, 0)

        sweep(False)
        sweep(True)
        for b in range(n_doc // LANES):
            at = slice(b * LANES, (b + 1) * LANES)
            value = peak[:, at] + jnp.log(total[:, at])
            lse_ref[:, b, :] = jnp.broadcast_to(value, (lse_ref.shape[0], LANES))

    pl.run_scoped(
        body,
        pltpu.VMEM(docs_hbm.shape, bf16),
        pltpu.VMEM(cents_hbm.shape, bf16),
        pltpu.VMEM((BLOCK, n_doc), f32),
        pltpu.VMEM((1, n_doc), f32),
        pltpu.VMEM((1, n_doc), f32),
    )


def row_kernel(log_ratio, t_ref, peak_ref, parts_ref, docs_hbm, cents_hbm, lse_ref, col_ref, wide, acc):
    n_cent, n_doc = t_ref.shape
    col = log_ratio - merge(parts_ref[...])
    col_ref[...] = col
    factor = jnp.exp(peak_ref[...] + col)
    for b in range(n_cent // LANES):
        column = to_column(factor[b : b + 1, :])
        wide[b * LANES : (b + 1) * LANES, :] = jnp.broadcast_to(column, (LANES, LANES))
    acc[...] = jnp.zeros(acc.shape, f32)
    step = 64

    def block(t, _):
        start = pl.multiple_of(t * step, step)
        scale = wide[pl.ds(start, step), :]
        for at in range(0, n_doc, LANES):
            x = t_ref[pl.ds(start, step), at : at + LANES] * scale
            part = x[:8, :]
            for r in range(8, step, 8):
                part = part + x[r : r + 8, :]
            acc[:, at : at + LANES] += part
        return 0

    lax.fori_loop(0, n_cent // step, block, 0)
    least = jnp.full((1, LANES), jnp.inf, f32)
    for b in range(n_doc // LANES):
        total = jnp.sum(acc[:, b * LANES : (b + 1) * LANES], axis=0, keepdims=True)
        least = jnp.minimum(least, total)
        lse_ref[:, b, :] = jnp.broadcast_to(jnp.log(total), (lse_ref.shape[0], LANES))

    @pl.when(jnp.logical_not(jnp.min(least) >= SMALL_SUM))
    def _():
        for b in range(n_cent // LANES):
            column = to_column(col[b : b + 1, :])
            wide[b * LANES : (b + 1) * LANES, :] = jnp.broadcast_to(column, (LANES, LANES))
        row_slow(docs_hbm, cents_hbm, wide, lse_ref)


def col_slow(docs_hbm, cents_hbm, row_pot, wide_lse):
    n_doc, n_cent = docs_hbm.shape[0], cents_hbm.shape[0]

    def body(docs, cents, x_ref):
        load_all(docs_hbm, cents_hbm, docs, cents)

        def block(t, _):
            start = pl.multiple_of(t * BLOCK, BLOCK)
            logits_block(cents[pl.ds(start, BLOCK), :], docs, x_ref, pl.ds(0, BLOCK))

            def chunk(c, _):
                at = pl.multiple_of(c * CHUNK, CHUNK)
                y = [
                    x_ref[pl.ds(at, CHUNK), b * LANES : (b + 1) * LANES] * SCALE + row_pot[b : b + 1, :]
                    for b in range(n_doc // LANES)
                ]
                peak = jnp.max(functools.reduce(jnp.maximum, y), axis=1, keepdims=True)
                total = jnp.sum(sum(jnp.exp(part - peak) for part in y), axis=1, keepdims=True)
                value = peak + jnp.log(total)
                wide_lse[pl.ds(start + at, CHUNK), :] = jnp.broadcast_to(value, (CHUNK, LANES))
                return 0

            return lax.fori_loop(0, BLOCK // CHUNK, chunk, 0)

        lax.fori_loop(0, n_cent // BLOCK, block, 0)

    pl.run_scoped(
        body,
        pltpu.VMEM(docs_hbm.shape, bf16),
        pltpu.VMEM(cents_hbm.shape, bf16),
        pltpu.VMEM((BLOCK, n_doc), f32),
    )


def col_kernel(t_ref, peak_ref, parts_ref, docs_hbm, cents_hbm, lse_ref, wide_lse):
    n_cent, n_doc = t_ref.shape
    row_pot = -merge(parts_ref[...])
    factor = jnp.exp(row_pot)
    step = 64

    def block(t, _):
        start = pl.multiple_of(t * step, step)
        total = jnp.zeros((step, LANES), f32)
        for b in range(n_doc // LANES):
            total = total + t_ref[pl.ds(start, step), b * LANES : (b + 1) * LANES] * factor[b : b + 1, :]
        total = jnp.sum(total, axis=1, keepdims=True)
        wide_lse[pl.ds(start, step), :] = jnp.log(jnp.broadcast_to(total, (step, LANES)))
        return 0

    lax.fori_loop(0, n_cent // step, block, 0)
    good = jnp.max(row_pot) <= LARGE_POT
    for b in range(n_cent // LANES):
        at = slice(b * LANES, (b + 1) * LANES)
        value = to_row(wide_lse[at, :]) + peak_ref[b : b + 1, :]
        lse_ref[:, b, :] = jnp.broadcast_to(value, (lse_ref.shape[0], LANES))

    @pl.when(jnp.logical_not(good))
    def _():
        def body(pot):
            pot[...] = row_pot
            col_slow(docs_hbm, cents_hbm, pot, wide_lse)

        pl.run_scoped(body, pltpu.VMEM(row_pot.shape, f32))
        for b in range(n_cent // LANES):
            value = to_row(wide_lse[b * LANES : (b + 1) * LANES, :])
            lse_ref[:, b, :] = jnp.broadcast_to(value, (lse_ref.shape[0], LANES))


def last_kernel(t_ref, peak_ref, col_ref, parts_ref, docs_ref, cents_hbm, sums_ref, mass_ref, wide, wide_mass, pot, plan):
    n_cent, n_doc = t_ref.shape
    row_pot = -merge(parts_ref[...])
    good = jnp.max(row_pot) <= LARGE_POT
    pot[...] = jnp.where(good, jnp.exp(row_pot), row_pot)
    by_col = jnp.where(good, jnp.exp(peak_ref[...] + col_ref[...]), col_ref[...])
    for b in range(n_cent // LANES):
        column = to_column(by_col[b : b + 1, :])
        wide[b * LANES : (b + 1) * LANES, :] = jnp.broadcast_to(column, (LANES, LANES))

    def finish(start):
        mass = None
        for b in range(n_doc // LANES):
            part = fold(plan[:, b * LANES : (b + 1) * LANES].astype(f32), jnp.add)
            mass = part if mass is None else mass + part
        mass = jnp.sum(mass, axis=1, keepdims=True)
        wide_mass[pl.ds(start, BLOCK), :] = jnp.broadcast_to(mass, (BLOCK, LANES))
        sums_ref[pl.ds(start, BLOCK), :] = jnp.dot(plan[...], docs_ref[...], preferred_element_type=f32)

    @pl.when(good)
    def _():
        def block(t, _):
            start = pl.multiple_of(t * BLOCK, BLOCK)
            scale = wide[pl.ds(start, BLOCK), :]
            for b in range(n_doc // LANES):
                at = slice(b * LANES, (b + 1) * LANES)
                plan[:, at] = (t_ref[pl.ds(start, BLOCK), at] * scale * pot[b : b + 1, :]).astype(bf16)
            finish(start)
            return 0

        lax.fori_loop(0, n_cent // BLOCK, block, 0)

    @pl.when(jnp.logical_not(good))
    def _():
        def body(cents, x_ref):
            pltpu.sync_copy(cents_hbm, cents)

            def block(t, _):
                start = pl.multiple_of(t * BLOCK, BLOCK)
                logits_block(cents[pl.ds(start, BLOCK), :], docs_ref, x_ref, pl.ds(0, BLOCK))
                col = wide[pl.ds(start, BLOCK), :]
                for b in range(n_doc // LANES):
                    at = slice(b * LANES, (b + 1) * LANES)
                    plan[:, at] = jnp.exp(x_ref[:, at] * SCALE + pot[b : b + 1, :] + col).astype(bf16)
                finish(start)
                return 0

            lax.fori_loop(0, n_cent // BLOCK, block, 0)

        pl.run_scoped(body, pltpu.VMEM(cents_hbm.shape, bf16), pltpu.VMEM((BLOCK, n_doc), f32))

    for b in range(n_cent // LANES):
        mass_ref[b : b + 1, :] = to_row(wide_mass[b * LANES : (b + 1) * LANES, :])


def divide_kernel(sums_ref, mass_ref, out_ref):
    mass = jnp.sum(mass_ref[...], axis=0)
    for b in range(mass.shape[0]):
        at = slice(b * LANES, (b + 1) * LANES)
        out_ref[at, :] = (sums_ref[at, :] / to_column(mass[b : b + 1, :])).astype(bf16)


IN_VMEM = pl.BlockSpec(memory_space=pltpu.VMEM)
IN_HBM = pl.BlockSpec(memory_space=pl.ANY)


def params(mib):
    return pltpu.CompilerParams(vmem_limit_bytes=mib * 2**20)


def shards(embeddings, centroids):
    groups, blocks = lax.axis_size("dp"), lax.axis_size("cent")
    docs = lax.all_gather(embeddings, "cent", axis=0, tiled=True)
    n_doc, depth = docs.shape
    n_cent = centroids.shape[0]
    log_ratio = math.log(n_doc * groups / (n_cent * blocks))
    row_shape = (n_doc // LANES, LANES)
    col_shape = (n_cent // LANES, LANES)
    shaped = jax.ShapeDtypeStruct
    by_group = shaped((groups, *col_shape), f32)
    by_block = shaped((blocks, *row_shape), f32)
    wide = pltpu.VMEM((n_cent, LANES), f32)

    t, peak, lse = pl.pallas_call(
        first_kernel,
        out_shape=(pltpu.VMEM((n_cent, n_doc), f32), shaped(col_shape, f32), by_group),
        in_specs=[IN_VMEM, IN_VMEM],
        out_specs=(IN_VMEM, IN_VMEM, IN_VMEM),
        scratch_shapes=[wide, wide],
        compiler_params=params(20),
    )(docs, centroids)

    def rows(lse):
        parts = lax.all_to_all(lse, "dp", 0, 0)
        return pl.pallas_call(
            functools.partial(row_kernel, log_ratio),
            out_shape=(by_block, shaped(col_shape, f32)),
            in_specs=[IN_VMEM, IN_VMEM, IN_VMEM, IN_HBM, IN_HBM],
            out_specs=(IN_VMEM, IN_VMEM),
            scratch_shapes=[wide, pltpu.VMEM((8, n_doc), f32)],
            compiler_params=params(20),
        )(t, peak, parts, docs, centroids)

    def cols(lse):
        parts = lax.all_to_all(lse, "cent", 0, 0)
        return pl.pallas_call(
            col_kernel,
            out_shape=by_group,
            in_specs=[IN_VMEM, IN_VMEM, IN_VMEM, IN_HBM, IN_HBM],
            out_specs=IN_VMEM,
            scratch_shapes=[wide],
            compiler_params=params(20),
        )(t, peak, parts, docs, centroids)

    lse, _ = rows(lse)
    lse = cols(lse)
    lse, col = rows(lse)
    parts = lax.all_to_all(lse, "cent", 0, 0)
    sums, mass = pl.pallas_call(
        last_kernel,
        out_shape=(shaped((n_cent, depth), f32), shaped(col_shape, f32)),
        in_specs=[IN_VMEM, IN_VMEM, IN_VMEM, IN_VMEM, IN_VMEM, IN_HBM],
        out_specs=(IN_VMEM, IN_VMEM),
        scratch_shapes=[wide, wide, pltpu.VMEM(row_shape, f32), pltpu.VMEM((BLOCK, n_doc), bf16)],
        compiler_params=params(30),
    )(t, peak, col, parts, docs, centroids)
    sums = lax.psum_scatter(sums, "dp", scatter_dimension=0, tiled=True)
    mass = lax.all_to_all(mass.reshape(groups, n_cent // groups // LANES, LANES), "dp", 0, 0)
    new = pl.pallas_call(
        divide_kernel,
        out_shape=shaped(sums.shape, bf16),
        in_specs=[IN_VMEM, IN_VMEM],
        out_specs=IN_VMEM,
    )(sums, mass)
    return lax.all_gather(new, "dp", axis=0, tiled=True)


def solution(mesh):
    placed = (P(("dp", "cent"), None), P("cent", None))
    return jax.shard_map(
        shards, mesh=mesh, in_specs=placed, out_specs=P("cent", None), check_vma=False
    )
```

```python
import functools
import math

import jax
import jax.numpy as jnp
from jax import lax
from jax.experimental import pallas as pl
from jax.experimental.pallas import tpu as pltpu
from jax.sharding import PartitionSpec as P

f32 = jnp.float32
bf16 = jnp.bfloat16
LANES = 128
BLOCK = 256
CHUNK = 16
SCALE = 3.0
SMALL_SUM = 1e-20
LARGE_POT = 46.0
PAD = 16
NT = (((1,), (1,)), ((), ()))


def eye():
    rows = lax.broadcasted_iota(jnp.int32, (LANES, LANES), 0)
    cols = lax.broadcasted_iota(jnp.int32, (LANES, LANES), 1)
    return rows == cols


def to_row(column):
    return jnp.sum(jnp.where(eye(), column, 0.0), axis=0, keepdims=True)


def to_column(row):
    return jnp.sum(jnp.where(eye(), row, 0.0), axis=1, keepdims=True)


def fold(x, op):
    out = x[:, :LANES]
    for at in range(LANES, x.shape[1], LANES):
        out = op(out, x[:, at : at + LANES])
    return out


def merge(parts):
    peak = jnp.max(parts, axis=0)
    return peak + jnp.log(jnp.sum(jnp.exp(parts - peak[None]), axis=0))


def logits_block(cents, docs_ref, out_ref, rows):
    width = 512
    for at in range(0, docs_ref.shape[0], width):
        out_ref[rows, at : at + width] = lax.dot_general(
            cents, docs_ref[at : at + width, :], NT, preferred_element_type=f32
        )


def first_kernel(docs_ref, cents_ref, t_ref, peak_ref, lse_ref, wide_peak, wide_lse):
    n_cent = cents_ref.shape[0]

    def block(t, _):
        start = pl.multiple_of(t * BLOCK, BLOCK)
        rows = pl.ds(start, BLOCK)
        logits_block(cents_ref[rows, :], docs_ref, t_ref, rows)
        for c in range(BLOCK // CHUNK):
            at = pl.ds(start + c * CHUNK, CHUNK)
            x = t_ref[at, :]
            peak = jnp.max(fold(x, jnp.maximum), axis=1, keepdims=True)
            e = jnp.exp((x - peak) * SCALE)
            t_ref[at, :] = e
            total = jnp.sum(fold(e, jnp.add), axis=1, keepdims=True)
            peak = jnp.broadcast_to(peak * SCALE, (CHUNK, LANES))
            wide_peak[at, :] = peak
            wide_lse[at, :] = peak + jnp.log(jnp.broadcast_to(total, (CHUNK, LANES)))
        return 0

    lax.fori_loop(0, n_cent // BLOCK, block, 0)
    for b in range(n_cent // LANES):
        at = slice(b * LANES, (b + 1) * LANES)
        peak_ref[b : b + 1, :] = to_row(wide_peak[at, :])
        lse_ref[:, b, :] = jnp.broadcast_to(to_row(wide_lse[at, :]), (lse_ref.shape[0], LANES))


def load_all(docs_hbm, cents_hbm, docs, cents):
    pltpu.sync_copy(docs_hbm, docs)
    pltpu.sync_copy(cents_hbm, cents)


def row_slow(docs_hbm, cents_hbm, col_wide, lse_ref):
    n_doc, n_cent = docs_hbm.shape[0], cents_hbm.shape[0]

    def body(docs, cents, x_ref, peak, total):
        load_all(docs_hbm, cents_hbm, docs, cents)
        peak[...] = jnp.full(peak.shape, -jnp.inf, f32)
        total[...] = jnp.zeros(total.shape, f32)

        def sweep(last):
            def block(t, _):
                start = pl.multiple_of(t * BLOCK, BLOCK)
                rows = pl.ds(start, BLOCK)
                logits_block(cents[rows, :], docs, x_ref, pl.ds(0, BLOCK))
                for at in range(0, n_doc, LANES):
                    y = x_ref[:, at : at + LANES] * SCALE + col_wide[rows, :]
                    here = peak[:, at : at + LANES]
                    if last:
                        total[:, at : at + LANES] += jnp.sum(jnp.exp(y - here), axis=0, keepdims=True)
                    else:
                        peak[:, at : at + LANES] = jnp.maximum(here, jnp.max(y, axis=0, keepdims=True))
                return 0

            lax.fori_loop(0, n_cent // BLOCK, block, 0)

        sweep(False)
        sweep(True)
        for b in range(n_doc // LANES):
            at = slice(b * LANES, (b + 1) * LANES)
            value = peak[:, at] + jnp.log(total[:, at])
            lse_ref[:, b, :] = jnp.broadcast_to(value, (lse_ref.shape[0], LANES))

    pl.run_scoped(
        body,
        pltpu.VMEM(docs_hbm.shape, bf16),
        pltpu.VMEM(cents_hbm.shape, bf16),
        pltpu.VMEM((BLOCK, n_doc), f32),
        pltpu.VMEM((1, n_doc), f32),
        pltpu.VMEM((1, n_doc), f32),
    )


def row_kernel(log_ratio, t_ref, peak_ref, parts_ref, docs_hbm, cents_hbm, lse_ref, col_ref, wide, acc):
    n_cent, n_doc = t_ref.shape
    col = log_ratio - merge(parts_ref[...])
    col_ref[...] = col
    factor = jnp.exp(peak_ref[...] + col)
    for b in range(n_cent // LANES):
        column = to_column(factor[b : b + 1, :])
        wide[b * LANES : (b + 1) * LANES, :] = jnp.broadcast_to(column, (LANES, LANES))
    acc[...] = jnp.zeros(acc.shape, f32)
    step = 64

    def block(t, _):
        start = pl.multiple_of(t * step, step)
        scale = wide[pl.ds(start, step), :]
        for at in range(0, n_doc, LANES):
            x = t_ref[pl.ds(start, step), at : at + LANES] * scale
            part = x[:8, :]
            for r in range(8, step, 8):
                part = part + x[r : r + 8, :]
            acc[:, at : at + LANES] += part
        return 0

    lax.fori_loop(0, n_cent // step, block, 0)
    least = jnp.full((1, LANES), jnp.inf, f32)
    for b in range(n_doc // LANES):
        total = jnp.sum(acc[:, b * LANES : (b + 1) * LANES], axis=0, keepdims=True)
        least = jnp.minimum(least, total)
        lse_ref[:, b, :] = jnp.broadcast_to(jnp.log(total), (lse_ref.shape[0], LANES))

    @pl.when(jnp.logical_not(jnp.min(least) >= SMALL_SUM))
    def _():
        for b in range(n_cent // LANES):
            column = to_column(col[b : b + 1, :])
            wide[b * LANES : (b + 1) * LANES, :] = jnp.broadcast_to(column, (LANES, LANES))
        row_slow(docs_hbm, cents_hbm, wide, lse_ref)


def col_slow(docs_hbm, cents_hbm, row_pot, wide_lse):
    n_doc, n_cent = docs_hbm.shape[0], cents_hbm.shape[0]

    def body(docs, cents, x_ref):
        load_all(docs_hbm, cents_hbm, docs, cents)

        def block(t, _):
            start = pl.multiple_of(t * BLOCK, BLOCK)
            logits_block(cents[pl.ds(start, BLOCK), :], docs, x_ref, pl.ds(0, BLOCK))

            def chunk(c, _):
                at = pl.multiple_of(c * CHUNK, CHUNK)
                y = [
                    x_ref[pl.ds(at, CHUNK), b * LANES : (b + 1) * LANES] * SCALE + row_pot[b : b + 1, :]
                    for b in range(n_doc // LANES)
                ]
                peak = jnp.max(functools.reduce(jnp.maximum, y), axis=1, keepdims=True)
                total = jnp.sum(sum(jnp.exp(part - peak) for part in y), axis=1, keepdims=True)
                value = peak + jnp.log(total)
                wide_lse[pl.ds(start + at, CHUNK), :] = jnp.broadcast_to(value, (CHUNK, LANES))
                return 0

            return lax.fori_loop(0, BLOCK // CHUNK, chunk, 0)

        lax.fori_loop(0, n_cent // BLOCK, block, 0)

    pl.run_scoped(
        body,
        pltpu.VMEM(docs_hbm.shape, bf16),
        pltpu.VMEM(cents_hbm.shape, bf16),
        pltpu.VMEM((BLOCK, n_doc), f32),
    )


def col_kernel(t_ref, peak_ref, parts_ref, docs_hbm, cents_hbm, lse_ref, wide_lse):
    n_cent, n_doc = t_ref.shape
    row_pot = -merge(parts_ref[...])
    factor = jnp.exp(row_pot)
    step = 64

    def block(t, _):
        start = pl.multiple_of(t * step, step)
        total = jnp.zeros((step, LANES), f32)
        for b in range(n_doc // LANES):
            total = total + t_ref[pl.ds(start, step), b * LANES : (b + 1) * LANES] * factor[b : b + 1, :]
        total = jnp.sum(total, axis=1, keepdims=True)
        wide_lse[pl.ds(start, step), :] = jnp.log(jnp.broadcast_to(total, (step, LANES)))
        return 0

    lax.fori_loop(0, n_cent // step, block, 0)
    good = jnp.max(row_pot) <= LARGE_POT
    for b in range(n_cent // LANES):
        at = slice(b * LANES, (b + 1) * LANES)
        value = to_row(wide_lse[at, :]) + peak_ref[b : b + 1, :]
        lse_ref[:, b, :] = jnp.broadcast_to(value, (lse_ref.shape[0], LANES))

    @pl.when(jnp.logical_not(good))
    def _():
        def body(pot):
            pot[...] = row_pot
            col_slow(docs_hbm, cents_hbm, pot, wide_lse)

        pl.run_scoped(body, pltpu.VMEM(row_pot.shape, f32))
        for b in range(n_cent // LANES):
            value = to_row(wide_lse[b * LANES : (b + 1) * LANES, :])
            lse_ref[:, b, :] = jnp.broadcast_to(value, (lse_ref.shape[0], LANES))


def prepare_kernel(peak_ref, col_ref, parts_ref, wide, pot_ref, row_ref):
    row_pot = -merge(parts_ref[...])
    good = jnp.max(row_pot) <= LARGE_POT
    row_ref[...] = row_pot
    pot_ref[...] = jnp.where(good, jnp.exp(row_pot), row_pot)
    by_col = jnp.where(good, jnp.exp(peak_ref[...] + col_ref[...]), col_ref[...])
    for b in range(by_col.shape[0]):
        column = to_column(by_col[b : b + 1, :])
        wide[b * LANES : (b + 1) * LANES, :] = jnp.broadcast_to(column, (LANES, LANES))


def split(value):
    high = value.astype(bf16).astype(f32)
    middle = (value - high).astype(bf16).astype(f32)
    low = value - high - middle
    row = lax.broadcasted_iota(jnp.int32, (PAD, LANES), 0)
    rows = jnp.where(row == 0, high, jnp.where(row == 1, middle, jnp.where(row == 2, low, 0.0)))
    return rows.astype(bf16)


def joined(rows):
    rows = rows.astype(f32)
    return rows[0:1] + rows[1:2] + rows[2:3]


def step_kernel(step, n_in, ends, *refs):
    t_ref, wide, pot_ref, row_ref, docs_ref, cents_hbm = refs[:6]
    came = refs[6 : 6 + n_in]
    first, second, rest_first, rest_second = refs[6 + n_in : 10 + n_in]
    if ends:
        mass_ref = refs[10 + n_in]
    groups, me = lax.axis_size("dp"), lax.axis_index("dp")
    ids = [lax.rem(me + shift, groups) for shift in (groups // 2 - step, groups // 2 + 1 + step)]
    plan = refs[-1]
    n_doc = docs_ref.shape[0]
    half = docs_ref.shape[1] // 2
    good = jnp.max(row_ref[...]) <= LARGE_POT
    for k, (out, rest) in enumerate(((first, rest_first), (second, rest_second))):
        start = pl.multiple_of(ids[k] * BLOCK, BLOCK)

        @pl.when(good)
        def _():
            for r in range(0, BLOCK, LANES):
                rows = pl.ds(start + r, LANES)
                scale = wide[rows, :]
                for b in range(n_doc // LANES):
                    at = slice(b * LANES, (b + 1) * LANES)
                    plan[k, r : r + LANES, at] = (t_ref[rows, at] * scale * pot_ref[b : b + 1, :]).astype(bf16)

        @pl.when(jnp.logical_not(good))
        def _():
            def body(cents, x_ref):
                pltpu.sync_copy(cents_hbm.at[pl.ds(start, BLOCK), :], cents)
                logits_block(cents[...], docs_ref, x_ref, pl.ds(0, BLOCK))
                col = wide[pl.ds(start, BLOCK), :]
                for b in range(n_doc // LANES):
                    at = slice(b * LANES, (b + 1) * LANES)
                    plan[k, :, at] = jnp.exp(x_ref[:, at] * SCALE + pot_ref[b : b + 1, :] + col).astype(bf16)

            pl.run_scoped(body, pltpu.VMEM((BLOCK, cents_hbm.shape[1]), bf16), pltpu.VMEM((BLOCK, n_doc), f32))

        sums = jnp.dot(plan[k], docs_ref[...], preferred_element_type=f32)
        rest[...] = sums[:, half:].astype(rest.dtype)
        sums = sums[:, :half]
        if n_in:
            sums = sums + came[k][:BLOCK, :].astype(f32)
        if ends and k == 1:
            out[...] = sums
        else:
            out[:BLOCK, :] = sums.astype(bf16)
            out[BLOCK:, :] = jnp.zeros((PAD, half), bf16)
        for r in range(0, BLOCK, LANES):
            mass = fold(plan[k, r : r + LANES, :].astype(f32), jnp.add)
            mass = to_row(jnp.broadcast_to(jnp.sum(mass, axis=1, keepdims=True), (LANES, LANES)))
            if n_in:
                mass = mass + joined(came[k][BLOCK:, r : r + LANES])
            if ends and k == 1:
                mass_ref[r // LANES : r // LANES + 1, :] = mass
            else:
                out[BLOCK:, r : r + LANES] = split(mass)


def add_kernel(ends, *refs):
    for k in range(2):
        total = refs[k][...] + refs[2 + k][...].astype(f32)
        out = refs[4 + k]
        out[...] = total if ends and k == 1 else total.astype(bf16)


def divide_kernel(sums_ref, came_ref, mass_ref, out_ref, total_ref):
    for b in range(BLOCK // LANES):
        at = slice(b * LANES, (b + 1) * LANES)
        mass = mass_ref[b : b + 1, :] + joined(came_ref[BLOCK:, at])
        total_ref[b : b + 1, :] = mass
        out_ref[at, :] = ((sums_ref[at, :] + came_ref[at, :].astype(f32)) / to_column(mass)).astype(bf16)


def divide_rest_kernel(sums_ref, came_ref, mass_ref, out_ref):
    for b in range(BLOCK // LANES):
        at = slice(b * LANES, (b + 1) * LANES)
        out_ref[at, :] = (
            (sums_ref[at, :] + came_ref[at, :].astype(f32)) / to_column(mass_ref[b : b + 1, :])
        ).astype(bf16)


def place_kernel(shifts, *refs):
    n = len(shifts)
    me = lax.axis_index("dp")
    blocks, out, sems = refs[: 2 * n], refs[2 * n], refs[2 * n + 1]
    half = out.shape[1] // 2
    copies = []
    for at in range(2 * n):
        start = pl.multiple_of(lax.rem(me + shifts[at % n], n) * BLOCK, BLOCK)
        to = out.at[pl.ds(start, BLOCK), pl.ds((at // n) * half, half)]
        copy = pltpu.make_async_copy(blocks[at], to, sems.at[at])
        copy.start()
        copies.append(copy)
    for copy in copies:
        copy.wait()


IN_VMEM = pl.BlockSpec(memory_space=pltpu.VMEM)
IN_HBM = pl.BlockSpec(memory_space=pl.ANY)


def params(mib):
    return pltpu.CompilerParams(vmem_limit_bytes=mib * 2**20)


def shards(embeddings, centroids):
    groups, blocks = lax.axis_size("dp"), lax.axis_size("cent")
    docs = lax.all_gather(embeddings, "cent", axis=0, tiled=True)
    n_doc, depth = docs.shape
    n_cent = centroids.shape[0]
    log_ratio = math.log(n_doc * groups / (n_cent * blocks))
    row_shape = (n_doc // LANES, LANES)
    col_shape = (n_cent // LANES, LANES)
    shaped = jax.ShapeDtypeStruct
    by_group = shaped((groups, *col_shape), f32)
    by_block = shaped((blocks, *row_shape), f32)
    wide = pltpu.VMEM((n_cent, LANES), f32)

    t, peak, lse = pl.pallas_call(
        first_kernel,
        out_shape=(pltpu.VMEM((n_cent, n_doc), f32), shaped(col_shape, f32), by_group),
        in_specs=[IN_VMEM, IN_VMEM],
        out_specs=(IN_VMEM, IN_VMEM, IN_VMEM),
        scratch_shapes=[wide, wide],
        compiler_params=params(20),
    )(docs, centroids)

    def rows(lse):
        parts = lax.all_to_all(lse, "dp", 0, 0)
        return pl.pallas_call(
            functools.partial(row_kernel, log_ratio),
            out_shape=(by_block, shaped(col_shape, f32)),
            in_specs=[IN_VMEM, IN_VMEM, IN_VMEM, IN_HBM, IN_HBM],
            out_specs=(IN_VMEM, IN_VMEM),
            scratch_shapes=[wide, pltpu.VMEM((8, n_doc), f32)],
            compiler_params=params(20),
        )(t, peak, parts, docs, centroids)

    def cols(lse):
        parts = lax.all_to_all(lse, "cent", 0, 0)
        return pl.pallas_call(
            col_kernel,
            out_shape=by_group,
            in_specs=[IN_VMEM, IN_VMEM, IN_VMEM, IN_HBM, IN_HBM],
            out_specs=IN_VMEM,
            scratch_shapes=[wide],
            compiler_params=params(20),
        )(t, peak, parts, docs, centroids)

    lse, _ = rows(lse)
    lse = cols(lse)
    lse, col = rows(lse)
    parts = lax.all_to_all(lse, "cent", 0, 0)
    wide_col, pot, row = pl.pallas_call(
        prepare_kernel,
        out_shape=(pltpu.VMEM((n_cent, LANES), f32), shaped(row_shape, f32), shaped(row_shape, f32)),
        in_specs=[IN_VMEM] * 3,
        out_specs=(IN_VMEM,) * 3,
        compiler_params=params(4),
    )(peak, col, parts)

    far = groups // 2
    half = depth // 2
    message = shaped((BLOCK + PAD, half), bf16)
    rest_message = shaped((BLOCK, half), bf16)
    rest = shaped((BLOCK, half), f32)

    def move(x, by):
        return lax.ppermute(x, "dp", [(i, (i + by) % groups) for i in range(groups)])

    came, rest_came = (), ()
    for s in range(far):
        ends = s == far - 1
        kept = rest if s else rest_message
        out = (message, rest if ends else message, kept, rest if ends else kept)
        out += (shaped((2, LANES), f32),) if ends else ()
        out = pl.pallas_call(
            functools.partial(step_kernel, s, len(came), ends),
            out_shape=out,
            in_specs=[IN_VMEM] * 5 + [IN_HBM] + [IN_VMEM] * len(came),
            out_specs=(IN_VMEM,) * len(out),
            scratch_shapes=[pltpu.VMEM((2, BLOCK, n_doc), bf16)],
            compiler_params=params(20),
            cost_estimate=pl.CostEstimate(flops=4 * BLOCK * n_doc * depth, bytes_accessed=4 * 2**20, transcendentals=0),
        )(t, wide_col, pot, row, docs, centroids, *came)
        if ends:
            right, own, rest_right, rest_own, mass = out
            came = (move(right, 1),)
        else:
            right, left, rest_right, rest_own = out
            came = (move(right, 1), move(left, -1))
        if s:
            rest_right, rest_own = pl.pallas_call(
                functools.partial(add_kernel, ends),
                out_shape=(rest_message, rest if ends else rest_message),
                in_specs=[IN_VMEM] * 4,
                out_specs=(IN_VMEM,) * 2,
                compiler_params=params(4),
            )(rest_right, rest_own, *rest_came)
        rest_came = (move(rest_right, 1),) if ends else (move(rest_right, 1), move(rest_own, -1))

    new, total = pl.pallas_call(
        divide_kernel,
        out_shape=(rest_message, shaped((2, LANES), f32)),
        in_specs=[IN_VMEM] * 3,
        out_specs=(IN_VMEM,) * 2,
        compiler_params=params(4),
    )(own, came[0], mass)
    rest_new = pl.pallas_call(
        divide_rest_kernel,
        out_shape=rest_message,
        in_specs=[IN_VMEM] * 3,
        out_specs=IN_VMEM,
        compiler_params=params(4),
    )(rest_own, rest_came[0], total)

    blocks, rest_blocks, shifts = [new], [rest_new], [0]
    for hop in range(1, far + 1):
        for by in (-1, 1):
            if hop == far and by == 1:
                continue
            at = 0 if hop == 1 else (len(blocks) - 2)
            blocks.append(move(blocks[at], by))
            rest_blocks.append(move(rest_blocks[at], by))
            shifts.append(-by * hop % groups)
    return pl.pallas_call(
        functools.partial(place_kernel, shifts),
        out_shape=shaped((n_cent, depth), bf16),
        in_specs=[IN_HBM] * (2 * groups),
        out_specs=IN_HBM,
        scratch_shapes=[pltpu.SemaphoreType.DMA((2 * groups,))],
        compiler_params=params(4),
    )(*blocks, *rest_blocks)


def solution(mesh):
    placed = (P(("dp", "cent"), None), P("cent", None))
    return jax.shard_map(
        shards, mesh=mesh, in_specs=placed, out_specs=P("cent", None), check_vma=False
    )
```

```python
import functools
import math

import jax
import jax.numpy as jnp
from jax import lax
from jax.experimental import pallas as pl
from jax.experimental.pallas import tpu as pltpu
from jax.sharding import PartitionSpec as P

f32 = jnp.float32
bf16 = jnp.bfloat16
LANES = 128
BLOCK = 256
CHUNK = 16
SCALE = 3.0
EXP2_SCALE = SCALE * math.log2(math.e)
RING_Y, RING_X, CORES = 4, 4, 2
SMALL_SUM = 1e-20
LARGE_POT = 46.0
PAD = 16
NT = (((1,), (1,)), ((), ()))


def eye():
    rows = lax.broadcasted_iota(jnp.int32, (LANES, LANES), 0)
    cols = lax.broadcasted_iota(jnp.int32, (LANES, LANES), 1)
    return rows == cols


def to_row(column):
    return jnp.sum(jnp.where(eye(), column, 0.0), axis=0, keepdims=True)


def to_column(row):
    return jnp.sum(jnp.where(eye(), row, 0.0), axis=1, keepdims=True)


def fold(x, op):
    out = x[:, :LANES]
    for at in range(LANES, x.shape[1], LANES):
        out = op(out, x[:, at : at + LANES])
    return out


def merge(parts):
    peak = jnp.max(parts, axis=0)
    return peak + jnp.log(jnp.sum(jnp.exp(parts - peak[None]), axis=0))


def logits_block(cents, docs_ref, out_ref, rows, offset=0):
    width = 512
    for at in range(0, docs_ref.shape[0], width):
        out_ref[rows, offset + at : offset + at + width] = lax.dot_general(
            cents, docs_ref[at : at + width, :], NT, preferred_element_type=f32
        )


def place_on_cent():
    at = lax.axis_index("cent")
    return at // (RING_X * CORES), at // CORES % RING_X, at % CORES


def shifted(x, dy=0, dx=0, dc=0):
    pairs = []
    for y in range(RING_Y):
        for x_at in range(RING_X):
            for c in range(CORES):
                to = ((y + dy) % RING_Y * RING_X + (x_at + dx) % RING_X) * CORES + (c + dc) % CORES
                pairs.append(((y * RING_X + x_at) * CORES + c, to))
    return lax.ppermute(x, "cent", pairs)


def stack_blocks(out, offset, at, ring, own, before, after, across):
    size = own.shape[0]
    for shift, block in ((0, own), (ring - 1, before), (1, after), (2, across)):
        start = pl.multiple_of(offset + lax.rem(at + shift, ring) * size, size)
        out[pl.ds(start, size), :] = block


def near_kernel(own, x_before, x_after, x_across, y_before, y_after, y_across, along_x, along_y):
    y, x, _ = place_on_cent()
    half = own.shape[0] // 2
    stack_blocks(along_x, 0, x, RING_X, own[:half, :], x_before[...], x_after[...], x_across[...])
    stack_blocks(along_y, 0, y, RING_Y, own[half:, :], y_before[...], y_after[...], y_across[...])


def far_kernel(along_x, y_before, y_after, y_across, along_y, x_before, x_after, x_across, docs):
    y, x, _ = place_on_cent()
    stack_blocks(docs, 0, y, RING_Y, along_x[...], y_before[...], y_after[...], y_across[...])
    offset = docs.shape[0] // 2
    stack_blocks(docs, offset, x, RING_X, along_y[...], x_before[...], x_after[...], x_across[...])


def gather(own):
    half = own.shape[0] // 2
    first, second = own[:half], own[half:]
    along_x, along_y = pl.pallas_call(
        near_kernel,
        out_shape=[jax.ShapeDtypeStruct((4 * half, own.shape[1]), bf16)] * 2,
        in_specs=[IN_VMEM] * 7,
        out_specs=[IN_VMEM] * 2,
        compiler_params=params(8),
    )(
        own,
        *(shifted(first, dx=by) for by in (1, -1, 2)),
        *(shifted(second, dy=by) for by in (1, -1, 2)),
    )
    return pl.pallas_call(
        far_kernel,
        out_shape=jax.ShapeDtypeStruct((32 * half, own.shape[1]), bf16),
        in_specs=[IN_VMEM] * 8,
        out_specs=IN_VMEM,
        compiler_params=params(8),
    )(
        along_x,
        *(shifted(along_x, dy=by) for by in (1, -1, 2)),
        along_y,
        *(shifted(along_y, dx=by) for by in (1, -1, 2)),
    )


def own_kernel(docs_ref, cents_ref, raw_ref):
    def block(t, _):
        rows = pl.ds(pl.multiple_of(t * BLOCK, BLOCK), BLOCK)
        logits_block(cents_ref[rows, :], docs_ref, raw_ref, rows)
        return 0

    lax.fori_loop(0, cents_ref.shape[0] // BLOCK, block, 0)


def first_kernel(raw_ref, docs_ref, cents_ref, t_ref, peak_ref, lse_ref, even, odd, wide_peak, wide_lse, small):
    n_cent, n_own = raw_ref.shape
    n_blocks = n_cent // BLOCK
    tiles = n_own // LANES
    k = EXP2_SCALE

    def multiply(t, x_ref):
        start = pl.multiple_of(jnp.minimum(t, n_blocks - 1) * BLOCK, BLOCK)
        logits_block(cents_ref[pl.ds(start, BLOCK), :], docs_ref, x_ref, pl.ds(0, BLOCK))

    def finish(t, x_ref):
        for r in range(0, BLOCK, LANES):
            rows = pl.ds(pl.multiple_of(t * BLOCK + r, LANES), LANES)
            parts = [lambda b=b: raw_ref[rows, b * LANES : (b + 1) * LANES] for b in range(tiles)]
            parts += [lambda b=b: x_ref[r : r + LANES, b * LANES : (b + 1) * LANES] for b in range(tiles)]
            peak = parts[0]()
            for part in parts[1:]:
                peak = jnp.maximum(peak, part())
            peak = jnp.broadcast_to(jnp.max(peak, axis=1, keepdims=True), (LANES, LANES))
            total = jnp.zeros((LANES, LANES), f32)
            for b, part in enumerate(parts):
                e = jnp.exp2((part() - peak) * k)
                t_ref[rows, b * LANES : (b + 1) * LANES] = e
                total = total + e
            total = jnp.broadcast_to(jnp.sum(total, axis=1, keepdims=True), (LANES, LANES))
            wide_peak[rows, :] = peak * SCALE
            wide_lse[rows, :] = peak * SCALE + jnp.log(total)

    multiply(0, even)

    def pair(i, _):
        multiply(2 * i + 1, odd)
        finish(2 * i, even)
        multiply(2 * i + 2, even)
        finish(2 * i + 1, odd)
        return 0

    lax.fori_loop(0, n_blocks // 2, pair, 0)
    for b in range(n_cent // LANES):
        at = slice(b * LANES, (b + 1) * LANES)
        peak_ref[b : b + 1, :] = to_row(wide_peak[at, :])
        small[b : b + 1, :] = to_row(wide_lse[at, :])
    lse_ref[...] = jnp.broadcast_to(small[...][None], lse_ref.shape)


def common_order(b, n):
    _, _, core = place_on_cent()
    return lax.rem(b + core * (n // CORES), n)


def local_order(rows):
    _, _, core = place_on_cent()
    half = rows.shape[0] // CORES
    return jnp.where(core == 1, jnp.concatenate([rows[half:], rows[:half]], axis=0), rows)


def load_all(docs_hbm, cents_hbm, docs, cents):
    half = docs.shape[0] // 2
    pltpu.sync_copy(docs_hbm[0], docs.at[:half, :])
    pltpu.sync_copy(docs_hbm[1], docs.at[half:, :])
    pltpu.sync_copy(cents_hbm, cents)


def row_slow(docs_hbm, cents_hbm, col_wide, small):
    n_doc, n_cent = 2 * docs_hbm[0].shape[0], cents_hbm.shape[0]

    def body(docs, cents, x_ref, peak, total):
        load_all(docs_hbm, cents_hbm, docs, cents)
        peak[...] = jnp.full(peak.shape, -jnp.inf, f32)
        total[...] = jnp.zeros(total.shape, f32)

        def sweep(last):
            def block(t, _):
                start = pl.multiple_of(t * BLOCK, BLOCK)
                rows = pl.ds(start, BLOCK)
                logits_block(cents[rows, :], docs, x_ref, pl.ds(0, BLOCK))
                for at in range(0, n_doc, LANES):
                    y = x_ref[:, at : at + LANES] * SCALE + col_wide[rows, :]
                    here = peak[:, at : at + LANES]
                    if last:
                        total[:, at : at + LANES] += jnp.sum(jnp.exp(y - here), axis=0, keepdims=True)
                    else:
                        peak[:, at : at + LANES] = jnp.maximum(here, jnp.max(y, axis=0, keepdims=True))
                return 0

            lax.fori_loop(0, n_cent // BLOCK, block, 0)

        sweep(False)
        sweep(True)
        for b in range(n_doc // LANES):
            at = slice(b * LANES, (b + 1) * LANES)
            small[pl.ds(common_order(b, n_doc // LANES), 1), :] = peak[:, at] + jnp.log(total[:, at])

    pl.run_scoped(
        body,
        pltpu.VMEM((n_doc, cents_hbm.shape[1]), bf16),
        pltpu.VMEM(cents_hbm.shape, bf16),
        pltpu.VMEM((BLOCK, n_doc), f32),
        pltpu.VMEM((1, n_doc), f32),
        pltpu.VMEM((1, n_doc), f32),
    )


def row_kernel(log_ratio, t_ref, peak_ref, parts_ref, own_hbm, other_hbm, cents_hbm, lse_ref, col_ref, wide, acc, small):
    n_cent, n_doc = t_ref.shape
    col = log_ratio - merge(parts_ref[...])
    col_ref[...] = col
    factor = jnp.exp(peak_ref[...] + col)
    for b in range(n_cent // LANES):
        column = to_column(factor[b : b + 1, :])
        wide[b * LANES : (b + 1) * LANES, :] = jnp.broadcast_to(column, (LANES, LANES))
    acc[...] = jnp.zeros(acc.shape, f32)
    step = 64

    def block(t, _):
        start = pl.multiple_of(t * step, step)
        scale = wide[pl.ds(start, step), :]
        for at in range(0, n_doc, LANES):
            x = t_ref[pl.ds(start, step), at : at + LANES] * scale
            part = x[:8, :]
            for r in range(8, step, 8):
                part = part + x[r : r + 8, :]
            acc[:, at : at + LANES] += part
        return 0

    lax.fori_loop(0, n_cent // step, block, 0)
    least = jnp.full((1, LANES), jnp.inf, f32)
    for b in range(n_doc // LANES):
        total = jnp.sum(acc[:, b * LANES : (b + 1) * LANES], axis=0, keepdims=True)
        least = jnp.minimum(least, total)
        small[pl.ds(common_order(b, n_doc // LANES), 1), :] = jnp.log(total)

    @pl.when(jnp.logical_not(jnp.min(least) >= SMALL_SUM))
    def _():
        for b in range(n_cent // LANES):
            column = to_column(col[b : b + 1, :])
            wide[b * LANES : (b + 1) * LANES, :] = jnp.broadcast_to(column, (LANES, LANES))
        row_slow((own_hbm, other_hbm), cents_hbm, wide, small)

    lse_ref[...] = jnp.broadcast_to(small[...][None], lse_ref.shape)


def col_slow(docs_hbm, cents_hbm, row_pot, wide_lse):
    n_doc, n_cent = 2 * docs_hbm[0].shape[0], cents_hbm.shape[0]

    def body(docs, cents, x_ref):
        load_all(docs_hbm, cents_hbm, docs, cents)

        def block(t, _):
            start = pl.multiple_of(t * BLOCK, BLOCK)
            logits_block(cents[pl.ds(start, BLOCK), :], docs, x_ref, pl.ds(0, BLOCK))

            def chunk(c, _):
                at = pl.multiple_of(c * CHUNK, CHUNK)
                y = [
                    x_ref[pl.ds(at, CHUNK), b * LANES : (b + 1) * LANES] * SCALE + row_pot[b : b + 1, :]
                    for b in range(n_doc // LANES)
                ]
                peak = jnp.max(functools.reduce(jnp.maximum, y), axis=1, keepdims=True)
                total = jnp.sum(sum(jnp.exp(part - peak) for part in y), axis=1, keepdims=True)
                value = peak + jnp.log(total)
                wide_lse[pl.ds(start + at, CHUNK), :] = jnp.broadcast_to(value, (CHUNK, LANES))
                return 0

            return lax.fori_loop(0, BLOCK // CHUNK, chunk, 0)

        lax.fori_loop(0, n_cent // BLOCK, block, 0)

    pl.run_scoped(
        body,
        pltpu.VMEM((n_doc, cents_hbm.shape[1]), bf16),
        pltpu.VMEM(cents_hbm.shape, bf16),
        pltpu.VMEM((BLOCK, n_doc), f32),
    )


def col_kernel(t_ref, peak_ref, parts_ref, own_hbm, other_hbm, cents_hbm, lse_ref, wide_lse, small):
    n_cent, n_doc = t_ref.shape
    row_pot = local_order(-merge(parts_ref[...]))
    factor = jnp.exp(row_pot)
    step = 64

    def block(t, _):
        start = pl.multiple_of(t * step, step)
        total = jnp.zeros((step, LANES), f32)
        for b in range(n_doc // LANES):
            total = total + t_ref[pl.ds(start, step), b * LANES : (b + 1) * LANES] * factor[b : b + 1, :]
        total = jnp.sum(total, axis=1, keepdims=True)
        wide_lse[pl.ds(start, step), :] = jnp.log(jnp.broadcast_to(total, (step, LANES)))
        return 0

    lax.fori_loop(0, n_cent // step, block, 0)
    good = jnp.max(row_pot) <= LARGE_POT
    for b in range(n_cent // LANES):
        at = slice(b * LANES, (b + 1) * LANES)
        small[b : b + 1, :] = to_row(wide_lse[at, :]) + peak_ref[b : b + 1, :]

    @pl.when(jnp.logical_not(good))
    def _():
        def body(pot):
            pot[...] = row_pot
            col_slow((own_hbm, other_hbm), cents_hbm, pot, wide_lse)

        pl.run_scoped(body, pltpu.VMEM(row_pot.shape, f32))
        for b in range(n_cent // LANES):
            small[b : b + 1, :] = to_row(wide_lse[b * LANES : (b + 1) * LANES, :])

    lse_ref[...] = jnp.broadcast_to(small[...][None], lse_ref.shape)


def prepare_kernel(peak_ref, col_ref, parts_ref, wide, pot_ref, row_ref):
    row_pot = local_order(-merge(parts_ref[...]))
    good = jnp.max(row_pot) <= LARGE_POT
    row_ref[...] = row_pot
    pot_ref[...] = jnp.where(good, jnp.exp(row_pot), row_pot)
    by_col = jnp.where(good, jnp.exp(peak_ref[...] + col_ref[...]), col_ref[...])
    for b in range(by_col.shape[0]):
        column = to_column(by_col[b : b + 1, :])
        wide[b * LANES : (b + 1) * LANES, :] = jnp.broadcast_to(column, (LANES, LANES))


def split(value):
    high = value.astype(bf16).astype(f32)
    middle = (value - high).astype(bf16).astype(f32)
    low = value - high - middle
    row = lax.broadcasted_iota(jnp.int32, (PAD, LANES), 0)
    rows = jnp.where(row == 0, high, jnp.where(row == 1, middle, jnp.where(row == 2, low, 0.0)))
    return rows.astype(bf16)


def joined(rows):
    rows = rows.astype(f32)
    return rows[0:1] + rows[1:2] + rows[2:3]


def step_kernel(step, n_in, ends, *refs):
    t_ref, wide, pot_ref, row_ref, own_ref, other_ref, cents_hbm = refs[:7]
    came = refs[7 : 7 + n_in]
    first, second, rest_first, rest_second = refs[7 + n_in : 11 + n_in]
    if ends:
        mass_ref = refs[11 + n_in]
    groups, me = lax.axis_size("dp"), lax.axis_index("dp")
    ids = [lax.rem(me + shift, groups) for shift in (groups // 2 - step, groups // 2 + 1 + step)]
    plan = refs[-1]
    n_own, half = own_ref.shape[0], own_ref.shape[1] // 2
    n_doc = 2 * n_own
    good = jnp.max(row_ref[...]) <= LARGE_POT
    for k, (out, rest) in enumerate(((first, rest_first), (second, rest_second))):
        start = pl.multiple_of(ids[k] * BLOCK, BLOCK)

        @pl.when(good)
        def _():
            for r in range(0, BLOCK, LANES):
                rows = pl.ds(start + r, LANES)
                scale = wide[rows, :]
                for b in range(n_doc // LANES):
                    at = slice(b * LANES, (b + 1) * LANES)
                    plan[k, r : r + LANES, at] = (t_ref[rows, at] * scale * pot_ref[b : b + 1, :]).astype(bf16)

        @pl.when(jnp.logical_not(good))
        def _():
            def body(cents, x_ref):
                pltpu.sync_copy(cents_hbm.at[pl.ds(start, BLOCK), :], cents)
                logits_block(cents[...], own_ref, x_ref, pl.ds(0, BLOCK))
                logits_block(cents[...], other_ref, x_ref, pl.ds(0, BLOCK), n_own)
                col = wide[pl.ds(start, BLOCK), :]
                for b in range(n_doc // LANES):
                    at = slice(b * LANES, (b + 1) * LANES)
                    plan[k, :, at] = jnp.exp(x_ref[:, at] * SCALE + pot_ref[b : b + 1, :] + col).astype(bf16)

            pl.run_scoped(body, pltpu.VMEM((BLOCK, cents_hbm.shape[1]), bf16), pltpu.VMEM((BLOCK, n_doc), f32))

        sums = jnp.dot(plan[k, :, :n_own], own_ref[...], preferred_element_type=f32)
        sums = sums + jnp.dot(plan[k, :, n_own:], other_ref[...], preferred_element_type=f32)
        rest[...] = sums[:, half:].astype(rest.dtype)
        sums = sums[:, :half]
        if n_in:
            sums = sums + came[k][:BLOCK, :].astype(f32)
        if ends and k == 1:
            out[...] = sums
        else:
            out[:BLOCK, :] = sums.astype(bf16)
            out[BLOCK:, :] = jnp.zeros((PAD, half), bf16)
        for r in range(0, BLOCK, LANES):
            mass = fold(plan[k, r : r + LANES, :].astype(f32), jnp.add)
            mass = to_row(jnp.broadcast_to(jnp.sum(mass, axis=1, keepdims=True), (LANES, LANES)))
            if n_in:
                mass = mass + joined(came[k][BLOCK:, r : r + LANES])
            if ends and k == 1:
                mass_ref[r // LANES : r // LANES + 1, :] = mass
            else:
                out[BLOCK:, r : r + LANES] = split(mass)


def add_kernel(ends, *refs):
    for k in range(2):
        total = refs[k][...] + refs[2 + k][...].astype(f32)
        out = refs[4 + k]
        out[...] = total if ends and k == 1 else total.astype(bf16)


def divide_kernel(sums_ref, came_ref, mass_ref, out_ref, total_ref):
    for b in range(BLOCK // LANES):
        at = slice(b * LANES, (b + 1) * LANES)
        mass = mass_ref[b : b + 1, :] + joined(came_ref[BLOCK:, at])
        total_ref[b : b + 1, :] = mass
        out_ref[at, :] = ((sums_ref[at, :] + came_ref[at, :].astype(f32)) / to_column(mass)).astype(bf16)


def divide_rest_kernel(sums_ref, came_ref, mass_ref, out_ref):
    for b in range(BLOCK // LANES):
        at = slice(b * LANES, (b + 1) * LANES)
        out_ref[at, :] = (
            (sums_ref[at, :] + came_ref[at, :].astype(f32)) / to_column(mass_ref[b : b + 1, :])
        ).astype(bf16)


def place_kernel(shifts, *refs):
    n = len(shifts)
    me = lax.axis_index("dp")
    blocks, out, sems = refs[: 2 * n], refs[2 * n], refs[2 * n + 1]
    half = out.shape[1] // 2
    copies = []
    for at in range(2 * n):
        start = pl.multiple_of(lax.rem(me + shifts[at % n], n) * BLOCK, BLOCK)
        to = out.at[pl.ds(start, BLOCK), pl.ds((at // n) * half, half)]
        copy = pltpu.make_async_copy(blocks[at], to, sems.at[at])
        copy.start()
        copies.append(copy)
    for copy in copies:
        copy.wait()


IN_VMEM = pl.BlockSpec(memory_space=pltpu.VMEM)
IN_HBM = pl.BlockSpec(memory_space=pl.ANY)


def params(mib):
    return pltpu.CompilerParams(vmem_limit_bytes=mib * 2**20)


def shards(embeddings, centroids):
    groups, blocks = lax.axis_size("dp"), lax.axis_size("cent")
    own = gather(embeddings)
    other = shifted(own, dc=1)
    n_doc, depth = CORES * own.shape[0], own.shape[1]
    n_cent = centroids.shape[0]
    log_ratio = math.log(n_doc * groups / (n_cent * blocks))
    row_shape = (n_doc // LANES, LANES)
    col_shape = (n_cent // LANES, LANES)
    shaped = jax.ShapeDtypeStruct
    by_group = shaped((groups, *col_shape), f32)
    by_block = shaped((blocks, *row_shape), f32)
    wide = pltpu.VMEM((n_cent, LANES), f32)

    raw = pl.pallas_call(
        own_kernel,
        out_shape=pltpu.VMEM((n_cent, own.shape[0]), f32),
        in_specs=[IN_VMEM] * 2,
        out_specs=IN_VMEM,
        compiler_params=params(10),
        cost_estimate=pl.CostEstimate(flops=2 * n_cent * own.shape[0] * depth, bytes_accessed=12 * 2**20, transcendentals=0),
    )(own, centroids)
    t, peak, lse = pl.pallas_call(
        first_kernel,
        out_shape=(pltpu.VMEM((n_cent, n_doc), f32), shaped(col_shape, f32), by_group),
        in_specs=[IN_VMEM] * 3,
        out_specs=(IN_VMEM,) * 3,
        scratch_shapes=[pltpu.VMEM((BLOCK, own.shape[0]), f32)] * 2 + [wide, wide, pltpu.VMEM(col_shape, f32)],
        compiler_params=params(16),
    )(raw, other, centroids)

    def rows(lse):
        parts = lax.all_to_all(lse, "dp", 0, 0)
        return pl.pallas_call(
            functools.partial(row_kernel, log_ratio),
            out_shape=(by_block, shaped(col_shape, f32)),
            in_specs=[IN_VMEM] * 3 + [IN_HBM] * 3,
            out_specs=(IN_VMEM, IN_VMEM),
            scratch_shapes=[wide, pltpu.VMEM((8, n_doc), f32), pltpu.VMEM(row_shape, f32)],
            compiler_params=params(20),
        )(t, peak, parts, own, other, centroids)

    def cols(lse):
        parts = lax.all_to_all(lse, "cent", 0, 0)
        return pl.pallas_call(
            col_kernel,
            out_shape=by_group,
            in_specs=[IN_VMEM] * 3 + [IN_HBM] * 3,
            out_specs=IN_VMEM,
            scratch_shapes=[wide, pltpu.VMEM(col_shape, f32)],
            compiler_params=params(20),
        )(t, peak, parts, own, other, centroids)

    lse, _ = rows(lse)
    lse = cols(lse)
    lse, col = rows(lse)
    parts = lax.all_to_all(lse, "cent", 0, 0)
    wide_col, pot, row = pl.pallas_call(
        prepare_kernel,
        out_shape=(pltpu.VMEM((n_cent, LANES), f32), shaped(row_shape, f32), shaped(row_shape, f32)),
        in_specs=[IN_VMEM] * 3,
        out_specs=(IN_VMEM,) * 3,
        compiler_params=params(4),
    )(peak, col, parts)

    far = groups // 2
    half = depth // 2
    message = shaped((BLOCK + PAD, half), bf16)
    rest_message = shaped((BLOCK, half), bf16)
    rest = shaped((BLOCK, half), f32)

    def move(x, by):
        return lax.ppermute(x, "dp", [(i, (i + by) % groups) for i in range(groups)])

    came, rest_came = (), ()
    for s in range(far):
        ends = s == far - 1
        kept = rest if s else rest_message
        out = (message, rest if ends else message, kept, rest if ends else kept)
        out += (shaped((2, LANES), f32),) if ends else ()
        out = pl.pallas_call(
            functools.partial(step_kernel, s, len(came), ends),
            out_shape=out,
            in_specs=[IN_VMEM] * 6 + [IN_HBM] + [IN_VMEM] * len(came),
            out_specs=(IN_VMEM,) * len(out),
            scratch_shapes=[pltpu.VMEM((2, BLOCK, n_doc), bf16)],
            compiler_params=params(20),
            cost_estimate=pl.CostEstimate(flops=4 * BLOCK * n_doc * depth, bytes_accessed=4 * 2**20, transcendentals=0),
        )(t, wide_col, pot, row, own, other, centroids, *came)
        if ends:
            right, own, rest_right, rest_own, mass = out
            came = (move(right, 1),)
        else:
            right, left, rest_right, rest_own = out
            came = (move(right, 1), move(left, -1))
        if s:
            rest_right, rest_own = pl.pallas_call(
                functools.partial(add_kernel, ends),
                out_shape=(rest_message, rest if ends else rest_message),
                in_specs=[IN_VMEM] * 4,
                out_specs=(IN_VMEM,) * 2,
                compiler_params=params(4),
            )(rest_right, rest_own, *rest_came)
        rest_came = (move(rest_right, 1),) if ends else (move(rest_right, 1), move(rest_own, -1))

    new, total = pl.pallas_call(
        divide_kernel,
        out_shape=(rest_message, shaped((2, LANES), f32)),
        in_specs=[IN_VMEM] * 3,
        out_specs=(IN_VMEM,) * 2,
        compiler_params=params(4),
    )(own, came[0], mass)
    rest_new = pl.pallas_call(
        divide_rest_kernel,
        out_shape=rest_message,
        in_specs=[IN_VMEM] * 3,
        out_specs=IN_VMEM,
        compiler_params=params(4),
    )(rest_own, rest_came[0], total)

    blocks, rest_blocks, shifts = [new], [rest_new], [0]
    for hop in range(1, far + 1):
        for by in (-1, 1):
            if hop == far and by == 1:
                continue
            at = 0 if hop == 1 else (len(blocks) - 2)
            blocks.append(move(blocks[at], by))
            rest_blocks.append(move(rest_blocks[at], by))
            shifts.append(-by * hop % groups)
    return pl.pallas_call(
        functools.partial(place_kernel, shifts),
        out_shape=shaped((n_cent, depth), bf16),
        in_specs=[IN_HBM] * (2 * groups),
        out_specs=IN_HBM,
        scratch_shapes=[pltpu.SemaphoreType.DMA((2 * groups,))],
        compiler_params=params(4),
    )(*blocks, *rest_blocks)


def solution(mesh):
    placed = (P(("dp", "cent"), None), P("cent", None))
    return jax.shard_map(
        shards, mesh=mesh, in_specs=placed, out_specs=P("cent", None), check_vma=False
    )
```

```python
import functools
import math

import jax
import jax.numpy as jnp
from jax import lax
from jax.experimental import pallas as pl
from jax.experimental.pallas import tpu as pltpu
from jax.sharding import PartitionSpec as P

f32 = jnp.float32
bf16 = jnp.bfloat16
LANES = 128
BLOCK = 256
CHUNK = 16
SCALE = 3.0
EXP2_SCALE = SCALE * math.log2(math.e)
RING_Y, RING_X, CORES = 4, 4, 2
SMALL_SUM = 1e-20
LARGE_POT = 46.0
PAD = 16
NT = (((1,), (1,)), ((), ()))


def eye():
    rows = lax.broadcasted_iota(jnp.int32, (LANES, LANES), 0)
    cols = lax.broadcasted_iota(jnp.int32, (LANES, LANES), 1)
    return rows == cols


def to_row(column):
    return jnp.sum(jnp.where(eye(), column, 0.0), axis=0, keepdims=True)


def to_column(row):
    return jnp.sum(jnp.where(eye(), row, 0.0), axis=1, keepdims=True)


def fold(x, op):
    out = x[:, :LANES]
    for at in range(LANES, x.shape[1], LANES):
        out = op(out, x[:, at : at + LANES])
    return out


def merge(parts):
    peak = jnp.max(parts, axis=0)
    return peak + jnp.log(jnp.sum(jnp.exp(parts - peak[None]), axis=0))


def logits_block(cents, docs_ref, out_ref, rows, offset=0):
    width = 512
    for at in range(0, docs_ref.shape[0], width):
        out_ref[rows, offset + at : offset + at + width] = lax.dot_general(
            cents, docs_ref[at : at + width, :], NT, preferred_element_type=f32
        )


def place_on_cent():
    at = lax.axis_index("cent")
    return at // (RING_X * CORES), at // CORES % RING_X, at % CORES


def shifted(x, dy=0, dx=0, dc=0):
    pairs = []
    for y in range(RING_Y):
        for x_at in range(RING_X):
            for c in range(CORES):
                to = ((y + dy) % RING_Y * RING_X + (x_at + dx) % RING_X) * CORES + (c + dc) % CORES
                pairs.append(((y * RING_X + x_at) * CORES + c, to))
    return lax.ppermute(x, "cent", pairs)


def stack_blocks(out, offset, at, ring, own, before, after, across):
    size = own.shape[0]
    for shift, block in ((0, own), (ring - 1, before), (1, after), (2, across)):
        start = pl.multiple_of(offset + lax.rem(at + shift, ring) * size, size)
        out[pl.ds(start, size), :] = block


def near_kernel(own, x_before, x_after, x_across, y_before, y_after, y_across, along_x, along_y):
    y, x, _ = place_on_cent()
    half = own.shape[0] // 2
    stack_blocks(along_x, 0, x, RING_X, own[:half, :], x_before[...], x_after[...], x_across[...])
    stack_blocks(along_y, 0, y, RING_Y, own[half:, :], y_before[...], y_after[...], y_across[...])


def far_kernel(along_x, y_before, y_after, y_across, along_y, x_before, x_after, x_across, docs):
    y, x, _ = place_on_cent()
    stack_blocks(docs, 0, y, RING_Y, along_x[...], y_before[...], y_after[...], y_across[...])
    offset = docs.shape[0] // 2
    stack_blocks(docs, offset, x, RING_X, along_y[...], x_before[...], x_after[...], x_across[...])


def gather(own):
    half = own.shape[0] // 2
    first, second = own[:half], own[half:]
    along_x, along_y = pl.pallas_call(
        near_kernel,
        out_shape=[jax.ShapeDtypeStruct((4 * half, own.shape[1]), bf16)] * 2,
        in_specs=[IN_VMEM] * 7,
        out_specs=[IN_VMEM] * 2,
        compiler_params=params(8),
    )(
        own,
        *(shifted(first, dx=by) for by in (1, -1, 2)),
        *(shifted(second, dy=by) for by in (1, -1, 2)),
    )
    return pl.pallas_call(
        far_kernel,
        out_shape=jax.ShapeDtypeStruct((32 * half, own.shape[1]), bf16),
        in_specs=[IN_VMEM] * 8,
        out_specs=IN_VMEM,
        compiler_params=params(8),
    )(
        along_x,
        *(shifted(along_x, dy=by) for by in (1, -1, 2)),
        along_y,
        *(shifted(along_y, dx=by) for by in (1, -1, 2)),
    )


def own_kernel(docs_ref, cents_ref, raw_ref):
    def block(t, _):
        rows = pl.ds(pl.multiple_of(t * BLOCK, BLOCK), BLOCK)
        logits_block(cents_ref[rows, :], docs_ref, raw_ref, rows)
        return 0

    lax.fori_loop(0, cents_ref.shape[0] // BLOCK, block, 0)


def first_kernel(raw_ref, docs_ref, cents_ref, t_ref, peak_ref, lse_ref, even, odd, wide_peak, wide_lse, small):
    n_cent, n_own = raw_ref.shape
    n_blocks = n_cent // BLOCK
    tiles = n_own // LANES
    k = EXP2_SCALE

    def multiply(t, x_ref):
        start = pl.multiple_of(jnp.minimum(t, n_blocks - 1) * BLOCK, BLOCK)
        logits_block(cents_ref[pl.ds(start, BLOCK), :], docs_ref, x_ref, pl.ds(0, BLOCK))

    def finish(t, x_ref):
        for r in range(0, BLOCK, LANES):
            rows = pl.ds(pl.multiple_of(t * BLOCK + r, LANES), LANES)
            parts = [lambda b=b: raw_ref[rows, b * LANES : (b + 1) * LANES] for b in range(tiles)]
            parts += [lambda b=b: x_ref[r : r + LANES, b * LANES : (b + 1) * LANES] for b in range(tiles)]
            peak = parts[0]()
            for part in parts[1:]:
                peak = jnp.maximum(peak, part())
            peak = jnp.broadcast_to(jnp.max(peak, axis=1, keepdims=True), (LANES, LANES))
            total = jnp.zeros((LANES, LANES), f32)
            for b, part in enumerate(parts):
                e = jnp.exp2((part() - peak) * k)
                t_ref[rows, b * LANES : (b + 1) * LANES] = e
                total = total + e
            total = jnp.broadcast_to(jnp.sum(total, axis=1, keepdims=True), (LANES, LANES))
            wide_peak[rows, :] = peak * SCALE
            wide_lse[rows, :] = peak * SCALE + jnp.log(total)

    multiply(0, even)

    def pair(i, _):
        multiply(2 * i + 1, odd)
        finish(2 * i, even)
        multiply(2 * i + 2, even)
        finish(2 * i + 1, odd)
        return 0

    lax.fori_loop(0, n_blocks // 2, pair, 0)
    for b in range(n_cent // LANES):
        at = slice(b * LANES, (b + 1) * LANES)
        peak_ref[b : b + 1, :] = to_row(wide_peak[at, :])
        small[b : b + 1, :] = to_row(wide_lse[at, :])
    lse_ref[...] = jnp.broadcast_to(small[...][None], lse_ref.shape)


def common_order(b, n):
    _, _, core = place_on_cent()
    return lax.rem(b + core * (n // CORES), n)


def local_order(rows):
    _, _, core = place_on_cent()
    half = rows.shape[0] // CORES
    return jnp.where(core == 1, jnp.concatenate([rows[half:], rows[:half]], axis=0), rows)


def load_all(docs_hbm, cents_hbm, docs, cents):
    half = docs.shape[0] // 2
    pltpu.sync_copy(docs_hbm[0], docs.at[:half, :])
    pltpu.sync_copy(docs_hbm[1], docs.at[half:, :])
    pltpu.sync_copy(cents_hbm, cents)


def row_slow(docs_hbm, cents_hbm, col_wide, small):
    n_doc, n_cent = 2 * docs_hbm[0].shape[0], cents_hbm.shape[0]

    def body(docs, cents, x_ref, peak, total):
        load_all(docs_hbm, cents_hbm, docs, cents)
        peak[...] = jnp.full(peak.shape, -jnp.inf, f32)
        total[...] = jnp.zeros(total.shape, f32)

        def sweep(last):
            def block(t, _):
                start = pl.multiple_of(t * BLOCK, BLOCK)
                rows = pl.ds(start, BLOCK)
                logits_block(cents[rows, :], docs, x_ref, pl.ds(0, BLOCK))
                for at in range(0, n_doc, LANES):
                    y = x_ref[:, at : at + LANES] * SCALE + col_wide[rows, :]
                    here = peak[:, at : at + LANES]
                    if last:
                        total[:, at : at + LANES] += jnp.sum(jnp.exp(y - here), axis=0, keepdims=True)
                    else:
                        peak[:, at : at + LANES] = jnp.maximum(here, jnp.max(y, axis=0, keepdims=True))
                return 0

            lax.fori_loop(0, n_cent // BLOCK, block, 0)

        sweep(False)
        sweep(True)
        for b in range(n_doc // LANES):
            at = slice(b * LANES, (b + 1) * LANES)
            small[pl.ds(common_order(b, n_doc // LANES), 1), :] = peak[:, at] + jnp.log(total[:, at])

    pl.run_scoped(
        body,
        pltpu.VMEM((n_doc, cents_hbm.shape[1]), bf16),
        pltpu.VMEM(cents_hbm.shape, bf16),
        pltpu.VMEM((BLOCK, n_doc), f32),
        pltpu.VMEM((1, n_doc), f32),
        pltpu.VMEM((1, n_doc), f32),
    )


def row_kernel(log_ratio, t_ref, peak_ref, parts_ref, own_hbm, other_hbm, cents_hbm, lse_ref, col_ref, wide, acc, small):
    n_cent, n_doc = t_ref.shape
    col = log_ratio - merge(parts_ref[...])
    col_ref[...] = col
    factor = jnp.exp(peak_ref[...] + col)
    for b in range(n_cent // LANES):
        column = to_column(factor[b : b + 1, :])
        wide[b * LANES : (b + 1) * LANES, :] = jnp.broadcast_to(column, (LANES, LANES))
    acc[...] = jnp.zeros(acc.shape, f32)
    step = 64

    def block(t, _):
        start = pl.multiple_of(t * step, step)
        scale = wide[pl.ds(start, step), :]
        for at in range(0, n_doc, LANES):
            x = t_ref[pl.ds(start, step), at : at + LANES] * scale
            part = x[:8, :]
            for r in range(8, step, 8):
                part = part + x[r : r + 8, :]
            acc[:, at : at + LANES] += part
        return 0

    lax.fori_loop(0, n_cent // step, block, 0)
    least = jnp.full((1, LANES), jnp.inf, f32)
    for b in range(n_doc // LANES):
        total = jnp.sum(acc[:, b * LANES : (b + 1) * LANES], axis=0, keepdims=True)
        least = jnp.minimum(least, total)
        small[pl.ds(common_order(b, n_doc // LANES), 1), :] = jnp.log(total)

    @pl.when(jnp.logical_not(jnp.min(least) >= SMALL_SUM))
    def _():
        for b in range(n_cent // LANES):
            column = to_column(col[b : b + 1, :])
            wide[b * LANES : (b + 1) * LANES, :] = jnp.broadcast_to(column, (LANES, LANES))
        row_slow((own_hbm, other_hbm), cents_hbm, wide, small)

    lse_ref[...] = jnp.broadcast_to(small[...][None], lse_ref.shape)


def col_slow(docs_hbm, cents_hbm, row_pot, wide_lse):
    n_doc, n_cent = 2 * docs_hbm[0].shape[0], cents_hbm.shape[0]

    def body(docs, cents, x_ref):
        load_all(docs_hbm, cents_hbm, docs, cents)

        def block(t, _):
            start = pl.multiple_of(t * BLOCK, BLOCK)
            logits_block(cents[pl.ds(start, BLOCK), :], docs, x_ref, pl.ds(0, BLOCK))

            def chunk(c, _):
                at = pl.multiple_of(c * CHUNK, CHUNK)
                y = [
                    x_ref[pl.ds(at, CHUNK), b * LANES : (b + 1) * LANES] * SCALE + row_pot[b : b + 1, :]
                    for b in range(n_doc // LANES)
                ]
                peak = jnp.max(functools.reduce(jnp.maximum, y), axis=1, keepdims=True)
                total = jnp.sum(sum(jnp.exp(part - peak) for part in y), axis=1, keepdims=True)
                value = peak + jnp.log(total)
                wide_lse[pl.ds(start + at, CHUNK), :] = jnp.broadcast_to(value, (CHUNK, LANES))
                return 0

            return lax.fori_loop(0, BLOCK // CHUNK, chunk, 0)

        lax.fori_loop(0, n_cent // BLOCK, block, 0)

    pl.run_scoped(
        body,
        pltpu.VMEM((n_doc, cents_hbm.shape[1]), bf16),
        pltpu.VMEM(cents_hbm.shape, bf16),
        pltpu.VMEM((BLOCK, n_doc), f32),
    )


def col_kernel(t_ref, peak_ref, parts_ref, own_hbm, other_hbm, cents_hbm, lse_ref, wide_lse, small):
    n_cent, n_doc = t_ref.shape
    row_pot = local_order(-merge(parts_ref[...]))
    factor = jnp.exp(row_pot)
    step = 64

    def block(t, _):
        start = pl.multiple_of(t * step, step)
        total = jnp.zeros((step, LANES), f32)
        for b in range(n_doc // LANES):
            total = total + t_ref[pl.ds(start, step), b * LANES : (b + 1) * LANES] * factor[b : b + 1, :]
        total = jnp.sum(total, axis=1, keepdims=True)
        wide_lse[pl.ds(start, step), :] = jnp.log(jnp.broadcast_to(total, (step, LANES)))
        return 0

    lax.fori_loop(0, n_cent // step, block, 0)
    good = jnp.max(row_pot) <= LARGE_POT
    for b in range(n_cent // LANES):
        at = slice(b * LANES, (b + 1) * LANES)
        small[b : b + 1, :] = to_row(wide_lse[at, :]) + peak_ref[b : b + 1, :]

    @pl.when(jnp.logical_not(good))
    def _():
        def body(pot):
            pot[...] = row_pot
            col_slow((own_hbm, other_hbm), cents_hbm, pot, wide_lse)

        pl.run_scoped(body, pltpu.VMEM(row_pot.shape, f32))
        for b in range(n_cent // LANES):
            small[b : b + 1, :] = to_row(wide_lse[b * LANES : (b + 1) * LANES, :])

    lse_ref[...] = jnp.broadcast_to(small[...][None], lse_ref.shape)


def prepare_kernel(peak_ref, col_ref, parts_ref, wide, pot_ref, row_ref):
    row_pot = local_order(-merge(parts_ref[...]))
    good = jnp.max(row_pot) <= LARGE_POT
    row_ref[...] = row_pot
    pot_ref[...] = jnp.where(good, jnp.exp(row_pot), row_pot)
    by_col = jnp.where(good, jnp.exp(peak_ref[...] + col_ref[...]), col_ref[...])
    for b in range(by_col.shape[0]):
        column = to_column(by_col[b : b + 1, :])
        wide[b * LANES : (b + 1) * LANES, :] = jnp.broadcast_to(column, (LANES, LANES))


def split(value):
    high = value.astype(bf16).astype(f32)
    middle = (value - high).astype(bf16).astype(f32)
    low = value - high - middle
    row = lax.broadcasted_iota(jnp.int32, (PAD, LANES), 0)
    rows = jnp.where(row == 0, high, jnp.where(row == 1, middle, jnp.where(row == 2, low, 0.0)))
    return rows.astype(bf16)


def joined(rows):
    rows = rows.astype(f32)
    return rows[0:1] + rows[1:2] + rows[2:3]


def step_kernel(step, n_in, ends, *refs):
    t_ref, wide, pot_ref, row_ref, own_ref, other_ref, cents_hbm = refs[:7]
    came = refs[7 : 7 + n_in]
    first, second, rest_first, rest_second = refs[7 + n_in : 11 + n_in]
    if ends:
        mass_ref = refs[11 + n_in]
    groups, me = lax.axis_size("dp"), lax.axis_index("dp")
    ids = [lax.rem(me + shift, groups) for shift in (groups // 2 - step, groups // 2 + 1 + step)]
    plan = refs[-1]
    n_own, half = own_ref.shape[0], own_ref.shape[1] // 2
    n_doc = 2 * n_own
    good = jnp.max(row_ref[...]) <= LARGE_POT
    for k, (out, rest) in enumerate(((first, rest_first), (second, rest_second))):
        start = pl.multiple_of(ids[k] * BLOCK, BLOCK)

        @pl.when(good)
        def _():
            for r in range(0, BLOCK, LANES):
                rows = pl.ds(start + r, LANES)
                scale = wide[rows, :]
                for b in range(n_doc // LANES):
                    at = slice(b * LANES, (b + 1) * LANES)
                    plan[k, r : r + LANES, at] = (t_ref[rows, at] * scale * pot_ref[b : b + 1, :]).astype(bf16)

        @pl.when(jnp.logical_not(good))
        def _():
            def body(cents, x_ref):
                pltpu.sync_copy(cents_hbm.at[pl.ds(start, BLOCK), :], cents)
                logits_block(cents[...], own_ref, x_ref, pl.ds(0, BLOCK))
                logits_block(cents[...], other_ref, x_ref, pl.ds(0, BLOCK), n_own)
                col = wide[pl.ds(start, BLOCK), :]
                for b in range(n_doc // LANES):
                    at = slice(b * LANES, (b + 1) * LANES)
                    plan[k, :, at] = jnp.exp(x_ref[:, at] * SCALE + pot_ref[b : b + 1, :] + col).astype(bf16)

            pl.run_scoped(body, pltpu.VMEM((BLOCK, cents_hbm.shape[1]), bf16), pltpu.VMEM((BLOCK, n_doc), f32))

        sums = jnp.dot(plan[k, :, :n_own], own_ref[...], preferred_element_type=f32)
        sums = sums + jnp.dot(plan[k, :, n_own:], other_ref[...], preferred_element_type=f32)
        rest[...] = sums[:, half:].astype(rest.dtype)
        sums = sums[:, :half]
        if n_in:
            sums = sums + came[k][:BLOCK, :].astype(f32)
        if ends and k == 1:
            out[...] = sums
        else:
            out[:BLOCK, :] = sums.astype(bf16)
            out[BLOCK:, :] = jnp.zeros((PAD, half), bf16)
        for r in range(0, BLOCK, LANES):
            mass = fold(plan[k, r : r + LANES, :].astype(f32), jnp.add)
            mass = to_row(jnp.broadcast_to(jnp.sum(mass, axis=1, keepdims=True), (LANES, LANES)))
            if n_in:
                mass = mass + joined(came[k][BLOCK:, r : r + LANES])
            if ends and k == 1:
                mass_ref[r // LANES : r // LANES + 1, :] = mass
            else:
                out[BLOCK:, r : r + LANES] = split(mass)


def add_kernel(ends, *refs):
    for k in range(2):
        total = refs[k][...] + refs[2 + k][...].astype(f32)
        out = refs[4 + k]
        out[...] = total if ends and k == 1 else total.astype(bf16)


def divide_kernel(sums_ref, came_ref, mass_ref, out_ref, total_ref):
    for b in range(BLOCK // LANES):
        at = slice(b * LANES, (b + 1) * LANES)
        mass = mass_ref[b : b + 1, :] + joined(came_ref[BLOCK:, at])
        total_ref[b : b + 1, :] = mass
        out_ref[at, :] = ((sums_ref[at, :] + came_ref[at, :].astype(f32)) / to_column(mass)).astype(bf16)


def divide_rest_kernel(sums_ref, came_ref, mass_ref, out_ref):
    for b in range(BLOCK // LANES):
        at = slice(b * LANES, (b + 1) * LANES)
        out_ref[at, :] = (
            (sums_ref[at, :] + came_ref[at, :].astype(f32)) / to_column(mass_ref[b : b + 1, :])
        ).astype(bf16)


def place_kernel(shifts, *refs):
    n = len(shifts)
    me = lax.axis_index("dp")
    blocks, out, sems = refs[: 2 * n], refs[2 * n], refs[2 * n + 1]
    half = out.shape[1] // 2
    copies = []
    for at in range(2 * n):
        start = pl.multiple_of(lax.rem(me + shifts[at % n], n) * BLOCK, BLOCK)
        to = out.at[pl.ds(start, BLOCK), pl.ds((at // n) * half, half)]
        copy = pltpu.make_async_copy(blocks[at], to, sems.at[at])
        copy.start()
        copies.append(copy)
    for copy in copies:
        copy.wait()


IN_VMEM = pl.BlockSpec(memory_space=pltpu.VMEM)
IN_HBM = pl.BlockSpec(memory_space=pl.ANY)


def params(mib):
    return pltpu.CompilerParams(vmem_limit_bytes=mib * 2**20)


def shards(embeddings, centroids):
    groups, blocks = lax.axis_size("dp"), lax.axis_size("cent")
    own = gather(embeddings)
    other = shifted(own, dc=1)
    n_doc, depth = CORES * own.shape[0], own.shape[1]
    n_cent = centroids.shape[0]
    log_ratio = math.log(n_doc * groups / (n_cent * blocks))
    row_shape = (n_doc // LANES, LANES)
    col_shape = (n_cent // LANES, LANES)
    shaped = jax.ShapeDtypeStruct
    by_group = shaped((groups, *col_shape), f32)
    by_block = shaped((blocks, *row_shape), f32)
    wide = pltpu.VMEM((n_cent, LANES), f32)

    raw = pl.pallas_call(
        own_kernel,
        out_shape=pltpu.VMEM((n_cent, own.shape[0]), f32),
        in_specs=[IN_VMEM] * 2,
        out_specs=IN_VMEM,
        compiler_params=params(10),
        cost_estimate=pl.CostEstimate(flops=2 * n_cent * own.shape[0] * depth, bytes_accessed=12 * 2**20, transcendentals=0),
    )(own, centroids)
    t, peak, lse = pl.pallas_call(
        first_kernel,
        out_shape=(pltpu.VMEM((n_cent, n_doc), f32), shaped(col_shape, f32), by_group),
        in_specs=[IN_VMEM] * 3,
        out_specs=(IN_VMEM,) * 3,
        scratch_shapes=[pltpu.VMEM((BLOCK, own.shape[0]), f32)] * 2 + [wide, wide, pltpu.VMEM(col_shape, f32)],
        compiler_params=params(16),
    )(raw, other, centroids)

    def rows(lse):
        parts = lax.all_to_all(lse, "dp", 0, 0)
        return pl.pallas_call(
            functools.partial(row_kernel, log_ratio),
            out_shape=(by_block, shaped(col_shape, f32)),
            in_specs=[IN_VMEM] * 3 + [IN_HBM] * 3,
            out_specs=(IN_VMEM, IN_VMEM),
            scratch_shapes=[wide, pltpu.VMEM((8, n_doc), f32), pltpu.VMEM(row_shape, f32)],
            compiler_params=params(20),
        )(t, peak, parts, own, other, centroids)

    def cols(lse):
        parts = lax.all_to_all(lse, "cent", 0, 0)
        return pl.pallas_call(
            col_kernel,
            out_shape=by_group,
            in_specs=[IN_VMEM] * 3 + [IN_HBM] * 3,
            out_specs=IN_VMEM,
            scratch_shapes=[wide, pltpu.VMEM(col_shape, f32)],
            compiler_params=params(20),
        )(t, peak, parts, own, other, centroids)

    lse, _ = rows(lse)
    lse = cols(lse)
    lse, col = rows(lse)
    parts = lax.all_to_all(lse, "cent", 0, 0)
    wide_col, pot, row = pl.pallas_call(
        prepare_kernel,
        out_shape=(pltpu.VMEM((n_cent, LANES), f32), shaped(row_shape, f32), shaped(row_shape, f32)),
        in_specs=[IN_VMEM] * 3,
        out_specs=(IN_VMEM,) * 3,
        compiler_params=params(4),
    )(peak, col, parts)

    far = groups // 2
    half = depth // 2
    message = shaped((BLOCK + PAD, half), bf16)
    rest_message = shaped((BLOCK, half), bf16)
    rest = shaped((BLOCK, half), f32)

    def move(x, by):
        return lax.ppermute(x, "dp", [(i, (i + by) % groups) for i in range(groups)])

    came, rest_came = (), ()
    for s in range(far):
        ends = s == far - 1
        kept = rest if s else rest_message
        out = (message, rest if ends else message, kept, rest if ends else kept)
        out += (shaped((2, LANES), f32),) if ends else ()
        out = pl.pallas_call(
            functools.partial(step_kernel, s, len(came), ends),
            out_shape=out,
            in_specs=[IN_VMEM] * 6 + [IN_HBM] + [IN_VMEM] * len(came),
            out_specs=(IN_VMEM,) * len(out),
            scratch_shapes=[pltpu.VMEM((2, BLOCK, n_doc), bf16)],
            compiler_params=params(20),
            cost_estimate=pl.CostEstimate(flops=1, bytes_accessed=1, transcendentals=0),
        )(t, wide_col, pot, row, own, other, centroids, *came)
        if ends:
            right, own, rest_right, rest_own, mass = out
            came = (move(right, 1),)
        else:
            right, left, rest_right, rest_own = out
            came = (move(right, 1), move(left, -1))
        if s:
            rest_right, rest_own = pl.pallas_call(
                functools.partial(add_kernel, ends),
                out_shape=(rest_message, rest if ends else rest_message),
                in_specs=[IN_VMEM] * 4,
                out_specs=(IN_VMEM,) * 2,
                compiler_params=params(4),
            )(rest_right, rest_own, *rest_came)
        rest_came = (move(rest_right, 1),) if ends else (move(rest_right, 1), move(rest_own, -1))

    new, total = pl.pallas_call(
        divide_kernel,
        out_shape=(rest_message, shaped((2, LANES), f32)),
        in_specs=[IN_VMEM] * 3,
        out_specs=(IN_VMEM,) * 2,
        compiler_params=params(4),
    )(own, came[0], mass)
    rest_new = pl.pallas_call(
        divide_rest_kernel,
        out_shape=rest_message,
        in_specs=[IN_VMEM] * 3,
        out_specs=IN_VMEM,
        compiler_params=params(4),
    )(rest_own, rest_came[0], total)

    blocks, rest_blocks, shifts = [new], [rest_new], [0]
    for hop in range(1, far + 1):
        for by in (-1, 1):
            if hop == far and by == 1:
                continue
            at = 0 if hop == 1 else (len(blocks) - 2)
            blocks.append(move(blocks[at], by))
            rest_blocks.append(move(rest_blocks[at], by))
            shifts.append(-by * hop % groups)
    return pl.pallas_call(
        functools.partial(place_kernel, shifts),
        out_shape=shaped((n_cent, depth), bf16),
        in_specs=[IN_HBM] * (2 * groups),
        out_specs=IN_HBM,
        scratch_shapes=[pltpu.SemaphoreType.DMA((2 * groups,))],
        compiler_params=params(4),
    )(*blocks, *rest_blocks)


def solution(mesh):
    placed = (P(("dp", "cent"), None), P("cent", None))
    return jax.shard_map(
        shards, mesh=mesh, in_specs=placed, out_specs=P("cent", None), check_vma=False
    )
```

```python
import functools
import math

import jax
import jax.numpy as jnp
from jax import lax
from jax.experimental import pallas as pl
from jax.experimental.pallas import tpu as pltpu
from jax.sharding import PartitionSpec as P

f32 = jnp.float32
bf16 = jnp.bfloat16
LANES = 128
BLOCK = 256
CHUNK = 16
SCALE = 3.0
EXP2_SCALE = SCALE * math.log2(math.e)
RING_Y, RING_X, CORES = 4, 4, 2
SMALL_SUM = 1e-20
LARGE_POT = 46.0
PAD = 16
NT = (((1,), (1,)), ((), ()))


def eye():
    rows = lax.broadcasted_iota(jnp.int32, (LANES, LANES), 0)
    cols = lax.broadcasted_iota(jnp.int32, (LANES, LANES), 1)
    return rows == cols


def to_row(column):
    return jnp.sum(jnp.where(eye(), column, 0.0), axis=0, keepdims=True)


def to_column(row):
    return jnp.sum(jnp.where(eye(), row, 0.0), axis=1, keepdims=True)


def fold(x, op):
    out = x[:, :LANES]
    for at in range(LANES, x.shape[1], LANES):
        out = op(out, x[:, at : at + LANES])
    return out


def merge(parts):
    peak = jnp.max(parts, axis=0)
    return peak + jnp.log(jnp.sum(jnp.exp(parts - peak[None]), axis=0))


def logits_block(cents, docs_ref, out_ref, rows, offset=0):
    width = 512
    for at in range(0, docs_ref.shape[0], width):
        out_ref[rows, offset + at : offset + at + width] = lax.dot_general(
            cents, docs_ref[at : at + width, :], NT, preferred_element_type=f32
        )


def place_on_cent():
    at = lax.axis_index("cent")
    return at // (RING_X * CORES), at // CORES % RING_X, at % CORES


def shifted(x, dy=0, dx=0, dc=0):
    pairs = []
    for y in range(RING_Y):
        for x_at in range(RING_X):
            for c in range(CORES):
                to = ((y + dy) % RING_Y * RING_X + (x_at + dx) % RING_X) * CORES + (c + dc) % CORES
                pairs.append(((y * RING_X + x_at) * CORES + c, to))
    return lax.ppermute(x, "cent", pairs)


def stack_blocks(out, offset, at, ring, own, before, after, across):
    size = own.shape[0]
    for shift, block in ((0, own), (ring - 1, before), (1, after), (2, across)):
        start = pl.multiple_of(offset + lax.rem(at + shift, ring) * size, size)
        out[pl.ds(start, size), :] = block


def near_kernel(first, second, x_before, x_after, x_across, y_before, y_after, y_across, along_x, along_y):
    y, x, _ = place_on_cent()
    stack_blocks(along_x, 0, x, RING_X, first[...], x_before[...], x_after[...], x_across[...])
    stack_blocks(along_y, 0, y, RING_Y, second[...], y_before[...], y_after[...], y_across[...])


def far_kernel(along_x, y_before, y_after, y_across, along_y, x_before, x_after, x_across, docs):
    y, x, _ = place_on_cent()
    stack_blocks(docs, 0, y, RING_Y, along_x[...], y_before[...], y_after[...], y_across[...])
    offset = docs.shape[0] // 2
    stack_blocks(docs, offset, x, RING_X, along_y[...], x_before[...], x_after[...], x_across[...])


def gather(own):
    half = own.shape[0] // 2
    first, second = own[:half], own[half:]
    along_x, along_y = pl.pallas_call(
        near_kernel,
        out_shape=[jax.ShapeDtypeStruct((4 * half, own.shape[1]), bf16)] * 2,
        in_specs=[IN_VMEM] * 8,
        out_specs=[IN_VMEM] * 2,
        compiler_params=params(8),
    )(
        first,
        second,
        *(shifted(first, dx=by) for by in (1, -1, 2)),
        *(shifted(second, dy=by) for by in (1, -1, 2)),
    )
    return pl.pallas_call(
        far_kernel,
        out_shape=jax.ShapeDtypeStruct((32 * half, own.shape[1]), bf16),
        in_specs=[IN_VMEM] * 8,
        out_specs=IN_VMEM,
        compiler_params=params(8),
    )(
        along_x,
        *(shifted(along_x, dy=by) for by in (1, -1, 2)),
        along_y,
        *(shifted(along_y, dx=by) for by in (1, -1, 2)),
    )


def own_kernel(docs_ref, cents_ref, raw_ref):
    def block(t, _):
        rows = pl.ds(pl.multiple_of(t * BLOCK, BLOCK), BLOCK)
        logits_block(cents_ref[rows, :], docs_ref, raw_ref, rows)
        return 0

    lax.fori_loop(0, cents_ref.shape[0] // BLOCK, block, 0)


def first_kernel(raw_ref, docs_ref, cents_ref, t_ref, peak_ref, lse_ref, even, odd, wide_peak, wide_lse, small):
    n_cent, n_own = raw_ref.shape
    n_blocks = n_cent // BLOCK
    tiles = n_own // LANES
    k = EXP2_SCALE

    def multiply(t, x_ref):
        start = pl.multiple_of(jnp.minimum(t, n_blocks - 1) * BLOCK, BLOCK)
        logits_block(cents_ref[pl.ds(start, BLOCK), :], docs_ref, x_ref, pl.ds(0, BLOCK))

    def finish(t, x_ref):
        for r in range(0, BLOCK, LANES):
            rows = pl.ds(pl.multiple_of(t * BLOCK + r, LANES), LANES)
            parts = [lambda b=b: raw_ref[rows, b * LANES : (b + 1) * LANES] for b in range(tiles)]
            parts += [lambda b=b: x_ref[r : r + LANES, b * LANES : (b + 1) * LANES] for b in range(tiles)]
            peak = parts[0]()
            for part in parts[1:]:
                peak = jnp.maximum(peak, part())
            peak = jnp.broadcast_to(jnp.max(peak, axis=1, keepdims=True), (LANES, LANES))
            total = jnp.zeros((LANES, LANES), f32)
            for b, part in enumerate(parts):
                e = jnp.exp2((part() - peak) * k)
                t_ref[rows, b * LANES : (b + 1) * LANES] = e
                total = total + e
            total = jnp.broadcast_to(jnp.sum(total, axis=1, keepdims=True), (LANES, LANES))
            wide_peak[rows, :] = peak * SCALE
            wide_lse[rows, :] = peak * SCALE + jnp.log(total)

    multiply(0, even)

    def pair(i, _):
        multiply(2 * i + 1, odd)
        finish(2 * i, even)
        multiply(2 * i + 2, even)
        finish(2 * i + 1, odd)
        return 0

    lax.fori_loop(0, n_blocks // 2, pair, 0)
    for b in range(n_cent // LANES):
        at = slice(b * LANES, (b + 1) * LANES)
        peak_ref[b : b + 1, :] = to_row(wide_peak[at, :])
        small[b : b + 1, :] = to_row(wide_lse[at, :])
    lse_ref[...] = jnp.broadcast_to(small[...][None], lse_ref.shape)


def common_order(b, n):
    _, _, core = place_on_cent()
    return lax.rem(b + core * (n // CORES), n)


def local_order(rows):
    _, _, core = place_on_cent()
    half = rows.shape[0] // CORES
    return jnp.where(core == 1, jnp.concatenate([rows[half:], rows[:half]], axis=0), rows)


def load_all(docs_hbm, cents_hbm, docs, cents):
    half = docs.shape[0] // 2
    pltpu.sync_copy(docs_hbm[0], docs.at[:half, :])
    pltpu.sync_copy(docs_hbm[1], docs.at[half:, :])
    pltpu.sync_copy(cents_hbm, cents)


def row_slow(docs_hbm, cents_hbm, col_wide, small):
    n_doc, n_cent = 2 * docs_hbm[0].shape[0], cents_hbm.shape[0]

    def body(docs, cents, x_ref, peak, total):
        load_all(docs_hbm, cents_hbm, docs, cents)
        peak[...] = jnp.full(peak.shape, -jnp.inf, f32)
        total[...] = jnp.zeros(total.shape, f32)

        def sweep(last):
            def block(t, _):
                start = pl.multiple_of(t * BLOCK, BLOCK)
                rows = pl.ds(start, BLOCK)
                logits_block(cents[rows, :], docs, x_ref, pl.ds(0, BLOCK))
                for at in range(0, n_doc, LANES):
                    y = x_ref[:, at : at + LANES] * SCALE + col_wide[rows, :]
                    here = peak[:, at : at + LANES]
                    if last:
                        total[:, at : at + LANES] += jnp.sum(jnp.exp(y - here), axis=0, keepdims=True)
                    else:
                        peak[:, at : at + LANES] = jnp.maximum(here, jnp.max(y, axis=0, keepdims=True))
                return 0

            lax.fori_loop(0, n_cent // BLOCK, block, 0)

        sweep(False)
        sweep(True)
        for b in range(n_doc // LANES):
            at = slice(b * LANES, (b + 1) * LANES)
            small[pl.ds(common_order(b, n_doc // LANES), 1), :] = peak[:, at] + jnp.log(total[:, at])

    pl.run_scoped(
        body,
        pltpu.VMEM((n_doc, cents_hbm.shape[1]), bf16),
        pltpu.VMEM(cents_hbm.shape, bf16),
        pltpu.VMEM((BLOCK, n_doc), f32),
        pltpu.VMEM((1, n_doc), f32),
        pltpu.VMEM((1, n_doc), f32),
    )


def row_kernel(log_ratio, t_ref, peak_ref, parts_ref, own_hbm, other_hbm, cents_hbm, lse_ref, col_ref, wide, acc, small):
    n_cent, n_doc = t_ref.shape
    col = log_ratio - merge(parts_ref[...])
    col_ref[...] = col
    factor = jnp.exp(peak_ref[...] + col)
    for b in range(n_cent // LANES):
        column = to_column(factor[b : b + 1, :])
        wide[b * LANES : (b + 1) * LANES, :] = jnp.broadcast_to(column, (LANES, LANES))
    acc[...] = jnp.zeros(acc.shape, f32)
    step = 64

    def block(t, _):
        start = pl.multiple_of(t * step, step)
        scale = wide[pl.ds(start, step), :]
        for at in range(0, n_doc, LANES):
            x = t_ref[pl.ds(start, step), at : at + LANES] * scale
            part = x[:8, :]
            for r in range(8, step, 8):
                part = part + x[r : r + 8, :]
            acc[:, at : at + LANES] += part
        return 0

    lax.fori_loop(0, n_cent // step, block, 0)
    least = jnp.full((1, LANES), jnp.inf, f32)
    for b in range(n_doc // LANES):
        total = jnp.sum(acc[:, b * LANES : (b + 1) * LANES], axis=0, keepdims=True)
        least = jnp.minimum(least, total)
        small[pl.ds(common_order(b, n_doc // LANES), 1), :] = jnp.log(total)

    @pl.when(jnp.logical_not(jnp.min(least) >= SMALL_SUM))
    def _():
        for b in range(n_cent // LANES):
            column = to_column(col[b : b + 1, :])
            wide[b * LANES : (b + 1) * LANES, :] = jnp.broadcast_to(column, (LANES, LANES))
        row_slow((own_hbm, other_hbm), cents_hbm, wide, small)

    lse_ref[...] = jnp.broadcast_to(small[...][None], lse_ref.shape)


def col_slow(docs_hbm, cents_hbm, row_pot, wide_lse):
    n_doc, n_cent = 2 * docs_hbm[0].shape[0], cents_hbm.shape[0]

    def body(docs, cents, x_ref):
        load_all(docs_hbm, cents_hbm, docs, cents)

        def block(t, _):
            start = pl.multiple_of(t * BLOCK, BLOCK)
            logits_block(cents[pl.ds(start, BLOCK), :], docs, x_ref, pl.ds(0, BLOCK))

            def chunk(c, _):
                at = pl.multiple_of(c * CHUNK, CHUNK)
                y = [
                    x_ref[pl.ds(at, CHUNK), b * LANES : (b + 1) * LANES] * SCALE + row_pot[b : b + 1, :]
                    for b in range(n_doc // LANES)
                ]
                peak = jnp.max(functools.reduce(jnp.maximum, y), axis=1, keepdims=True)
                total = jnp.sum(sum(jnp.exp(part - peak) for part in y), axis=1, keepdims=True)
                value = peak + jnp.log(total)
                wide_lse[pl.ds(start + at, CHUNK), :] = jnp.broadcast_to(value, (CHUNK, LANES))
                return 0

            return lax.fori_loop(0, BLOCK // CHUNK, chunk, 0)

        lax.fori_loop(0, n_cent // BLOCK, block, 0)

    pl.run_scoped(
        body,
        pltpu.VMEM((n_doc, cents_hbm.shape[1]), bf16),
        pltpu.VMEM(cents_hbm.shape, bf16),
        pltpu.VMEM((BLOCK, n_doc), f32),
    )


def col_kernel(t_ref, peak_ref, parts_ref, own_hbm, other_hbm, cents_hbm, lse_ref, wide_lse, small):
    n_cent, n_doc = t_ref.shape
    row_pot = local_order(-merge(parts_ref[...]))
    factor = jnp.exp(row_pot)
    step = 64

    def block(t, _):
        start = pl.multiple_of(t * step, step)
        total = jnp.zeros((step, LANES), f32)
        for b in range(n_doc // LANES):
            total = total + t_ref[pl.ds(start, step), b * LANES : (b + 1) * LANES] * factor[b : b + 1, :]
        wide_lse[pl.ds(start, step), :] = total
        return 0

    lax.fori_loop(0, n_cent // step, block, 0)
    good = jnp.max(row_pot) <= LARGE_POT
    for b in range(n_cent // LANES):
        at = slice(b * LANES, (b + 1) * LANES)
        total = jnp.sum(wide_lse[at, :], axis=1, keepdims=True)
        small[b : b + 1, :] = jnp.log(to_row(jnp.broadcast_to(total, (LANES, LANES)))) + peak_ref[b : b + 1, :]

    @pl.when(jnp.logical_not(good))
    def _():
        def body(pot):
            pot[...] = row_pot
            col_slow((own_hbm, other_hbm), cents_hbm, pot, wide_lse)

        pl.run_scoped(body, pltpu.VMEM(row_pot.shape, f32))
        for b in range(n_cent // LANES):
            small[b : b + 1, :] = to_row(wide_lse[b * LANES : (b + 1) * LANES, :])

    lse_ref[...] = jnp.broadcast_to(small[...][None], lse_ref.shape)


def prepare_kernel(peak_ref, col_ref, parts_ref, wide, pot_ref, row_ref):
    row_pot = local_order(-merge(parts_ref[...]))
    good = jnp.max(row_pot) <= LARGE_POT
    row_ref[...] = row_pot
    pot_ref[...] = jnp.where(good, jnp.exp(row_pot), row_pot)
    by_col = jnp.where(good, jnp.exp(peak_ref[...] + col_ref[...]), col_ref[...])
    for b in range(by_col.shape[0]):
        column = to_column(by_col[b : b + 1, :])
        wide[b * LANES : (b + 1) * LANES, :] = jnp.broadcast_to(column, (LANES, LANES))


def split(value):
    high = value.astype(bf16).astype(f32)
    middle = (value - high).astype(bf16).astype(f32)
    low = value - high - middle
    row = lax.broadcasted_iota(jnp.int32, (PAD, LANES), 0)
    rows = jnp.where(row == 0, high, jnp.where(row == 1, middle, jnp.where(row == 2, low, 0.0)))
    return rows.astype(bf16)


def joined(rows):
    rows = rows.astype(f32)
    return rows[0:1] + rows[1:2] + rows[2:3]


def product_kernel(shifts, *refs):
    t_ref, wide, pot_ref, row_ref, own_ref, other_ref, cents_hbm = refs[:7]
    outs, mass_ref, plan = refs[7:-2], refs[-2], refs[-1]
    groups, me = lax.axis_size("dp"), lax.axis_index("dp")
    n_own = own_ref.shape[0]
    n_doc = 2 * n_own
    half = own_ref.shape[1] // 2
    good = jnp.max(row_ref[...]) <= LARGE_POT
    for k, shift in enumerate(shifts):
        start = pl.multiple_of(lax.rem(me + shift, groups) * BLOCK, BLOCK)

        @pl.when(good)
        def _():
            for r in range(0, BLOCK, LANES):
                rows = pl.ds(start + r, LANES)
                scale = wide[rows, :]
                for b in range(n_doc // LANES):
                    at = slice(b * LANES, (b + 1) * LANES)
                    plan[k, r : r + LANES, at] = (t_ref[rows, at] * scale * pot_ref[b : b + 1, :]).astype(bf16)

        @pl.when(jnp.logical_not(good))
        def _():
            def body(cents, x_ref):
                pltpu.sync_copy(cents_hbm.at[pl.ds(start, BLOCK), :], cents)
                logits_block(cents[...], own_ref, x_ref, pl.ds(0, BLOCK))
                logits_block(cents[...], other_ref, x_ref, pl.ds(0, BLOCK), n_own)
                col = wide[pl.ds(start, BLOCK), :]
                for b in range(n_doc // LANES):
                    at = slice(b * LANES, (b + 1) * LANES)
                    plan[k, :, at] = jnp.exp(x_ref[:, at] * SCALE + pot_ref[b : b + 1, :] + col).astype(bf16)

            pl.run_scoped(body, pltpu.VMEM((BLOCK, cents_hbm.shape[1]), bf16), pltpu.VMEM((BLOCK, n_doc), f32))

        masses = []
        for r in range(0, BLOCK, LANES):
            mass = fold(plan[k, r : r + LANES, :].astype(f32), jnp.add)
            masses.append(to_row(jnp.broadcast_to(jnp.sum(mass, axis=1, keepdims=True), (LANES, LANES))))
        sums = jnp.dot(plan[k, :, :n_own], own_ref[...], preferred_element_type=f32)
        sums = sums + jnp.dot(plan[k, :, n_own:], other_ref[...], preferred_element_type=f32)
        if len(outs) == 2:
            for j, mass in enumerate(masses):
                mass_ref[2 * k + j : 2 * k + j + 1, :] = mass
            outs[0][k * BLOCK : (k + 1) * BLOCK, :] = sums[:, :half]
            outs[1][k * BLOCK : (k + 1) * BLOCK, :] = sums[:, half:]
        else:
            mass_ref[...] = jnp.concatenate(masses, axis=0)
            for j, mass in enumerate(masses):
                rows = slice(j * LANES, (j + 1) * LANES)
                send(outs[j], sums[rows, :half], [mass])
                outs[2 + j][...] = sums[rows, half:].astype(bf16)


def send(out, sums, masses):
    n = sums.shape[0]
    out[:n, :] = sums.astype(bf16)
    out[n:, :] = jnp.zeros((PAD, sums.shape[1]), bf16)
    for j, mass in enumerate(masses):
        out[n:, j * LANES : (j + 1) * LANES] = split(mass)


def mass_of(came, j):
    return joined(came[came.shape[0] - PAD :, j * LANES : (j + 1) * LANES])


def add_kernel(part, sums_ref, mass_ref, right_ref, left_ref, right_out, left_out):
    for k, (came, out) in enumerate(((right_ref, right_out), (left_ref, left_out))):
        sums = sums_ref[k * BLOCK : (k + 1) * BLOCK, :]
        masses = [mass_ref[2 * k + j : 2 * k + j + 1, :] for j in range(2)]
        n = came.shape[0] - PAD
        if part:
            parts = [sums[:n, :], sums[n:, :]]
            parts[k] = parts[k] + came[:n, :].astype(f32)
            masses[k] = masses[k] + mass_of(came, 0)
            sums = jnp.concatenate(parts, axis=0)
        else:
            sums = sums + came[:n, :].astype(f32)
            masses = [mass + mass_of(came, j) for j, mass in enumerate(masses)]
        send(out, sums, masses)


def add_rest_kernel(part, sums_ref, right_ref, left_ref, right_out, left_out):
    for k, (came, out) in enumerate(((right_ref, right_out), (left_ref, left_out))):
        n = came.shape[0]
        first = k * BLOCK
        if part:
            for j in range(2):
                sums = sums_ref[first + j * n : first + (j + 1) * n, :]
                out[j * n : (j + 1) * n, :] = (sums + came[...].astype(f32) if j == k else sums).astype(bf16)
        else:
            out[...] = (sums_ref[first : first + BLOCK, :] + came[...].astype(f32)).astype(bf16)


def divide_kernel(sums_ref, mass_ref, right_ref, left_ref, out_ref, total_ref):
    for b in range(BLOCK // LANES):
        at = slice(b * LANES, (b + 1) * LANES)
        mass = mass_ref[b : b + 1, :] + (mass_of(right_ref, b) + mass_of(left_ref, b))
        total_ref[b : b + 1, :] = mass
        sums = sums_ref[at, :] + (right_ref[at, :].astype(f32) + left_ref[at, :].astype(f32))
        out_ref[at, :] = (sums / to_column(mass)).astype(bf16)


def divide_rest_kernel(sums_ref, mass_ref, right_ref, left_ref, out_ref):
    for b in range(BLOCK // LANES):
        at = slice(b * LANES, (b + 1) * LANES)
        sums = sums_ref[at, :] + (right_ref[at, :].astype(f32) + left_ref[at, :].astype(f32))
        out_ref[at, :] = (sums / to_column(mass_ref[b : b + 1, :])).astype(bf16)


def place_kernel(places, *refs):
    blocks, out, sems = refs[: len(places)], refs[-2], refs[-1]
    groups, me = lax.axis_size("dp"), lax.axis_index("dp")
    half = out.shape[1] // 2
    copies = []
    for at, (shift, row, column) in enumerate(places):
        start = pl.multiple_of(lax.rem(me + shift, groups) * BLOCK + row, LANES)
        to = out.at[pl.ds(start, blocks[at].shape[0]), pl.ds(column * half, half)]
        copy = pltpu.make_async_copy(blocks[at], to, sems.at[at])
        copy.start()
        copies.append(copy)
    for copy in copies:
        copy.wait()


IN_VMEM = pl.BlockSpec(memory_space=pltpu.VMEM)
IN_HBM = pl.BlockSpec(memory_space=pl.ANY)


def params(mib):
    return pltpu.CompilerParams(vmem_limit_bytes=mib * 2**20)


def shards(embeddings, centroids):
    groups, blocks = lax.axis_size("dp"), lax.axis_size("cent")
    own = gather(embeddings)
    other = shifted(own, dc=1)
    n_doc, depth = CORES * own.shape[0], own.shape[1]
    n_cent = centroids.shape[0]
    log_ratio = math.log(n_doc * groups / (n_cent * blocks))
    row_shape = (n_doc // LANES, LANES)
    col_shape = (n_cent // LANES, LANES)
    shaped = jax.ShapeDtypeStruct
    by_group = shaped((groups, *col_shape), f32)
    by_block = shaped((blocks, *row_shape), f32)
    wide = pltpu.VMEM((n_cent, LANES), f32)

    raw = pl.pallas_call(
        own_kernel,
        out_shape=pltpu.VMEM((n_cent, own.shape[0]), f32),
        in_specs=[IN_VMEM] * 2,
        out_specs=IN_VMEM,
        compiler_params=params(10),
        cost_estimate=pl.CostEstimate(flops=2 * n_cent * own.shape[0] * depth, bytes_accessed=12 * 2**20, transcendentals=0),
    )(own, centroids)
    t, peak, lse = pl.pallas_call(
        first_kernel,
        out_shape=(pltpu.VMEM((n_cent, n_doc), f32), shaped(col_shape, f32), by_group),
        in_specs=[IN_VMEM] * 3,
        out_specs=(IN_VMEM,) * 3,
        scratch_shapes=[pltpu.VMEM((BLOCK, own.shape[0]), f32)] * 2 + [wide, wide, pltpu.VMEM(col_shape, f32)],
        compiler_params=params(16),
    )(raw, other, centroids)

    def rows(lse):
        parts = lax.all_to_all(lse, "dp", 0, 0)
        return pl.pallas_call(
            functools.partial(row_kernel, log_ratio),
            out_shape=(by_block, shaped(col_shape, f32)),
            in_specs=[IN_VMEM] * 3 + [IN_HBM] * 3,
            out_specs=(IN_VMEM, IN_VMEM),
            scratch_shapes=[wide, pltpu.VMEM((8, n_doc), f32), pltpu.VMEM(row_shape, f32)],
            compiler_params=params(20),
        )(t, peak, parts, own, other, centroids)

    def cols(lse):
        parts = lax.all_to_all(lse, "cent", 0, 0)
        return pl.pallas_call(
            col_kernel,
            out_shape=by_group,
            in_specs=[IN_VMEM] * 3 + [IN_HBM] * 3,
            out_specs=IN_VMEM,
            scratch_shapes=[wide, pltpu.VMEM(col_shape, f32)],
            compiler_params=params(20),
        )(t, peak, parts, own, other, centroids)

    lse, _ = rows(lse)
    lse = cols(lse)
    lse, col = rows(lse)
    parts = lax.all_to_all(lse, "cent", 0, 0)
    wide_col, pot, row = pl.pallas_call(
        prepare_kernel,
        out_shape=(pltpu.VMEM((n_cent, LANES), f32), shaped(row_shape, f32), shaped(row_shape, f32)),
        in_specs=[IN_VMEM] * 3,
        out_specs=(IN_VMEM,) * 3,
        compiler_params=params(4),
    )(peak, col, parts)

    far = groups // 2
    half = depth // 2
    free = pl.CostEstimate(flops=1, bytes_accessed=1, transcendentals=0)

    def message(rows):
        return shaped((rows, half), bf16)

    def move(x, by):
        return lax.ppermute(x, "dp", [(i, (i + by) % groups) for i in range(groups)])

    def products(shifts, outs, n_mass):
        return pl.pallas_call(
            functools.partial(product_kernel, shifts),
            out_shape=(*outs, shaped((n_mass, LANES), f32)),
            in_specs=[IN_VMEM] * 6 + [IN_HBM],
            out_specs=(IN_VMEM,) * (len(outs) + 1),
            scratch_shapes=[pltpu.VMEM((len(shifts), BLOCK, n_doc), bf16)],
            compiler_params=params(20),
            cost_estimate=free,
        )(t, wide_col, pot, row, own, other, centroids)

    def small_call(kernel, outs, *args):
        return pl.pallas_call(
            kernel,
            out_shape=outs,
            in_specs=[IN_VMEM] * len(args),
            out_specs=(IN_VMEM,) * len(outs) if isinstance(outs, tuple) else IN_VMEM,
            compiler_params=params(6),
            cost_estimate=free,
        )(*args)

    outs = (message(LANES + PAD),) * 2 + (message(LANES),) * 2
    right, left, rest_right, rest_left, _ = products([far], outs, 2)
    for s in range(1, far):
        right, left = move(right, 1), move(left, -1)
        rest_right, rest_left = move(rest_right, 1), move(rest_left, -1)
        outs = (shaped((2 * BLOCK, half), f32),) * 2
        sums, rest, mass = products([far - s, far + s], outs, 4)
        right, left = small_call(
            functools.partial(add_kernel, s == 1), (message(BLOCK + PAD),) * 2, sums, mass, right, left
        )
        rest_right, rest_left = small_call(
            functools.partial(add_rest_kernel, s == 1), (message(BLOCK),) * 2, rest, rest_right, rest_left
        )
    right, left = move(right, 1), move(left, -1)
    rest_right, rest_left = move(rest_right, 1), move(rest_left, -1)
    sums, rest, mass = products([0], (shaped((BLOCK, half), f32),) * 2, 2)
    new, total = small_call(
        divide_kernel, (message(BLOCK), shaped((2, LANES), f32)), sums, mass, right, left
    )
    rest_new = small_call(divide_rest_kernel, message(BLOCK), rest, total, rest_right, rest_left)

    blocks, places = [], []
    for column, block in enumerate((new, rest_new)):
        blocks.append(block)
        places.append((0, 0, column))
        held = {1: block, -1: block}
        for hop in range(1, far + 1):
            for by, rows in ((1, slice(0, LANES)), (-1, slice(LANES, BLOCK))):
                held[by] = move(held[by][rows] if hop == far else held[by], by)
                blocks.append(held[by])
                places.append((-by * hop % groups, rows.start if hop == far else 0, column))
    return pl.pallas_call(
        functools.partial(place_kernel, places),
        out_shape=shaped((n_cent, depth), bf16),
        in_specs=[IN_HBM] * len(blocks),
        out_specs=IN_HBM,
        scratch_shapes=[pltpu.SemaphoreType.DMA((len(blocks),))],
        compiler_params=params(4),
    )(*blocks)


def solution(mesh):
    placed = (P(("dp", "cent"), None), P("cent", None))
    return jax.shard_map(
        shards, mesh=mesh, in_specs=placed, out_specs=P("cent", None), check_vma=False
    )
```

```python
import functools
import math

import jax
import jax.numpy as jnp
from jax import lax
from jax.experimental import pallas as pl
from jax.experimental.pallas import tpu as pltpu
from jax.sharding import PartitionSpec as P

f32 = jnp.float32
bf16 = jnp.bfloat16
LANES = 128
BLOCK = 256
CHUNK = 16
SCALE = 3.0
EXP2_SCALE = SCALE * math.log2(math.e)
RING_Y, RING_X, CORES = 4, 4, 2
SMALL_SUM = 1e-20
LARGE_POT = 46.0
PAD = 16
NT = (((1,), (1,)), ((), ()))


def eye():
    rows = lax.broadcasted_iota(jnp.int32, (LANES, LANES), 0)
    cols = lax.broadcasted_iota(jnp.int32, (LANES, LANES), 1)
    return rows == cols


def to_row(column):
    return jnp.sum(jnp.where(eye(), column, 0.0), axis=0, keepdims=True)


def to_column(row):
    return jnp.sum(jnp.where(eye(), row, 0.0), axis=1, keepdims=True)


def fold(x, op):
    out = x[:, :LANES]
    for at in range(LANES, x.shape[1], LANES):
        out = op(out, x[:, at : at + LANES])
    return out


def merge(parts):
    peak = jnp.max(parts, axis=0)
    return peak + jnp.log(jnp.sum(jnp.exp(parts - peak[None]), axis=0))


def logits_block(cents, docs_ref, out_ref, rows, offset=0):
    width = 512
    for at in range(0, docs_ref.shape[0], width):
        out_ref[rows, offset + at : offset + at + width] = lax.dot_general(
            cents, docs_ref[at : at + width, :], NT, preferred_element_type=f32
        )


def place_on_cent():
    at = lax.axis_index("cent")
    return at // (RING_X * CORES), at // CORES % RING_X, at % CORES


def on_cent(x, place):
    pairs = []
    for y in range(RING_Y):
        for x_at in range(RING_X):
            for core in range(CORES):
                to_y, to_x, to_core = place(y, x_at, core)
                to = (to_y % RING_Y * RING_X + to_x % RING_X) * CORES + to_core % CORES
                pairs.append(((y * RING_X + x_at) * CORES + core, to))
    return lax.ppermute(x, "cent", pairs)


def along(x, first, by):
    return on_cent(x, lambda y, x_at, core: (y, x_at + by, core) if (core == 0) == first else (y + by, x_at, core))


def stack_kernel(first, own, before, after, across, out):
    y, x, core = place_on_cent()
    at = jnp.where((core == 0) == first, x, y)
    size = own.shape[0]
    for shift, block in ((0, own), (RING_X - 1, before), (1, after), (2, across)):
        start = pl.multiple_of(lax.rem(at + shift, RING_X) * size, size)
        out[pl.ds(start, size), :] = block[...]


def gather(own):
    for first in (True, False):
        own = pl.pallas_call(
            functools.partial(stack_kernel, first),
            out_shape=jax.ShapeDtypeStruct((RING_X * own.shape[0], own.shape[1]), bf16),
            in_specs=[IN_VMEM] * 4,
            out_specs=IN_VMEM,
            compiler_params=params(8),
        )(own, *(along(own, first, by) for by in (1, -1, 2)))
    return own


def own_kernel(docs_ref, cents_ref, raw_ref):
    def block(t, _):
        rows = pl.ds(pl.multiple_of(t * BLOCK, BLOCK), BLOCK)
        logits_block(cents_ref[rows, :], docs_ref, raw_ref, rows)
        return 0

    lax.fori_loop(0, cents_ref.shape[0] // BLOCK, block, 0)


def first_kernel(raw_ref, docs_ref, cents_ref, t_ref, peak_ref, lse_ref, even, odd, wide_peak, wide_lse, small):
    n_cent, n_own = raw_ref.shape
    n_blocks = n_cent // BLOCK
    tiles = n_own // LANES
    k = EXP2_SCALE

    def multiply(t, x_ref):
        start = pl.multiple_of(jnp.minimum(t, n_blocks - 1) * BLOCK, BLOCK)
        logits_block(cents_ref[pl.ds(start, BLOCK), :], docs_ref, x_ref, pl.ds(0, BLOCK))

    def finish(t, x_ref):
        for r in range(0, BLOCK, LANES):
            rows = pl.ds(pl.multiple_of(t * BLOCK + r, LANES), LANES)
            parts = [lambda b=b: raw_ref[rows, b * LANES : (b + 1) * LANES] for b in range(tiles)]
            parts += [lambda b=b: x_ref[r : r + LANES, b * LANES : (b + 1) * LANES] for b in range(tiles)]
            peak = parts[0]()
            for part in parts[1:]:
                peak = jnp.maximum(peak, part())
            peak = jnp.broadcast_to(jnp.max(peak, axis=1, keepdims=True), (LANES, LANES))
            total = jnp.zeros((LANES, LANES), f32)
            for b, part in enumerate(parts):
                e = jnp.exp2((part() - peak) * k)
                t_ref[rows, b * LANES : (b + 1) * LANES] = e
                total = total + e
            total = jnp.broadcast_to(jnp.sum(total, axis=1, keepdims=True), (LANES, LANES))
            wide_peak[rows, :] = peak * SCALE
            wide_lse[rows, :] = peak * SCALE + jnp.log(total)

    multiply(0, even)

    def pair(i, _):
        multiply(2 * i + 1, odd)
        finish(2 * i, even)
        multiply(2 * i + 2, even)
        finish(2 * i + 1, odd)
        return 0

    lax.fori_loop(0, n_blocks // 2, pair, 0)
    for b in range(n_cent // LANES):
        at = slice(b * LANES, (b + 1) * LANES)
        peak_ref[b : b + 1, :] = to_row(wide_peak[at, :])
        small[b : b + 1, :] = to_row(wide_lse[at, :])
    lse_ref[...] = jnp.broadcast_to(small[...][None], lse_ref.shape)


def common_order(b, n):
    _, _, core = place_on_cent()
    return lax.rem(b + core * (n // CORES), n)


def local_order(rows):
    _, _, core = place_on_cent()
    half = rows.shape[0] // CORES
    return jnp.where(core == 1, jnp.concatenate([rows[half:], rows[:half]], axis=0), rows)


def load_all(docs_hbm, cents_hbm, docs, cents):
    half = docs.shape[0] // 2
    pltpu.sync_copy(docs_hbm[0], docs.at[:half, :])
    pltpu.sync_copy(docs_hbm[1], docs.at[half:, :])
    pltpu.sync_copy(cents_hbm, cents)


def row_slow(docs_hbm, cents_hbm, col_wide, small):
    n_doc, n_cent = 2 * docs_hbm[0].shape[0], cents_hbm.shape[0]

    def body(docs, cents, x_ref, peak, total):
        load_all(docs_hbm, cents_hbm, docs, cents)
        peak[...] = jnp.full(peak.shape, -jnp.inf, f32)
        total[...] = jnp.zeros(total.shape, f32)

        def sweep(last):
            def block(t, _):
                start = pl.multiple_of(t * BLOCK, BLOCK)
                rows = pl.ds(start, BLOCK)
                logits_block(cents[rows, :], docs, x_ref, pl.ds(0, BLOCK))
                for at in range(0, n_doc, LANES):
                    y = x_ref[:, at : at + LANES] * SCALE + col_wide[rows, :]
                    here = peak[:, at : at + LANES]
                    if last:
                        total[:, at : at + LANES] += jnp.sum(jnp.exp(y - here), axis=0, keepdims=True)
                    else:
                        peak[:, at : at + LANES] = jnp.maximum(here, jnp.max(y, axis=0, keepdims=True))
                return 0

            lax.fori_loop(0, n_cent // BLOCK, block, 0)

        sweep(False)
        sweep(True)
        for b in range(n_doc // LANES):
            at = slice(b * LANES, (b + 1) * LANES)
            small[pl.ds(common_order(b, n_doc // LANES), 1), :] = peak[:, at] + jnp.log(total[:, at])

    pl.run_scoped(
        body,
        pltpu.VMEM((n_doc, cents_hbm.shape[1]), bf16),
        pltpu.VMEM(cents_hbm.shape, bf16),
        pltpu.VMEM((BLOCK, n_doc), f32),
        pltpu.VMEM((1, n_doc), f32),
        pltpu.VMEM((1, n_doc), f32),
    )


def row_kernel(log_ratio, t_ref, peak_ref, parts_ref, own_hbm, other_hbm, cents_hbm, lse_ref, col_ref, wide, acc, small):
    n_cent, n_doc = t_ref.shape
    col = log_ratio - merge(parts_ref[...])
    col_ref[...] = col
    factor = jnp.exp(peak_ref[...] + col)
    for b in range(n_cent // LANES):
        column = to_column(factor[b : b + 1, :])
        wide[b * LANES : (b + 1) * LANES, :] = jnp.broadcast_to(column, (LANES, LANES))
    acc[...] = jnp.zeros(acc.shape, f32)
    step = 64

    def block(t, _):
        start = pl.multiple_of(t * step, step)
        scale = wide[pl.ds(start, step), :]
        for at in range(0, n_doc, LANES):
            x = t_ref[pl.ds(start, step), at : at + LANES] * scale
            part = x[:8, :]
            for r in range(8, step, 8):
                part = part + x[r : r + 8, :]
            acc[:, at : at + LANES] += part
        return 0

    lax.fori_loop(0, n_cent // step, block, 0)
    least = jnp.full((1, LANES), jnp.inf, f32)
    for b in range(n_doc // LANES):
        total = jnp.sum(acc[:, b * LANES : (b + 1) * LANES], axis=0, keepdims=True)
        least = jnp.minimum(least, total)
        small[pl.ds(common_order(b, n_doc // LANES), 1), :] = jnp.log(total)

    @pl.when(jnp.logical_not(jnp.min(least) >= SMALL_SUM))
    def _():
        for b in range(n_cent // LANES):
            column = to_column(col[b : b + 1, :])
            wide[b * LANES : (b + 1) * LANES, :] = jnp.broadcast_to(column, (LANES, LANES))
        row_slow((own_hbm, other_hbm), cents_hbm, wide, small)

    lse_ref[...] = jnp.broadcast_to(small[...][None], lse_ref.shape)


def col_slow(docs_hbm, cents_hbm, row_pot, wide_lse):
    n_doc, n_cent = 2 * docs_hbm[0].shape[0], cents_hbm.shape[0]

    def body(docs, cents, x_ref):
        load_all(docs_hbm, cents_hbm, docs, cents)

        def block(t, _):
            start = pl.multiple_of(t * BLOCK, BLOCK)
            logits_block(cents[pl.ds(start, BLOCK), :], docs, x_ref, pl.ds(0, BLOCK))

            def chunk(c, _):
                at = pl.multiple_of(c * CHUNK, CHUNK)
                y = [
                    x_ref[pl.ds(at, CHUNK), b * LANES : (b + 1) * LANES] * SCALE + row_pot[b : b + 1, :]
                    for b in range(n_doc // LANES)
                ]
                peak = jnp.max(functools.reduce(jnp.maximum, y), axis=1, keepdims=True)
                total = jnp.sum(sum(jnp.exp(part - peak) for part in y), axis=1, keepdims=True)
                value = peak + jnp.log(total)
                wide_lse[pl.ds(start + at, CHUNK), :] = jnp.broadcast_to(value, (CHUNK, LANES))
                return 0

            return lax.fori_loop(0, BLOCK // CHUNK, chunk, 0)

        lax.fori_loop(0, n_cent // BLOCK, block, 0)

    pl.run_scoped(
        body,
        pltpu.VMEM((n_doc, cents_hbm.shape[1]), bf16),
        pltpu.VMEM(cents_hbm.shape, bf16),
        pltpu.VMEM((BLOCK, n_doc), f32),
    )


def col_kernel(t_ref, peak_ref, parts_ref, own_hbm, other_hbm, cents_hbm, lse_ref, wide_lse, small):
    n_cent, n_doc = t_ref.shape
    row_pot = local_order(-merge(parts_ref[...]))
    factor = jnp.exp(row_pot)
    step = 64

    def block(t, _):
        start = pl.multiple_of(t * step, step)
        total = jnp.zeros((step, LANES), f32)
        for b in range(n_doc // LANES):
            total = total + t_ref[pl.ds(start, step), b * LANES : (b + 1) * LANES] * factor[b : b + 1, :]
        wide_lse[pl.ds(start, step), :] = total
        return 0

    lax.fori_loop(0, n_cent // step, block, 0)
    good = jnp.max(row_pot) <= LARGE_POT
    for b in range(n_cent // LANES):
        at = slice(b * LANES, (b + 1) * LANES)
        total = jnp.sum(wide_lse[at, :], axis=1, keepdims=True)
        small[b : b + 1, :] = jnp.log(to_row(jnp.broadcast_to(total, (LANES, LANES)))) + peak_ref[b : b + 1, :]

    @pl.when(jnp.logical_not(good))
    def _():
        def body(pot):
            pot[...] = row_pot
            col_slow((own_hbm, other_hbm), cents_hbm, pot, wide_lse)

        pl.run_scoped(body, pltpu.VMEM(row_pot.shape, f32))
        for b in range(n_cent // LANES):
            small[b : b + 1, :] = to_row(wide_lse[b * LANES : (b + 1) * LANES, :])

    lse_ref[...] = jnp.broadcast_to(small[...][None], lse_ref.shape)


def prepare_kernel(peak_ref, col_ref, parts_ref, wide, pot_ref, row_ref):
    row_pot = local_order(-merge(parts_ref[...]))
    good = jnp.max(row_pot) <= LARGE_POT
    row_ref[...] = row_pot
    pot_ref[...] = jnp.where(good, jnp.exp(row_pot), row_pot)
    by_col = jnp.where(good, jnp.exp(peak_ref[...] + col_ref[...]), col_ref[...])
    for b in range(by_col.shape[0]):
        column = to_column(by_col[b : b + 1, :])
        wide[b * LANES : (b + 1) * LANES, :] = jnp.broadcast_to(column, (LANES, LANES))


def split(value):
    high = value.astype(bf16).astype(f32)
    middle = (value - high).astype(bf16).astype(f32)
    low = value - high - middle
    row = lax.broadcasted_iota(jnp.int32, (PAD, LANES), 0)
    rows = jnp.where(row == 0, high, jnp.where(row == 1, middle, jnp.where(row == 2, low, 0.0)))
    return rows.astype(bf16)


def joined(rows):
    rows = rows.astype(f32)
    return rows[0:1] + rows[1:2] + rows[2:3]


def product_kernel(shifts, *refs):
    t_ref, wide, pot_ref, row_ref, own_ref, other_ref, cents_hbm = refs[:7]
    outs, mass_ref, plan = refs[7:-2], refs[-2], refs[-1]
    groups, me = lax.axis_size("dp"), lax.axis_index("dp")
    n_own = own_ref.shape[0]
    n_doc = 2 * n_own
    half = own_ref.shape[1] // 2
    good = jnp.max(row_ref[...]) <= LARGE_POT
    starts = [pl.multiple_of(lax.rem(me + shift, groups) * BLOCK, BLOCK) for shift in shifts]

    def build(k):
        for r in range(0, BLOCK, LANES):
            rows = pl.ds(starts[k] + r, LANES)
            scale = wide[rows, :]
            for b in range(n_doc // LANES):
                at = slice(b * LANES, (b + 1) * LANES)
                plan[k, r : r + LANES, at] = (t_ref[rows, at] * scale * pot_ref[b : b + 1, :]).astype(bf16)

    def build_slow(k):
        def body(cents, x_ref):
            pltpu.sync_copy(cents_hbm.at[pl.ds(starts[k], BLOCK), :], cents)
            logits_block(cents[...], own_ref, x_ref, pl.ds(0, BLOCK))
            logits_block(cents[...], other_ref, x_ref, pl.ds(0, BLOCK), n_own)
            col = wide[pl.ds(starts[k], BLOCK), :]
            for b in range(n_doc // LANES):
                at = slice(b * LANES, (b + 1) * LANES)
                plan[k, :, at] = jnp.exp(x_ref[:, at] * SCALE + pot_ref[b : b + 1, :] + col).astype(bf16)

        pl.run_scoped(body, pltpu.VMEM((BLOCK, cents_hbm.shape[1]), bf16), pltpu.VMEM((BLOCK, n_doc), f32))

    def multiply(k):
        sums = jnp.dot(plan[k, :, :n_own], own_ref[...], preferred_element_type=f32)
        sums = sums + jnp.dot(plan[k, :, n_own:], other_ref[...], preferred_element_type=f32)
        masses = []
        for r in range(0, BLOCK, LANES):
            mass = fold(plan[k, r : r + LANES, :].astype(f32), jnp.add)
            masses.append(to_row(jnp.broadcast_to(jnp.sum(mass, axis=1, keepdims=True), (LANES, LANES))))
        if len(outs) == 2:
            for j, mass in enumerate(masses):
                mass_ref[2 * k + j : 2 * k + j + 1, :] = mass
            outs[0][k * BLOCK : (k + 1) * BLOCK, :] = sums[:, :half]
            outs[1][k * BLOCK : (k + 1) * BLOCK, :] = sums[:, half:]
        else:
            mass_ref[...] = jnp.concatenate(masses, axis=0)
            for j, mass in enumerate(masses):
                rows = slice(j * LANES, (j + 1) * LANES)
                send(outs[j], sums[rows, :half], [mass])
                outs[2 + j][...] = sums[rows, half:].astype(bf16)

    def all_of(build):
        build(0)
        for k in range(len(shifts)):
            if k + 1 < len(shifts):
                build(k + 1)
            multiply(k)

    @pl.when(good)
    def _():
        all_of(build)

    @pl.when(jnp.logical_not(good))
    def _():
        all_of(build_slow)


def send(out, sums, masses):
    n = sums.shape[0]
    out[:n, :] = sums.astype(bf16)
    out[n:, :] = jnp.zeros((PAD, sums.shape[1]), bf16)
    for j, mass in enumerate(masses):
        out[n:, j * LANES : (j + 1) * LANES] = split(mass)


def mass_of(came, j):
    return joined(came[came.shape[0] - PAD :, j * LANES : (j + 1) * LANES])


def add_kernel(part, sums_ref, mass_ref, right_ref, left_ref, right_out, left_out):
    for k, (came, out) in enumerate(((right_ref, right_out), (left_ref, left_out))):
        sums = sums_ref[k * BLOCK : (k + 1) * BLOCK, :]
        masses = [mass_ref[2 * k + j : 2 * k + j + 1, :] for j in range(2)]
        n = came.shape[0] - PAD
        if part:
            parts = [sums[:n, :], sums[n:, :]]
            parts[k] = parts[k] + came[:n, :].astype(f32)
            masses[k] = masses[k] + mass_of(came, 0)
            sums = jnp.concatenate(parts, axis=0)
        else:
            sums = sums + came[:n, :].astype(f32)
            masses = [mass + mass_of(came, j) for j, mass in enumerate(masses)]
        send(out, sums, masses)


def add_rest_kernel(part, sums_ref, right_ref, left_ref, right_out, left_out):
    for k, (came, out) in enumerate(((right_ref, right_out), (left_ref, left_out))):
        n = came.shape[0]
        first = k * BLOCK
        if part:
            for j in range(2):
                sums = sums_ref[first + j * n : first + (j + 1) * n, :]
                out[j * n : (j + 1) * n, :] = (sums + came[...].astype(f32) if j == k else sums).astype(bf16)
        else:
            out[...] = (sums_ref[first : first + BLOCK, :] + came[...].astype(f32)).astype(bf16)


def divide_kernel(sums_ref, mass_ref, right_ref, left_ref, out_ref, total_ref):
    for b in range(BLOCK // LANES):
        at = slice(b * LANES, (b + 1) * LANES)
        mass = mass_ref[b : b + 1, :] + (mass_of(right_ref, b) + mass_of(left_ref, b))
        total_ref[b : b + 1, :] = mass
        sums = sums_ref[at, :] + (right_ref[at, :].astype(f32) + left_ref[at, :].astype(f32))
        out_ref[at, :] = (sums / to_column(mass)).astype(bf16)


def divide_rest_kernel(sums_ref, mass_ref, right_ref, left_ref, out_ref):
    for b in range(BLOCK // LANES):
        at = slice(b * LANES, (b + 1) * LANES)
        sums = sums_ref[at, :] + (right_ref[at, :].astype(f32) + left_ref[at, :].astype(f32))
        out_ref[at, :] = (sums / to_column(mass_ref[b : b + 1, :])).astype(bf16)


def place_kernel(places, *refs):
    blocks, out, sems = refs[: len(places)], refs[-2], refs[-1]
    groups, me = lax.axis_size("dp"), lax.axis_index("dp")
    half = out.shape[1] // 2
    copies = []
    for at, (shift, row, column) in enumerate(places):
        start = pl.multiple_of(lax.rem(me + shift, groups) * BLOCK + row, LANES)
        to = out.at[pl.ds(start, blocks[at].shape[0]), pl.ds(column * half, half)]
        copy = pltpu.make_async_copy(blocks[at], to, sems.at[at])
        copy.start()
        copies.append(copy)
    for copy in copies:
        copy.wait()


IN_VMEM = pl.BlockSpec(memory_space=pltpu.VMEM)
IN_HBM = pl.BlockSpec(memory_space=pl.ANY)


def params(mib):
    return pltpu.CompilerParams(vmem_limit_bytes=mib * 2**20)


def shards(embeddings, centroids):
    groups, blocks = lax.axis_size("dp"), lax.axis_size("cent")
    own = gather(embeddings)
    other = on_cent(own, lambda y, x_at, core: (y, x_at, core + 1))
    n_doc, depth = CORES * own.shape[0], own.shape[1]
    n_cent = centroids.shape[0]
    log_ratio = math.log(n_doc * groups / (n_cent * blocks))
    row_shape = (n_doc // LANES, LANES)
    col_shape = (n_cent // LANES, LANES)
    shaped = jax.ShapeDtypeStruct
    by_group = shaped((groups, *col_shape), f32)
    by_block = shaped((blocks, *row_shape), f32)
    wide = pltpu.VMEM((n_cent, LANES), f32)

    raw = pl.pallas_call(
        own_kernel,
        out_shape=pltpu.VMEM((n_cent, own.shape[0]), f32),
        in_specs=[IN_VMEM] * 2,
        out_specs=IN_VMEM,
        compiler_params=params(10),
        cost_estimate=pl.CostEstimate(flops=2 * n_cent * own.shape[0] * depth, bytes_accessed=12 * 2**20, transcendentals=0),
    )(own, centroids)
    t, peak, lse = pl.pallas_call(
        first_kernel,
        out_shape=(pltpu.VMEM((n_cent, n_doc), f32), shaped(col_shape, f32), by_group),
        in_specs=[IN_VMEM] * 3,
        out_specs=(IN_VMEM,) * 3,
        scratch_shapes=[pltpu.VMEM((BLOCK, own.shape[0]), f32)] * 2 + [wide, wide, pltpu.VMEM(col_shape, f32)],
        compiler_params=params(16),
    )(raw, other, centroids)

    def rows(lse):
        parts = lax.all_to_all(lse, "dp", 0, 0)
        return pl.pallas_call(
            functools.partial(row_kernel, log_ratio),
            out_shape=(by_block, shaped(col_shape, f32)),
            in_specs=[IN_VMEM] * 3 + [IN_HBM] * 3,
            out_specs=(IN_VMEM, IN_VMEM),
            scratch_shapes=[wide, pltpu.VMEM((8, n_doc), f32), pltpu.VMEM(row_shape, f32)],
            compiler_params=params(20),
        )(t, peak, parts, own, other, centroids)

    def cols(lse):
        parts = lax.all_to_all(lse, "cent", 0, 0)
        return pl.pallas_call(
            col_kernel,
            out_shape=by_group,
            in_specs=[IN_VMEM] * 3 + [IN_HBM] * 3,
            out_specs=IN_VMEM,
            scratch_shapes=[wide, pltpu.VMEM(col_shape, f32)],
            compiler_params=params(20),
        )(t, peak, parts, own, other, centroids)

    lse, _ = rows(lse)
    lse = cols(lse)
    lse, col = rows(lse)
    parts = lax.all_to_all(lse, "cent", 0, 0)
    wide_col, pot, row = pl.pallas_call(
        prepare_kernel,
        out_shape=(pltpu.VMEM((n_cent, LANES), f32), shaped(row_shape, f32), shaped(row_shape, f32)),
        in_specs=[IN_VMEM] * 3,
        out_specs=(IN_VMEM,) * 3,
        compiler_params=params(4),
    )(peak, col, parts)

    far = groups // 2
    half = depth // 2
    free = pl.CostEstimate(flops=1, bytes_accessed=1, transcendentals=0)

    def message(rows):
        return shaped((rows, half), bf16)

    def move(x, by):
        return lax.ppermute(x, "dp", [(i, (i + by) % groups) for i in range(groups)])

    def products(shifts, outs, n_mass):
        return pl.pallas_call(
            functools.partial(product_kernel, shifts),
            out_shape=(*outs, shaped((n_mass, LANES), f32)),
            in_specs=[IN_VMEM] * 6 + [IN_HBM],
            out_specs=(IN_VMEM,) * (len(outs) + 1),
            scratch_shapes=[pltpu.VMEM((len(shifts), BLOCK, n_doc), bf16)],
            compiler_params=params(20),
            cost_estimate=free,
        )(t, wide_col, pot, row, own, other, centroids)

    def small_call(kernel, outs, *args):
        return pl.pallas_call(
            kernel,
            out_shape=outs,
            in_specs=[IN_VMEM] * len(args),
            out_specs=(IN_VMEM,) * len(outs) if isinstance(outs, tuple) else IN_VMEM,
            compiler_params=params(6),
            cost_estimate=free,
        )(*args)

    outs = (message(LANES + PAD),) * 2 + (message(LANES),) * 2
    right, left, rest_right, rest_left, _ = products([far], outs, 2)
    for s in range(1, far):
        right, left = move(right, 1), move(left, -1)
        rest_right, rest_left = move(rest_right, 1), move(rest_left, -1)
        outs = (shaped((2 * BLOCK, half), f32),) * 2
        sums, rest, mass = products([far - s, far + s], outs, 4)
        right, left = small_call(
            functools.partial(add_kernel, s == 1), (message(BLOCK + PAD),) * 2, sums, mass, right, left
        )
        rest_right, rest_left = small_call(
            functools.partial(add_rest_kernel, s == 1), (message(BLOCK),) * 2, rest, rest_right, rest_left
        )
    right, left = move(right, 1), move(left, -1)
    rest_right, rest_left = move(rest_right, 1), move(rest_left, -1)
    sums, rest, mass = products([0], (shaped((BLOCK, half), f32),) * 2, 2)
    new, total = small_call(
        divide_kernel, (message(BLOCK), shaped((2, LANES), f32)), sums, mass, right, left
    )
    rest_new = small_call(divide_rest_kernel, message(BLOCK), rest, total, rest_right, rest_left)

    near, last = [], []
    for column, block in enumerate((new, rest_new)):
        near.append((block, (0, 0, column)))
        held = {1: block, -1: block}
        for hop in range(1, far + 1):
            for by, rows in ((1, slice(0, LANES)), (-1, slice(LANES, BLOCK))):
                held[by] = move(held[by][rows] if hop == far else held[by], by)
                place = (-by * hop % groups, rows.start if hop == far else 0, column)
                (last if hop == far else near).append((held[by], place))

    def put(blocks, *into):
        arrays, places = zip(*blocks)
        return pl.pallas_call(
            functools.partial(place_kernel, places),
            out_shape=shaped((n_cent, depth), bf16),
            in_specs=[IN_HBM] * (len(arrays) + len(into)),
            out_specs=IN_HBM,
            scratch_shapes=[pltpu.SemaphoreType.DMA((len(arrays),))],
            input_output_aliases={len(arrays): 0} if into else {},
            compiler_params=params(4),
            cost_estimate=free,
        )(*arrays, *into)

    return put(last, put(near))


def solution(mesh):
    placed = (P(("dp", "cent"), None), P("cent", None))
    return jax.shard_map(
        shards, mesh=mesh, in_specs=placed, out_specs=P("cent", None), check_vma=False
    )
```

```python
import functools
import math

import jax
import jax.numpy as jnp
from jax import lax
from jax.experimental import pallas as pl
from jax.experimental.pallas import tpu as pltpu
from jax.sharding import PartitionSpec as P

f32 = jnp.float32
bf16 = jnp.bfloat16
LANES = 128
BLOCK = 256
CHUNK = 16
SCALE = 3.0
EXP2_SCALE = SCALE * math.log2(math.e)
RING_Y, RING_X, CORES = 4, 4, 2
SMALL_SUM = 1e-20
LARGE_POT = 46.0
PAD = 16
NT = (((1,), (1,)), ((), ()))


def eye():
    rows = lax.broadcasted_iota(jnp.int32, (LANES, LANES), 0)
    cols = lax.broadcasted_iota(jnp.int32, (LANES, LANES), 1)
    return rows == cols


def to_row(column):
    return jnp.sum(jnp.where(eye(), column, 0.0), axis=0, keepdims=True)


def to_column(row):
    return jnp.sum(jnp.where(eye(), row, 0.0), axis=1, keepdims=True)


def fold(x, op):
    out = x[:, :LANES]
    for at in range(LANES, x.shape[1], LANES):
        out = op(out, x[:, at : at + LANES])
    return out


def merge(parts):
    peak = jnp.max(parts, axis=0)
    return peak + jnp.log(jnp.sum(jnp.exp(parts - peak[None]), axis=0))


def logits_block(cents, docs_ref, out_ref, rows, offset=0):
    width = 512
    for at in range(0, docs_ref.shape[0], width):
        out_ref[rows, offset + at : offset + at + width] = lax.dot_general(
            cents, docs_ref[at : at + width, :], NT, preferred_element_type=f32
        )


def place_on_cent():
    at = lax.axis_index("cent")
    return at // (RING_X * CORES), at // CORES % RING_X, at % CORES


def on_cent(x, place):
    pairs = []
    for y in range(RING_Y):
        for x_at in range(RING_X):
            for core in range(CORES):
                to_y, to_x, to_core = place(y, x_at, core)
                to = (to_y % RING_Y * RING_X + to_x % RING_X) * CORES + to_core % CORES
                pairs.append(((y * RING_X + x_at) * CORES + core, to))
    return lax.ppermute(x, "cent", pairs)


def along(x, first, by):
    return on_cent(x, lambda y, x_at, core: (y, x_at + by, core) if (core == 0) == first else (y + by, x_at, core))


def stack_kernel(first, own, before, after, across, out):
    y, x, core = place_on_cent()
    at = jnp.where((core == 0) == first, x, y)
    size = own.shape[0]
    for shift, block in ((0, own), (RING_X - 1, before), (1, after), (2, across)):
        start = pl.multiple_of(lax.rem(at + shift, RING_X) * size, size)
        out[pl.ds(start, size), :] = block[...]


def copy_kernel(from_ref, to_ref):
    pltpu.sync_copy(from_ref, to_ref)


def gather(own):
    for first in (True, False):
        moved = [along(own, first, by) for by in (1, -1, 2)]
        if first:
            own = pl.pallas_call(
                copy_kernel,
                out_shape=pltpu.VMEM(own.shape, bf16),
                in_specs=[IN_HBM],
                out_specs=IN_VMEM,
                cost_estimate=pl.CostEstimate(flops=1, bytes_accessed=1, transcendentals=0),
                compiler_params=params(4),
            )(own)
        own = pl.pallas_call(
            functools.partial(stack_kernel, first),
            out_shape=jax.ShapeDtypeStruct((RING_X * own.shape[0], own.shape[1]), bf16),
            in_specs=[IN_VMEM] * 4,
            out_specs=IN_VMEM,
            compiler_params=params(8),
        )(own, *moved)
    return own


def own_kernel(docs_ref, cents_ref, raw_ref):
    tall, width = 1024, 256

    def block(t, _):
        rows = pl.ds(pl.multiple_of(t * tall, tall), tall)
        for at in range(0, docs_ref.shape[0], width):
            raw_ref[rows, at : at + width] = lax.dot_general(
                cents_ref[rows, :], docs_ref[at : at + width, :], NT, preferred_element_type=f32
            )
        return 0

    lax.fori_loop(0, cents_ref.shape[0] // tall, block, 0)


def first_kernel(raw_ref, docs_ref, cents_ref, t_ref, peak_ref, lse_ref, even, odd, wide_peak, wide_lse, small):
    n_cent, n_own = raw_ref.shape
    n_blocks = n_cent // BLOCK
    tiles = n_own // LANES
    k = EXP2_SCALE

    def multiply(t, x_ref):
        start = pl.multiple_of(jnp.minimum(t, n_blocks - 1) * BLOCK, BLOCK)
        logits_block(cents_ref[pl.ds(start, BLOCK), :], docs_ref, x_ref, pl.ds(0, BLOCK))

    def finish(t, x_ref):
        for r in range(0, BLOCK, LANES):
            rows = pl.ds(pl.multiple_of(t * BLOCK + r, LANES), LANES)
            parts = [lambda b=b: raw_ref[rows, b * LANES : (b + 1) * LANES] for b in range(tiles)]
            parts += [lambda b=b: x_ref[r : r + LANES, b * LANES : (b + 1) * LANES] for b in range(tiles)]
            peak = parts[0]()
            for part in parts[1:]:
                peak = jnp.maximum(peak, part())
            peak = jnp.broadcast_to(jnp.max(peak, axis=1, keepdims=True), (LANES, LANES))
            total = jnp.zeros((LANES, LANES), f32)
            for b, part in enumerate(parts):
                e = jnp.exp2((part() - peak) * k)
                t_ref[rows, b * LANES : (b + 1) * LANES] = e
                total = total + e
            total = jnp.broadcast_to(jnp.sum(total, axis=1, keepdims=True), (LANES, LANES))
            wide_peak[rows, :] = peak * SCALE
            wide_lse[rows, :] = peak * SCALE + jnp.log(total)

    multiply(0, even)

    def pair(i, _):
        multiply(2 * i + 1, odd)
        finish(2 * i, even)
        multiply(2 * i + 2, even)
        finish(2 * i + 1, odd)
        return 0

    lax.fori_loop(0, n_blocks // 2, pair, 0)
    for b in range(n_cent // LANES):
        at = slice(b * LANES, (b + 1) * LANES)
        peak_ref[b : b + 1, :] = to_row(wide_peak[at, :])
        small[b : b + 1, :] = to_row(wide_lse[at, :])
    lse_ref[...] = jnp.broadcast_to(small[...][None], lse_ref.shape)


def common_order(b, n):
    _, _, core = place_on_cent()
    return lax.rem(b + core * (n // CORES), n)


def local_order(rows):
    _, _, core = place_on_cent()
    half = rows.shape[0] // CORES
    return jnp.where(core == 1, jnp.concatenate([rows[half:], rows[:half]], axis=0), rows)


def load_all(docs_hbm, cents_hbm, docs, cents):
    half = docs.shape[0] // 2
    pltpu.sync_copy(docs_hbm[0], docs.at[:half, :])
    pltpu.sync_copy(docs_hbm[1], docs.at[half:, :])
    pltpu.sync_copy(cents_hbm, cents)


def row_slow(docs_hbm, cents_hbm, col_wide, small):
    n_doc, n_cent = 2 * docs_hbm[0].shape[0], cents_hbm.shape[0]

    def body(docs, cents, x_ref, peak, total):
        load_all(docs_hbm, cents_hbm, docs, cents)
        peak[...] = jnp.full(peak.shape, -jnp.inf, f32)
        total[...] = jnp.zeros(total.shape, f32)

        def sweep(last):
            def block(t, _):
                start = pl.multiple_of(t * BLOCK, BLOCK)
                rows = pl.ds(start, BLOCK)
                logits_block(cents[rows, :], docs, x_ref, pl.ds(0, BLOCK))
                for at in range(0, n_doc, LANES):
                    y = x_ref[:, at : at + LANES] * SCALE + col_wide[rows, :]
                    here = peak[:, at : at + LANES]
                    if last:
                        total[:, at : at + LANES] += jnp.sum(jnp.exp(y - here), axis=0, keepdims=True)
                    else:
                        peak[:, at : at + LANES] = jnp.maximum(here, jnp.max(y, axis=0, keepdims=True))
                return 0

            lax.fori_loop(0, n_cent // BLOCK, block, 0)

        sweep(False)
        sweep(True)
        for b in range(n_doc // LANES):
            at = slice(b * LANES, (b + 1) * LANES)
            small[pl.ds(common_order(b, n_doc // LANES), 1), :] = peak[:, at] + jnp.log(total[:, at])

    pl.run_scoped(
        body,
        pltpu.VMEM((n_doc, cents_hbm.shape[1]), bf16),
        pltpu.VMEM(cents_hbm.shape, bf16),
        pltpu.VMEM((BLOCK, n_doc), f32),
        pltpu.VMEM((1, n_doc), f32),
        pltpu.VMEM((1, n_doc), f32),
    )


def row_kernel(log_ratio, t_ref, peak_ref, parts_ref, own_hbm, other_hbm, cents_hbm, lse_ref, col_ref, wide, acc, small):
    n_cent, n_doc = t_ref.shape
    col = log_ratio - merge(parts_ref[...])
    col_ref[...] = col
    factor = jnp.exp(peak_ref[...] + col)
    for b in range(n_cent // LANES):
        column = to_column(factor[b : b + 1, :])
        wide[b * LANES : (b + 1) * LANES, :] = jnp.broadcast_to(column, (LANES, LANES))
    acc[...] = jnp.zeros(acc.shape, f32)
    step = 64

    def block(t, _):
        start = pl.multiple_of(t * step, step)
        scale = wide[pl.ds(start, step), :]
        for at in range(0, n_doc, LANES):
            x = t_ref[pl.ds(start, step), at : at + LANES] * scale
            part = x[:8, :]
            for r in range(8, step, 8):
                part = part + x[r : r + 8, :]
            acc[:, at : at + LANES] += part
        return 0

    lax.fori_loop(0, n_cent // step, block, 0)
    least = jnp.full((1, LANES), jnp.inf, f32)
    for b in range(n_doc // LANES):
        total = jnp.sum(acc[:, b * LANES : (b + 1) * LANES], axis=0, keepdims=True)
        least = jnp.minimum(least, total)
        small[pl.ds(common_order(b, n_doc // LANES), 1), :] = jnp.log(total)

    @pl.when(jnp.logical_not(jnp.min(least) >= SMALL_SUM))
    def _():
        for b in range(n_cent // LANES):
            column = to_column(col[b : b + 1, :])
            wide[b * LANES : (b + 1) * LANES, :] = jnp.broadcast_to(column, (LANES, LANES))
        row_slow((own_hbm, other_hbm), cents_hbm, wide, small)

    lse_ref[...] = jnp.broadcast_to(small[...][None], lse_ref.shape)


def col_slow(docs_hbm, cents_hbm, row_pot, wide_lse):
    n_doc, n_cent = 2 * docs_hbm[0].shape[0], cents_hbm.shape[0]

    def body(docs, cents, x_ref):
        load_all(docs_hbm, cents_hbm, docs, cents)

        def block(t, _):
            start = pl.multiple_of(t * BLOCK, BLOCK)
            logits_block(cents[pl.ds(start, BLOCK), :], docs, x_ref, pl.ds(0, BLOCK))

            def chunk(c, _):
                at = pl.multiple_of(c * CHUNK, CHUNK)
                y = [
                    x_ref[pl.ds(at, CHUNK), b * LANES : (b + 1) * LANES] * SCALE + row_pot[b : b + 1, :]
                    for b in range(n_doc // LANES)
                ]
                peak = jnp.max(functools.reduce(jnp.maximum, y), axis=1, keepdims=True)
                total = jnp.sum(sum(jnp.exp(part - peak) for part in y), axis=1, keepdims=True)
                value = peak + jnp.log(total)
                wide_lse[pl.ds(start + at, CHUNK), :] = jnp.broadcast_to(value, (CHUNK, LANES))
                return 0

            return lax.fori_loop(0, BLOCK // CHUNK, chunk, 0)

        lax.fori_loop(0, n_cent // BLOCK, block, 0)

    pl.run_scoped(
        body,
        pltpu.VMEM((n_doc, cents_hbm.shape[1]), bf16),
        pltpu.VMEM(cents_hbm.shape, bf16),
        pltpu.VMEM((BLOCK, n_doc), f32),
    )


def col_kernel(t_ref, peak_ref, parts_ref, own_hbm, other_hbm, cents_hbm, lse_ref, wide_lse, small):
    n_cent, n_doc = t_ref.shape
    row_pot = local_order(-merge(parts_ref[...]))
    factor = jnp.exp(row_pot)
    step = 64

    def block(t, _):
        start = pl.multiple_of(t * step, step)
        total = jnp.zeros((step, LANES), f32)
        for b in range(n_doc // LANES):
            total = total + t_ref[pl.ds(start, step), b * LANES : (b + 1) * LANES] * factor[b : b + 1, :]
        wide_lse[pl.ds(start, step), :] = total
        return 0

    lax.fori_loop(0, n_cent // step, block, 0)
    good = jnp.max(row_pot) <= LARGE_POT
    for b in range(n_cent // LANES):
        at = slice(b * LANES, (b + 1) * LANES)
        total = jnp.sum(wide_lse[at, :], axis=1, keepdims=True)
        small[b : b + 1, :] = jnp.log(to_row(jnp.broadcast_to(total, (LANES, LANES)))) + peak_ref[b : b + 1, :]

    @pl.when(jnp.logical_not(good))
    def _():
        def body(pot):
            pot[...] = row_pot
            col_slow((own_hbm, other_hbm), cents_hbm, pot, wide_lse)

        pl.run_scoped(body, pltpu.VMEM(row_pot.shape, f32))
        for b in range(n_cent // LANES):
            small[b : b + 1, :] = to_row(wide_lse[b * LANES : (b + 1) * LANES, :])

    lse_ref[...] = jnp.broadcast_to(small[...][None], lse_ref.shape)


def prepare_kernel(peak_ref, col_ref, parts_ref, wide, pot_ref, row_ref):
    row_pot = local_order(-merge(parts_ref[...]))
    good = jnp.max(row_pot) <= LARGE_POT
    row_ref[...] = row_pot
    pot_ref[...] = jnp.where(good, jnp.exp(row_pot), row_pot)
    by_col = jnp.where(good, jnp.exp(peak_ref[...] + col_ref[...]), col_ref[...])
    for b in range(by_col.shape[0]):
        column = to_column(by_col[b : b + 1, :])
        wide[b * LANES : (b + 1) * LANES, :] = jnp.broadcast_to(column, (LANES, LANES))


def split(value):
    high = value.astype(bf16).astype(f32)
    middle = (value - high).astype(bf16).astype(f32)
    low = value - high - middle
    row = lax.broadcasted_iota(jnp.int32, (PAD, LANES), 0)
    rows = jnp.where(row == 0, high, jnp.where(row == 1, middle, jnp.where(row == 2, low, 0.0)))
    return rows.astype(bf16)


def joined(rows):
    rows = rows.astype(f32)
    return rows[0:1] + rows[1:2] + rows[2:3]


def product_kernel(shifts, *refs):
    t_ref, wide, pot_ref, row_ref, own_ref, other_ref, cents_hbm = refs[:7]
    outs, mass_ref, plan = refs[7:-2], refs[-2], refs[-1]
    groups, me = lax.axis_size("dp"), lax.axis_index("dp")
    n_own = own_ref.shape[0]
    n_doc = 2 * n_own
    half = own_ref.shape[1] // 2
    good = jnp.max(row_ref[...]) <= LARGE_POT
    starts = [pl.multiple_of(lax.rem(me + shift, groups) * BLOCK, BLOCK) for shift in shifts]

    def build(k):
        for r in range(0, BLOCK, LANES):
            rows = pl.ds(starts[k] + r, LANES)
            scale = wide[rows, :]
            for b in range(n_doc // LANES):
                at = slice(b * LANES, (b + 1) * LANES)
                plan[k, r : r + LANES, at] = (t_ref[rows, at] * scale * pot_ref[b : b + 1, :]).astype(bf16)

    def build_slow(k):
        def body(cents, x_ref):
            pltpu.sync_copy(cents_hbm.at[pl.ds(starts[k], BLOCK), :], cents)
            logits_block(cents[...], own_ref, x_ref, pl.ds(0, BLOCK))
            logits_block(cents[...], other_ref, x_ref, pl.ds(0, BLOCK), n_own)
            col = wide[pl.ds(starts[k], BLOCK), :]
            for b in range(n_doc // LANES):
                at = slice(b * LANES, (b + 1) * LANES)
                plan[k, :, at] = jnp.exp(x_ref[:, at] * SCALE + pot_ref[b : b + 1, :] + col).astype(bf16)

        pl.run_scoped(body, pltpu.VMEM((BLOCK, cents_hbm.shape[1]), bf16), pltpu.VMEM((BLOCK, n_doc), f32))

    def multiply(k):
        sums = jnp.dot(plan[k, :, :n_own], own_ref[...], preferred_element_type=f32)
        sums = sums + jnp.dot(plan[k, :, n_own:], other_ref[...], preferred_element_type=f32)
        masses = []
        for r in range(0, BLOCK, LANES):
            mass = fold(plan[k, r : r + LANES, :].astype(f32), jnp.add)
            masses.append(to_row(jnp.broadcast_to(jnp.sum(mass, axis=1, keepdims=True), (LANES, LANES))))
        if len(outs) == 2:
            for j, mass in enumerate(masses):
                mass_ref[2 * k + j : 2 * k + j + 1, :] = mass
            outs[0][k * BLOCK : (k + 1) * BLOCK, :] = sums[:, :half]
            outs[1][k * BLOCK : (k + 1) * BLOCK, :] = sums[:, half:]
        else:
            mass_ref[...] = jnp.concatenate(masses, axis=0)
            for j, mass in enumerate(masses):
                rows = slice(j * LANES, (j + 1) * LANES)
                send(outs[j], sums[rows, :half], [mass])
                outs[2 + j][...] = sums[rows, half:].astype(bf16)

    def all_of(build):
        build(0)
        for k in range(len(shifts)):
            if k + 1 < len(shifts):
                build(k + 1)
            multiply(k)

    @pl.when(good)
    def _():
        all_of(build)

    @pl.when(jnp.logical_not(good))
    def _():
        all_of(build_slow)


def send(out, sums, masses):
    n = sums.shape[0]
    out[:n, :] = sums.astype(bf16)
    out[n:, :] = jnp.zeros((PAD, sums.shape[1]), bf16)
    for j, mass in enumerate(masses):
        out[n:, j * LANES : (j + 1) * LANES] = split(mass)


def mass_of(came, j):
    return joined(came[came.shape[0] - PAD :, j * LANES : (j + 1) * LANES])


def add_kernel(part, sums_ref, mass_ref, right_ref, left_ref, right_out, left_out):
    for k, (came, out) in enumerate(((right_ref, right_out), (left_ref, left_out))):
        sums = sums_ref[k * BLOCK : (k + 1) * BLOCK, :]
        masses = [mass_ref[2 * k + j : 2 * k + j + 1, :] for j in range(2)]
        n = came.shape[0] - PAD
        if part:
            parts = [sums[:n, :], sums[n:, :]]
            parts[k] = parts[k] + came[:n, :].astype(f32)
            masses[k] = masses[k] + mass_of(came, 0)
            sums = jnp.concatenate(parts, axis=0)
        else:
            sums = sums + came[:n, :].astype(f32)
            masses = [mass + mass_of(came, j) for j, mass in enumerate(masses)]
        send(out, sums, masses)


def add_rest_kernel(part, sums_ref, right_ref, left_ref, right_out, left_out):
    for k, (came, out) in enumerate(((right_ref, right_out), (left_ref, left_out))):
        n = came.shape[0]
        first = k * BLOCK
        if part:
            for j in range(2):
                sums = sums_ref[first + j * n : first + (j + 1) * n, :]
                out[j * n : (j + 1) * n, :] = (sums + came[...].astype(f32) if j == k else sums).astype(bf16)
        else:
            out[...] = (sums_ref[first : first + BLOCK, :] + came[...].astype(f32)).astype(bf16)


def divide_kernel(sums_ref, mass_ref, right_ref, left_ref, out_ref, total_ref):
    for b in range(BLOCK // LANES):
        at = slice(b * LANES, (b + 1) * LANES)
        mass = mass_ref[b : b + 1, :] + (mass_of(right_ref, b) + mass_of(left_ref, b))
        total_ref[b : b + 1, :] = mass
        sums = sums_ref[at, :] + (right_ref[at, :].astype(f32) + left_ref[at, :].astype(f32))
        out_ref[at, :] = (sums / to_column(mass)).astype(bf16)


def divide_rest_kernel(sums_ref, mass_ref, right_ref, left_ref, out_ref):
    for b in range(BLOCK // LANES):
        at = slice(b * LANES, (b + 1) * LANES)
        sums = sums_ref[at, :] + (right_ref[at, :].astype(f32) + left_ref[at, :].astype(f32))
        out_ref[at, :] = (sums / to_column(mass_ref[b : b + 1, :])).astype(bf16)


def place_kernel(places, *refs):
    blocks, out, sems = refs[: len(places)], refs[-2], refs[-1]
    groups, me = lax.axis_size("dp"), lax.axis_index("dp")
    half = out.shape[1] // 2
    copies = []
    for at, (shift, row, column) in enumerate(places):
        start = pl.multiple_of(lax.rem(me + shift, groups) * BLOCK + row, LANES)
        to = out.at[pl.ds(start, blocks[at].shape[0]), pl.ds(column * half, half)]
        copy = pltpu.make_async_copy(blocks[at], to, sems.at[at])
        copy.start()
        copies.append(copy)
    for copy in copies:
        copy.wait()


IN_VMEM = pl.BlockSpec(memory_space=pltpu.VMEM)
IN_HBM = pl.BlockSpec(memory_space=pl.ANY)


def params(mib):
    return pltpu.CompilerParams(vmem_limit_bytes=mib * 2**20)


def shards(embeddings, centroids):
    groups, blocks = lax.axis_size("dp"), lax.axis_size("cent")
    own = gather(embeddings)
    other = on_cent(own, lambda y, x_at, core: (y, x_at, core + 1))
    n_doc, depth = CORES * own.shape[0], own.shape[1]
    n_cent = centroids.shape[0]
    log_ratio = math.log(n_doc * groups / (n_cent * blocks))
    row_shape = (n_doc // LANES, LANES)
    col_shape = (n_cent // LANES, LANES)
    shaped = jax.ShapeDtypeStruct
    by_group = shaped((groups, *col_shape), f32)
    by_block = shaped((blocks, *row_shape), f32)
    wide = pltpu.VMEM((n_cent, LANES), f32)

    raw = pl.pallas_call(
        own_kernel,
        out_shape=pltpu.VMEM((n_cent, own.shape[0]), f32),
        in_specs=[IN_VMEM] * 2,
        out_specs=IN_VMEM,
        compiler_params=params(10),
        cost_estimate=pl.CostEstimate(flops=2 * n_cent * own.shape[0] * depth, bytes_accessed=12 * 2**20, transcendentals=0),
    )(own, centroids)
    t, peak, lse = pl.pallas_call(
        first_kernel,
        out_shape=(pltpu.VMEM((n_cent, n_doc), f32), shaped(col_shape, f32), by_group),
        in_specs=[IN_VMEM] * 3,
        out_specs=(IN_VMEM,) * 3,
        scratch_shapes=[pltpu.VMEM((BLOCK, own.shape[0]), f32)] * 2 + [wide, wide, pltpu.VMEM(col_shape, f32)],
        compiler_params=params(16),
    )(raw, other, centroids)

    def rows(lse):
        parts = lax.all_to_all(lse, "dp", 0, 0)
        return pl.pallas_call(
            functools.partial(row_kernel, log_ratio),
            out_shape=(by_block, shaped(col_shape, f32)),
            in_specs=[IN_VMEM] * 3 + [IN_HBM] * 3,
            out_specs=(IN_VMEM, IN_VMEM),
            scratch_shapes=[wide, pltpu.VMEM((8, n_doc), f32), pltpu.VMEM(row_shape, f32)],
            compiler_params=params(20),
        )(t, peak, parts, own, other, centroids)

    def cols(lse):
        parts = lax.all_to_all(lse, "cent", 0, 0)
        return pl.pallas_call(
            col_kernel,
            out_shape=by_group,
            in_specs=[IN_VMEM] * 3 + [IN_HBM] * 3,
            out_specs=IN_VMEM,
            scratch_shapes=[wide, pltpu.VMEM(col_shape, f32)],
            compiler_params=params(20),
        )(t, peak, parts, own, other, centroids)

    lse, _ = rows(lse)
    lse = cols(lse)
    lse, col = rows(lse)
    parts = lax.all_to_all(lse, "cent", 0, 0)
    wide_col, pot, row = pl.pallas_call(
        prepare_kernel,
        out_shape=(pltpu.VMEM((n_cent, LANES), f32), shaped(row_shape, f32), shaped(row_shape, f32)),
        in_specs=[IN_VMEM] * 3,
        out_specs=(IN_VMEM,) * 3,
        compiler_params=params(4),
    )(peak, col, parts)

    far = groups // 2
    half = depth // 2
    free = pl.CostEstimate(flops=1, bytes_accessed=1, transcendentals=0)

    def message(rows):
        return shaped((rows, half), bf16)

    def move(x, by):
        return lax.ppermute(x, "dp", [(i, (i + by) % groups) for i in range(groups)])

    def products(shifts, outs, n_mass):
        return pl.pallas_call(
            functools.partial(product_kernel, shifts),
            out_shape=(*outs, shaped((n_mass, LANES), f32)),
            in_specs=[IN_VMEM] * 6 + [IN_HBM],
            out_specs=(IN_VMEM,) * (len(outs) + 1),
            scratch_shapes=[pltpu.VMEM((len(shifts), BLOCK, n_doc), bf16)],
            compiler_params=params(20),
            cost_estimate=free,
        )(t, wide_col, pot, row, own, other, centroids)

    def small_call(kernel, outs, *args):
        return pl.pallas_call(
            kernel,
            out_shape=outs,
            in_specs=[IN_VMEM] * len(args),
            out_specs=(IN_VMEM,) * len(outs) if isinstance(outs, tuple) else IN_VMEM,
            compiler_params=params(6),
            cost_estimate=free,
        )(*args)

    outs = (message(LANES + PAD),) * 2 + (message(LANES),) * 2
    right, left, rest_right, rest_left, _ = products([far], outs, 2)
    for s in range(1, far):
        right, left = move(right, 1), move(left, -1)
        rest_right, rest_left = move(rest_right, 1), move(rest_left, -1)
        outs = (shaped((2 * BLOCK, half), f32),) * 2
        sums, rest, mass = products([far - s, far + s], outs, 4)
        right, left = small_call(
            functools.partial(add_kernel, s == 1), (message(BLOCK + PAD),) * 2, sums, mass, right, left
        )
        rest_right, rest_left = small_call(
            functools.partial(add_rest_kernel, s == 1), (message(BLOCK),) * 2, rest, rest_right, rest_left
        )
    right, left = move(right, 1), move(left, -1)
    rest_right, rest_left = move(rest_right, 1), move(rest_left, -1)
    sums, rest, mass = products([0], (shaped((BLOCK, half), f32),) * 2, 2)
    new, total = small_call(
        divide_kernel, (message(BLOCK), shaped((2, LANES), f32)), sums, mass, right, left
    )
    rest_new = small_call(divide_rest_kernel, message(BLOCK), rest, total, rest_right, rest_left)

    near, last = [], ([], [])
    for column, block in enumerate((new, rest_new)):
        near.append((block, (0, 0, column)))
        held = {1: block, -1: block}
        for hop in range(1, far + 1):
            for by, rows in ((1, slice(0, LANES)), (-1, slice(LANES, BLOCK))):
                held[by] = move(held[by][rows] if hop == far else held[by], by)
                place = (-by * hop % groups, rows.start if hop == far else 0, column)
                (last[column] if hop == far else near).append((held[by], place))

    def put(blocks, *into):
        arrays, places = zip(*blocks)
        return pl.pallas_call(
            functools.partial(place_kernel, places),
            out_shape=shaped((n_cent, depth), bf16),
            in_specs=[IN_HBM] * (len(arrays) + len(into)),
            out_specs=IN_HBM,
            scratch_shapes=[pltpu.SemaphoreType.DMA((len(arrays),))],
            input_output_aliases={len(arrays): 0} if into else {},
            compiler_params=params(4),
            cost_estimate=free,
        )(*arrays, *into)

    return put(last[1], put(last[0], put(near)))


def solution(mesh):
    placed = (P(("dp", "cent"), None), P("cent", None))
    return jax.shard_map(
        shards, mesh=mesh, in_specs=placed, out_specs=P("cent", None), check_vma=False
    )
```

```python
import functools
import math

import jax
import jax.numpy as jnp
from jax import lax
from jax.experimental import pallas as pl
from jax.experimental.pallas import tpu as pltpu
from jax.sharding import PartitionSpec as P

f32 = jnp.float32
bf16 = jnp.bfloat16
LANES = 128
BLOCK = 256
CHUNK = 16
SCALE = 3.0
EXP2_SCALE = SCALE * math.log2(math.e)
RING_Y, RING_X, CORES = 4, 4, 2
SMALL_SUM = 1e-20
LARGE_POT = 46.0
PAD = 16
NT = (((1,), (1,)), ((), ()))


def eye():
    rows = lax.broadcasted_iota(jnp.int32, (LANES, LANES), 0)
    cols = lax.broadcasted_iota(jnp.int32, (LANES, LANES), 1)
    return rows == cols


def to_row(column):
    return jnp.sum(jnp.where(eye(), column, 0.0), axis=0, keepdims=True)


def to_column(row):
    return jnp.sum(jnp.where(eye(), row, 0.0), axis=1, keepdims=True)


def fold(x, op):
    out = x[:, :LANES]
    for at in range(LANES, x.shape[1], LANES):
        out = op(out, x[:, at : at + LANES])
    return out


def merge(parts):
    peak = jnp.max(parts, axis=0)
    return peak + jnp.log(jnp.sum(jnp.exp(parts - peak[None]), axis=0))


def logits_block(cents, docs_ref, out_ref, rows, offset=0):
    width = 512
    for at in range(0, docs_ref.shape[0], width):
        out_ref[rows, offset + at : offset + at + width] = lax.dot_general(
            cents, docs_ref[at : at + width, :], NT, preferred_element_type=f32
        )


def place_on_cent():
    at = lax.axis_index("cent")
    return at // (RING_X * CORES), at // CORES % RING_X, at % CORES


def on_cent(x, place):
    pairs = []
    for y in range(RING_Y):
        for x_at in range(RING_X):
            for core in range(CORES):
                to_y, to_x, to_core = place(y, x_at, core)
                to = (to_y % RING_Y * RING_X + to_x % RING_X) * CORES + to_core % CORES
                pairs.append(((y * RING_X + x_at) * CORES + core, to))
    return lax.ppermute(x, "cent", pairs)


def along(x, first, by):
    return on_cent(x, lambda y, x_at, core: (y, x_at + by, core) if (core == 0) == first else (y + by, x_at, core))


def stack_kernel(first, own, before, after, across, out):
    y, x, core = place_on_cent()
    at = jnp.where((core == 0) == first, x, y)
    size = own.shape[0]
    for shift, block in ((0, own), (RING_X - 1, before), (1, after), (2, across)):
        start = pl.multiple_of(lax.rem(at + shift, RING_X) * size, size)
        out[pl.ds(start, size), :] = block[...]


def copy_kernel(from_ref, to_ref):
    pltpu.sync_copy(from_ref, to_ref)


def gather(own):
    for first in (True, False):
        moved = [along(own, first, by) for by in (1, -1, 2)]
        if first:
            own = pl.pallas_call(
                copy_kernel,
                out_shape=pltpu.VMEM(own.shape, bf16),
                in_specs=[IN_HBM],
                out_specs=IN_VMEM,
                cost_estimate=pl.CostEstimate(flops=1, bytes_accessed=1, transcendentals=0),
                compiler_params=params(4),
            )(own)
        own = pl.pallas_call(
            functools.partial(stack_kernel, first),
            out_shape=jax.ShapeDtypeStruct((RING_X * own.shape[0], own.shape[1]), bf16),
            in_specs=[IN_VMEM] * 4,
            out_specs=IN_VMEM,
            compiler_params=params(8),
        )(own, *moved)
    return own


def own_kernel(docs_ref, cents_ref, raw_ref):
    tall, width = 1024, 256

    def block(t, _):
        rows = pl.ds(pl.multiple_of(t * tall, tall), tall)
        for at in range(0, docs_ref.shape[0], width):
            raw_ref[rows, at : at + width] = lax.dot_general(
                cents_ref[rows, :], docs_ref[at : at + width, :], NT, preferred_element_type=f32
            )
        return 0

    lax.fori_loop(0, cents_ref.shape[0] // tall, block, 0)


def first_kernel(raw_ref, docs_ref, cents_ref, t_ref, peak_ref, lse_ref, even, odd, wide_peak, wide_lse, small):
    n_cent, n_own = raw_ref.shape
    n_blocks = n_cent // BLOCK
    tiles = n_own // LANES
    k = EXP2_SCALE

    def multiply(t, x_ref):
        start = pl.multiple_of(jnp.minimum(t, n_blocks - 1) * BLOCK, BLOCK)
        logits_block(cents_ref[pl.ds(start, BLOCK), :], docs_ref, x_ref, pl.ds(0, BLOCK))

    def finish(t, x_ref):
        for r in range(0, BLOCK, LANES):
            rows = pl.ds(pl.multiple_of(t * BLOCK + r, LANES), LANES)
            parts = [lambda b=b: raw_ref[rows, b * LANES : (b + 1) * LANES] for b in range(tiles)]
            parts += [lambda b=b: x_ref[r : r + LANES, b * LANES : (b + 1) * LANES] for b in range(tiles)]
            peak = parts[0]()
            for part in parts[1:]:
                peak = jnp.maximum(peak, part())
            peak = jnp.broadcast_to(jnp.max(peak, axis=1, keepdims=True), (LANES, LANES))
            total = jnp.zeros((LANES, LANES), f32)
            for b, part in enumerate(parts):
                e = jnp.exp2((part() - peak) * k)
                t_ref[rows, b * LANES : (b + 1) * LANES] = e
                total = total + e
            total = jnp.broadcast_to(jnp.sum(total, axis=1, keepdims=True), (LANES, LANES))
            wide_peak[rows, :] = peak * SCALE
            wide_lse[rows, :] = peak * SCALE + jnp.log(total)

    multiply(0, even)

    def pair(i, _):
        multiply(2 * i + 1, odd)
        finish(2 * i, even)
        multiply(2 * i + 2, even)
        finish(2 * i + 1, odd)
        return 0

    lax.fori_loop(0, n_blocks // 2, pair, 0)
    for b in range(n_cent // LANES):
        at = slice(b * LANES, (b + 1) * LANES)
        peak_ref[b : b + 1, :] = to_row(wide_peak[at, :])
        small[b : b + 1, :] = to_row(wide_lse[at, :])
    lse_ref[...] = jnp.broadcast_to(small[...][None], lse_ref.shape)


def common_order(b, n):
    _, _, core = place_on_cent()
    return lax.rem(b + core * (n // CORES), n)


def local_order(rows):
    _, _, core = place_on_cent()
    half = rows.shape[0] // CORES
    return jnp.where(core == 1, jnp.concatenate([rows[half:], rows[:half]], axis=0), rows)


def load_all(docs_hbm, cents_hbm, docs, cents):
    half = docs.shape[0] // 2
    pltpu.sync_copy(docs_hbm[0], docs.at[:half, :])
    pltpu.sync_copy(docs_hbm[1], docs.at[half:, :])
    pltpu.sync_copy(cents_hbm, cents)


def row_slow(docs_hbm, cents_hbm, col_wide, small):
    n_doc, n_cent = 2 * docs_hbm[0].shape[0], cents_hbm.shape[0]

    def body(docs, cents, x_ref, peak, total):
        load_all(docs_hbm, cents_hbm, docs, cents)
        peak[...] = jnp.full(peak.shape, -jnp.inf, f32)
        total[...] = jnp.zeros(total.shape, f32)

        def sweep(last):
            def block(t, _):
                start = pl.multiple_of(t * BLOCK, BLOCK)
                rows = pl.ds(start, BLOCK)
                logits_block(cents[rows, :], docs, x_ref, pl.ds(0, BLOCK))
                for at in range(0, n_doc, LANES):
                    y = x_ref[:, at : at + LANES] * SCALE + col_wide[rows, :]
                    here = peak[:, at : at + LANES]
                    if last:
                        total[:, at : at + LANES] += jnp.sum(jnp.exp(y - here), axis=0, keepdims=True)
                    else:
                        peak[:, at : at + LANES] = jnp.maximum(here, jnp.max(y, axis=0, keepdims=True))
                return 0

            lax.fori_loop(0, n_cent // BLOCK, block, 0)

        sweep(False)
        sweep(True)
        for b in range(n_doc // LANES):
            at = slice(b * LANES, (b + 1) * LANES)
            small[pl.ds(common_order(b, n_doc // LANES), 1), :] = peak[:, at] + jnp.log(total[:, at])

    pl.run_scoped(
        body,
        pltpu.VMEM((n_doc, cents_hbm.shape[1]), bf16),
        pltpu.VMEM(cents_hbm.shape, bf16),
        pltpu.VMEM((BLOCK, n_doc), f32),
        pltpu.VMEM((1, n_doc), f32),
        pltpu.VMEM((1, n_doc), f32),
    )


def row_kernel(log_ratio, t_ref, peak_ref, parts_ref, own_hbm, other_hbm, cents_hbm, lse_ref, col_ref, wide, acc, small):
    n_cent, n_doc = t_ref.shape
    col = log_ratio - merge(parts_ref[...])
    col_ref[...] = col
    factor = jnp.exp(peak_ref[...] + col)
    for b in range(n_cent // LANES):
        column = to_column(factor[b : b + 1, :])
        wide[b * LANES : (b + 1) * LANES, :] = jnp.broadcast_to(column, (LANES, LANES))
    acc[...] = jnp.zeros(acc.shape, f32)
    step = 64

    def block(t, _):
        start = pl.multiple_of(t * step, step)
        scale = wide[pl.ds(start, step), :]
        for at in range(0, n_doc, LANES):
            x = t_ref[pl.ds(start, step), at : at + LANES] * scale
            part = x[:8, :]
            for r in range(8, step, 8):
                part = part + x[r : r + 8, :]
            acc[:, at : at + LANES] += part
        return 0

    lax.fori_loop(0, n_cent // step, block, 0)
    least = jnp.full((1, LANES), jnp.inf, f32)
    for b in range(n_doc // LANES):
        total = jnp.sum(acc[:, b * LANES : (b + 1) * LANES], axis=0, keepdims=True)
        least = jnp.minimum(least, total)
        small[pl.ds(common_order(b, n_doc // LANES), 1), :] = jnp.log(total)

    @pl.when(jnp.logical_not(jnp.min(least) >= SMALL_SUM))
    def _():
        for b in range(n_cent // LANES):
            column = to_column(col[b : b + 1, :])
            wide[b * LANES : (b + 1) * LANES, :] = jnp.broadcast_to(column, (LANES, LANES))
        row_slow((own_hbm, other_hbm), cents_hbm, wide, small)

    lse_ref[...] = jnp.broadcast_to(small[...][None], lse_ref.shape)


def col_slow(docs_hbm, cents_hbm, row_pot, wide_lse):
    n_doc, n_cent = 2 * docs_hbm[0].shape[0], cents_hbm.shape[0]

    def body(docs, cents, x_ref):
        load_all(docs_hbm, cents_hbm, docs, cents)

        def block(t, _):
            start = pl.multiple_of(t * BLOCK, BLOCK)
            logits_block(cents[pl.ds(start, BLOCK), :], docs, x_ref, pl.ds(0, BLOCK))

            def chunk(c, _):
                at = pl.multiple_of(c * CHUNK, CHUNK)
                y = [
                    x_ref[pl.ds(at, CHUNK), b * LANES : (b + 1) * LANES] * SCALE + row_pot[b : b + 1, :]
                    for b in range(n_doc // LANES)
                ]
                peak = jnp.max(functools.reduce(jnp.maximum, y), axis=1, keepdims=True)
                total = jnp.sum(sum(jnp.exp(part - peak) for part in y), axis=1, keepdims=True)
                value = peak + jnp.log(total)
                wide_lse[pl.ds(start + at, CHUNK), :] = jnp.broadcast_to(value, (CHUNK, LANES))
                return 0

            return lax.fori_loop(0, BLOCK // CHUNK, chunk, 0)

        lax.fori_loop(0, n_cent // BLOCK, block, 0)

    pl.run_scoped(
        body,
        pltpu.VMEM((n_doc, cents_hbm.shape[1]), bf16),
        pltpu.VMEM(cents_hbm.shape, bf16),
        pltpu.VMEM((BLOCK, n_doc), f32),
    )


def col_kernel(t_ref, peak_ref, parts_ref, own_hbm, other_hbm, cents_hbm, lse_ref, wide_lse, small):
    n_cent, n_doc = t_ref.shape
    row_pot = local_order(-merge(parts_ref[...]))
    factor = jnp.exp(row_pot)
    step = 64

    def block(t, _):
        start = pl.multiple_of(t * step, step)
        total = jnp.zeros((step, LANES), f32)
        for b in range(n_doc // LANES):
            total = total + t_ref[pl.ds(start, step), b * LANES : (b + 1) * LANES] * factor[b : b + 1, :]
        wide_lse[pl.ds(start, step), :] = total
        return 0

    lax.fori_loop(0, n_cent // step, block, 0)
    good = jnp.max(row_pot) <= LARGE_POT
    for b in range(n_cent // LANES):
        at = slice(b * LANES, (b + 1) * LANES)
        total = jnp.sum(wide_lse[at, :], axis=1, keepdims=True)
        small[b : b + 1, :] = jnp.log(to_row(jnp.broadcast_to(total, (LANES, LANES)))) + peak_ref[b : b + 1, :]

    @pl.when(jnp.logical_not(good))
    def _():
        def body(pot):
            pot[...] = row_pot
            col_slow((own_hbm, other_hbm), cents_hbm, pot, wide_lse)

        pl.run_scoped(body, pltpu.VMEM(row_pot.shape, f32))
        for b in range(n_cent // LANES):
            small[b : b + 1, :] = to_row(wide_lse[b * LANES : (b + 1) * LANES, :])

    lse_ref[...] = jnp.broadcast_to(small[...][None], lse_ref.shape)


def prepare_kernel(peak_ref, col_ref, parts_ref, wide, pot_ref, row_ref):
    row_pot = local_order(-merge(parts_ref[...]))
    good = jnp.max(row_pot) <= LARGE_POT
    row_ref[...] = row_pot
    pot_ref[...] = jnp.where(good, jnp.exp(row_pot), row_pot)
    by_col = jnp.where(good, jnp.exp(peak_ref[...] + col_ref[...]), col_ref[...])
    for b in range(by_col.shape[0]):
        column = to_column(by_col[b : b + 1, :])
        wide[b * LANES : (b + 1) * LANES, :] = jnp.broadcast_to(column, (LANES, LANES))


def split(value):
    high = value.astype(bf16).astype(f32)
    middle = (value - high).astype(bf16).astype(f32)
    low = value - high - middle
    row = lax.broadcasted_iota(jnp.int32, (PAD, LANES), 0)
    rows = jnp.where(row == 0, high, jnp.where(row == 1, middle, jnp.where(row == 2, low, 0.0)))
    return rows.astype(bf16)


def joined(rows):
    rows = rows.astype(f32)
    return rows[0:1] + rows[1:2] + rows[2:3]


def product_kernel(shifts, *refs):
    t_ref, wide, pot_ref, row_ref, own_ref, other_ref, cents_hbm = refs[:7]
    outs, mass_ref, plan = refs[7:-2], refs[-2], refs[-1]
    groups, me = lax.axis_size("dp"), lax.axis_index("dp")
    n_own = own_ref.shape[0]
    n_doc = 2 * n_own
    half = own_ref.shape[1] // 2
    good = jnp.max(row_ref[...]) <= LARGE_POT
    starts = [pl.multiple_of(lax.rem(me + shift, groups) * BLOCK, BLOCK) for shift in shifts]

    def build(k):
        for r in range(0, BLOCK, LANES):
            rows = pl.ds(starts[k] + r, LANES)
            scale = wide[rows, :]
            for b in range(n_doc // LANES):
                at = slice(b * LANES, (b + 1) * LANES)
                plan[k, r : r + LANES, at] = (t_ref[rows, at] * scale * pot_ref[b : b + 1, :]).astype(bf16)

    def build_slow(k):
        def body(cents, x_ref):
            pltpu.sync_copy(cents_hbm.at[pl.ds(starts[k], BLOCK), :], cents)
            logits_block(cents[...], own_ref, x_ref, pl.ds(0, BLOCK))
            logits_block(cents[...], other_ref, x_ref, pl.ds(0, BLOCK), n_own)
            col = wide[pl.ds(starts[k], BLOCK), :]
            for b in range(n_doc // LANES):
                at = slice(b * LANES, (b + 1) * LANES)
                plan[k, :, at] = jnp.exp(x_ref[:, at] * SCALE + pot_ref[b : b + 1, :] + col).astype(bf16)

        pl.run_scoped(body, pltpu.VMEM((BLOCK, cents_hbm.shape[1]), bf16), pltpu.VMEM((BLOCK, n_doc), f32))

    def multiply(k):
        sums = jnp.dot(plan[k, :, :n_own], own_ref[...], preferred_element_type=f32)
        sums = sums + jnp.dot(plan[k, :, n_own:], other_ref[...], preferred_element_type=f32)
        masses = []
        for r in range(0, BLOCK, LANES):
            mass = fold(plan[k, r : r + LANES, :].astype(f32), jnp.add)
            masses.append(to_row(jnp.broadcast_to(jnp.sum(mass, axis=1, keepdims=True), (LANES, LANES))))
        if len(outs) == 2:
            for j, mass in enumerate(masses):
                mass_ref[2 * k + j : 2 * k + j + 1, :] = mass
            outs[0][k * BLOCK : (k + 1) * BLOCK, :] = sums[:, :half]
            outs[1][k * BLOCK : (k + 1) * BLOCK, :] = sums[:, half:]
        else:
            mass_ref[...] = jnp.concatenate(masses, axis=0)
            for j, mass in enumerate(masses):
                rows = slice(j * LANES, (j + 1) * LANES)
                send(outs[j], sums[rows, :half], [mass])
                outs[2 + j][...] = sums[rows, half:].astype(bf16)

    def all_of(build):
        build(0)
        for k in range(len(shifts)):
            if k + 1 < len(shifts):
                build(k + 1)
            multiply(k)

    @pl.when(good)
    def _():
        all_of(build)

    @pl.when(jnp.logical_not(good))
    def _():
        all_of(build_slow)


def send(out, sums, masses):
    n = sums.shape[0]
    out[:n, :] = sums.astype(bf16)
    out[n:, :] = jnp.zeros((PAD, sums.shape[1]), bf16)
    for j, mass in enumerate(masses):
        out[n:, j * LANES : (j + 1) * LANES] = split(mass)


def mass_of(came, j):
    return joined(came[came.shape[0] - PAD :, j * LANES : (j + 1) * LANES])


def add_kernel(part, sums_ref, mass_ref, right_ref, left_ref, right_out, left_out):
    for k, (came, out) in enumerate(((right_ref, right_out), (left_ref, left_out))):
        sums = sums_ref[k * BLOCK : (k + 1) * BLOCK, :]
        masses = [mass_ref[2 * k + j : 2 * k + j + 1, :] for j in range(2)]
        n = came.shape[0] - PAD
        if part:
            parts = [sums[:n, :], sums[n:, :]]
            parts[k] = parts[k] + came[:n, :].astype(f32)
            masses[k] = masses[k] + mass_of(came, 0)
            sums = jnp.concatenate(parts, axis=0)
        else:
            sums = sums + came[:n, :].astype(f32)
            masses = [mass + mass_of(came, j) for j, mass in enumerate(masses)]
        send(out, sums, masses)


def add_rest_kernel(part, sums_ref, right_ref, left_ref, right_out, left_out):
    for k, (came, out) in enumerate(((right_ref, right_out), (left_ref, left_out))):
        n = came.shape[0]
        first = k * BLOCK
        if part:
            for j in range(2):
                sums = sums_ref[first + j * n : first + (j + 1) * n, :]
                out[j * n : (j + 1) * n, :] = (sums + came[...].astype(f32) if j == k else sums).astype(bf16)
        else:
            out[...] = (sums_ref[first : first + BLOCK, :] + came[...].astype(f32)).astype(bf16)


def divide_kernel(sums_ref, mass_ref, right_ref, left_ref, out_ref, total_ref):
    for b in range(BLOCK // LANES):
        at = slice(b * LANES, (b + 1) * LANES)
        mass = mass_ref[b : b + 1, :] + (mass_of(right_ref, b) + mass_of(left_ref, b))
        total_ref[b : b + 1, :] = mass
        sums = sums_ref[at, :] + (right_ref[at, :].astype(f32) + left_ref[at, :].astype(f32))
        out_ref[at, :] = (sums / to_column(mass)).astype(bf16)


def divide_rest_kernel(sums_ref, mass_ref, right_ref, left_ref, out_ref):
    for b in range(BLOCK // LANES):
        at = slice(b * LANES, (b + 1) * LANES)
        sums = sums_ref[at, :] + (right_ref[at, :].astype(f32) + left_ref[at, :].astype(f32))
        out_ref[at, :] = (sums / to_column(mass_ref[b : b + 1, :])).astype(bf16)


def place_kernel(places, *refs):
    blocks, out, sems = refs[: len(places)], refs[-2], refs[-1]
    groups, me = lax.axis_size("dp"), lax.axis_index("dp")
    half = out.shape[1] // 2
    copies = []
    for at, (shift, row, column) in enumerate(places):
        start = pl.multiple_of(lax.rem(me + shift, groups) * BLOCK + row, LANES)
        to = out.at[pl.ds(start, blocks[at].shape[0]), pl.ds(column * half, half)]
        copy = pltpu.make_async_copy(blocks[at], to, sems.at[at])
        copy.start()
        copies.append(copy)
    for copy in copies:
        copy.wait()


IN_VMEM = pl.BlockSpec(memory_space=pltpu.VMEM)
IN_HBM = pl.BlockSpec(memory_space=pl.ANY)


def params(mib):
    return pltpu.CompilerParams(vmem_limit_bytes=mib * 2**20)


def shards(embeddings, centroids):
    groups, blocks = lax.axis_size("dp"), lax.axis_size("cent")
    own = gather(embeddings)
    other = on_cent(own, lambda y, x_at, core: (y, x_at, core + 1))
    n_doc, depth = CORES * own.shape[0], own.shape[1]
    n_cent = centroids.shape[0]
    log_ratio = math.log(n_doc * groups / (n_cent * blocks))
    row_shape = (n_doc // LANES, LANES)
    col_shape = (n_cent // LANES, LANES)
    shaped = jax.ShapeDtypeStruct
    by_group = shaped((groups, *col_shape), f32)
    by_block = shaped((blocks, *row_shape), f32)
    wide = pltpu.VMEM((n_cent, LANES), f32)

    raw = pl.pallas_call(
        own_kernel,
        out_shape=pltpu.VMEM((n_cent, own.shape[0]), f32),
        in_specs=[IN_VMEM] * 2,
        out_specs=IN_VMEM,
        compiler_params=params(10),
        cost_estimate=pl.CostEstimate(flops=2 * n_cent * own.shape[0] * depth, bytes_accessed=12 * 2**20, transcendentals=0),
    )(own, centroids)
    t, peak, lse = pl.pallas_call(
        first_kernel,
        out_shape=(pltpu.VMEM((n_cent, n_doc), f32), shaped(col_shape, f32), by_group),
        in_specs=[IN_VMEM] * 3,
        out_specs=(IN_VMEM,) * 3,
        scratch_shapes=[pltpu.VMEM((BLOCK, own.shape[0]), f32)] * 2 + [wide, wide, pltpu.VMEM(col_shape, f32)],
        compiler_params=params(16),
    )(raw, other, centroids)

    def rows(lse):
        parts = lax.all_to_all(lse, "dp", 0, 0)
        return pl.pallas_call(
            functools.partial(row_kernel, log_ratio),
            out_shape=(by_block, shaped(col_shape, f32)),
            in_specs=[IN_VMEM] * 3 + [IN_HBM] * 3,
            out_specs=(IN_VMEM, IN_VMEM),
            scratch_shapes=[wide, pltpu.VMEM((8, n_doc), f32), pltpu.VMEM(row_shape, f32)],
            compiler_params=params(20),
        )(t, peak, parts, own, other, centroids)

    def cols(lse):
        parts = lax.all_to_all(lse, "cent", 0, 0)
        return pl.pallas_call(
            col_kernel,
            out_shape=by_group,
            in_specs=[IN_VMEM] * 3 + [IN_HBM] * 3,
            out_specs=IN_VMEM,
            scratch_shapes=[wide, pltpu.VMEM(col_shape, f32)],
            compiler_params=params(20),
        )(t, peak, parts, own, other, centroids)

    lse, _ = rows(lse)
    lse = cols(lse)
    lse, col = rows(lse)
    parts = lax.all_to_all(lse, "cent", 0, 0)
    wide_col, pot, row = pl.pallas_call(
        prepare_kernel,
        out_shape=(pltpu.VMEM((n_cent, LANES), f32), shaped(row_shape, f32), shaped(row_shape, f32)),
        in_specs=[IN_VMEM] * 3,
        out_specs=(IN_VMEM,) * 3,
        compiler_params=params(4),
    )(peak, col, parts)

    far = groups // 2
    half = depth // 2
    free = pl.CostEstimate(flops=1, bytes_accessed=1, transcendentals=0)

    def message(rows):
        return shaped((rows, half), bf16)

    def move(x, by):
        return lax.ppermute(x, "dp", [(i, (i + by) % groups) for i in range(groups)])

    def products(shifts, outs, n_mass):
        return pl.pallas_call(
            functools.partial(product_kernel, shifts),
            out_shape=(*outs, shaped((n_mass, LANES), f32)),
            in_specs=[IN_VMEM] * 6 + [IN_HBM],
            out_specs=(IN_VMEM,) * (len(outs) + 1),
            scratch_shapes=[pltpu.VMEM((len(shifts), BLOCK, n_doc), bf16)],
            compiler_params=params(20),
            cost_estimate=free,
        )(t, wide_col, pot, row, own, other, centroids)

    def small_call(kernel, outs, *args):
        return pl.pallas_call(
            kernel,
            out_shape=outs,
            in_specs=[IN_VMEM] * len(args),
            out_specs=(IN_VMEM,) * len(outs) if isinstance(outs, tuple) else IN_VMEM,
            compiler_params=params(6),
            cost_estimate=free,
        )(*args)

    outs = (message(LANES + PAD),) * 2 + (message(LANES),) * 2
    right, left, rest_right, rest_left, _ = products([far], outs, 2)
    for s in range(1, far):
        right, left = move(right, 1), move(left, -1)
        rest_right, rest_left = move(rest_right, 1), move(rest_left, -1)
        outs = (shaped((2 * BLOCK, half), f32),) * 2
        sums, rest, mass = products([far - s, far + s], outs, 4)
        right, left = small_call(
            functools.partial(add_kernel, s == 1), (message(BLOCK + PAD),) * 2, sums, mass, right, left
        )
        rest_right, rest_left = small_call(
            functools.partial(add_rest_kernel, s == 1), (message(BLOCK),) * 2, rest, rest_right, rest_left
        )
    right, left = move(right, 1), move(left, -1)
    rest_right, rest_left = move(rest_right, 1), move(rest_left, -1)
    sums, rest, mass = products([0], (shaped((BLOCK, half), f32),) * 2, 2)
    new, total = small_call(
        divide_kernel, (message(BLOCK), shaped((2, LANES), f32)), sums, mass, right, left
    )
    rest_new = small_call(divide_rest_kernel, message(BLOCK), rest, total, rest_right, rest_left)

    near, last = [], []
    for column, block in enumerate((new, rest_new)):
        near.append((block, (0, 0, column)))
        held = {1: block, -1: block}
        for hop in range(1, far + 1):
            for by in (1, -1):
                if hop == far and by != (-1, 1)[column]:
                    continue
                held[by] = move(held[by], by)
                (last if hop == far else near).append((held[by], (-by * hop % groups, 0, column)))

    def put(blocks, *into):
        arrays, places = zip(*blocks)
        return pl.pallas_call(
            functools.partial(place_kernel, places),
            out_shape=shaped((n_cent, depth), bf16),
            in_specs=[IN_HBM] * (len(arrays) + len(into)),
            out_specs=IN_HBM,
            scratch_shapes=[pltpu.SemaphoreType.DMA((len(arrays),))],
            input_output_aliases={len(arrays): 0} if into else {},
            compiler_params=params(4),
            cost_estimate=free,
        )(*arrays, *into)

    return put(last, put(near))


def solution(mesh):
    placed = (P(("dp", "cent"), None), P("cent", None))
    return jax.shard_map(
        shards, mesh=mesh, in_specs=placed, out_specs=P("cent", None), check_vma=False
    )
```

```python
import functools
import math

import jax
import jax.numpy as jnp
from jax import lax
from jax.experimental import pallas as pl
from jax.experimental.pallas import tpu as pltpu
from jax.sharding import PartitionSpec as P

f32 = jnp.float32
bf16 = jnp.bfloat16
LANES = 128
BLOCK = 256
CHUNK = 16
SCALE = 3.0
EXP2_SCALE = SCALE * math.log2(math.e)
RING_Y, RING_X, CORES = 4, 4, 2
SMALL_SUM = 1e-20
LARGE_POT = 46.0
PAD = 16
NT = (((1,), (1,)), ((), ()))


def eye():
    rows = lax.broadcasted_iota(jnp.int32, (LANES, LANES), 0)
    cols = lax.broadcasted_iota(jnp.int32, (LANES, LANES), 1)
    return rows == cols


def to_row(column):
    return jnp.sum(jnp.where(eye(), column, 0.0), axis=0, keepdims=True)


def to_column(row):
    return jnp.sum(jnp.where(eye(), row, 0.0), axis=1, keepdims=True)


def fold(x, op):
    out = x[:, :LANES]
    for at in range(LANES, x.shape[1], LANES):
        out = op(out, x[:, at : at + LANES])
    return out


def merge(parts):
    peak = jnp.max(parts, axis=0)
    return peak + jnp.log(jnp.sum(jnp.exp(parts - peak[None]), axis=0))


def logits_block(cents, docs_ref, out_ref, rows, offset=0):
    width = 512
    for at in range(0, docs_ref.shape[0], width):
        out_ref[rows, offset + at : offset + at + width] = lax.dot_general(
            cents, docs_ref[at : at + width, :], NT, preferred_element_type=f32
        )


def place_on_cent():
    at = lax.axis_index("cent")
    return at // (RING_X * CORES), at // CORES % RING_X, at % CORES


def on_cent(x, place):
    pairs = []
    for y in range(RING_Y):
        for x_at in range(RING_X):
            for core in range(CORES):
                to_y, to_x, to_core = place(y, x_at, core)
                to = (to_y % RING_Y * RING_X + to_x % RING_X) * CORES + to_core % CORES
                pairs.append(((y * RING_X + x_at) * CORES + core, to))
    return lax.ppermute(x, "cent", pairs)


def along(x, first, by):
    return on_cent(x, lambda y, x_at, core: (y, x_at + by, core) if (core == 0) == first else (y + by, x_at, core))


def stack_kernel(first, own, before, after, across, out):
    y, x, core = place_on_cent()
    at = jnp.where((core == 0) == first, x, y)
    size = own.shape[0]
    for shift, block in ((0, own), (RING_X - 1, before), (1, after), (2, across)):
        start = pl.multiple_of(lax.rem(at + shift, RING_X) * size, size)
        out[pl.ds(start, size), :] = block[...]


def copy_kernel(from_ref, to_ref):
    pltpu.sync_copy(from_ref, to_ref)


def gather(own):
    for first in (True, False):
        moved = [along(own, first, by) for by in (1, -1, 2)]
        if first:
            own = pl.pallas_call(
                copy_kernel,
                out_shape=pltpu.VMEM(own.shape, bf16),
                in_specs=[IN_HBM],
                out_specs=IN_VMEM,
                cost_estimate=pl.CostEstimate(flops=1, bytes_accessed=1, transcendentals=0),
                compiler_params=params(4),
            )(own)
        own = pl.pallas_call(
            functools.partial(stack_kernel, first),
            out_shape=jax.ShapeDtypeStruct((RING_X * own.shape[0], own.shape[1]), bf16),
            in_specs=[IN_VMEM] * 4,
            out_specs=IN_VMEM,
            compiler_params=params(8),
        )(own, *moved)
    return own


def own_kernel(docs_ref, cents_ref, raw_ref):
    tall, width = 1024, 256

    def block(t, _):
        rows = pl.ds(pl.multiple_of(t * tall, tall), tall)
        for at in range(0, docs_ref.shape[0], width):
            raw_ref[rows, at : at + width] = lax.dot_general(
                cents_ref[rows, :], docs_ref[at : at + width, :], NT, preferred_element_type=f32
            )
        return 0

    lax.fori_loop(0, cents_ref.shape[0] // tall, block, 0)


def first_kernel(raw_ref, docs_ref, cents_ref, t_ref, peak_ref, lse_ref, even, odd, wide_peak, wide_lse, small):
    n_cent, n_own = raw_ref.shape
    n_blocks = n_cent // BLOCK
    tiles = n_own // LANES
    k = EXP2_SCALE

    def multiply(t, x_ref):
        start = pl.multiple_of(jnp.minimum(t, n_blocks - 1) * BLOCK, BLOCK)
        logits_block(cents_ref[pl.ds(start, BLOCK), :], docs_ref, x_ref, pl.ds(0, BLOCK))

    def finish(t, x_ref):
        for r in range(0, BLOCK, LANES):
            rows = pl.ds(pl.multiple_of(t * BLOCK + r, LANES), LANES)
            parts = [lambda b=b: raw_ref[rows, b * LANES : (b + 1) * LANES] for b in range(tiles)]
            parts += [lambda b=b: x_ref[r : r + LANES, b * LANES : (b + 1) * LANES] for b in range(tiles)]
            peak = parts[0]()
            for part in parts[1:]:
                peak = jnp.maximum(peak, part())
            peak = jnp.broadcast_to(jnp.max(peak, axis=1, keepdims=True), (LANES, LANES))
            total = jnp.zeros((LANES, LANES), f32)
            for b, part in enumerate(parts):
                e = jnp.exp2((part() - peak) * k)
                t_ref[rows, b * LANES : (b + 1) * LANES] = e
                total = total + e
            total = jnp.broadcast_to(jnp.sum(total, axis=1, keepdims=True), (LANES, LANES))
            wide_peak[rows, :] = peak * SCALE
            wide_lse[rows, :] = peak * SCALE + jnp.log(total)

    multiply(0, even)

    def pair(i, _):
        multiply(2 * i + 1, odd)
        finish(2 * i, even)
        multiply(2 * i + 2, even)
        finish(2 * i + 1, odd)
        return 0

    lax.fori_loop(0, n_blocks // 2, pair, 0)
    for b in range(n_cent // LANES):
        at = slice(b * LANES, (b + 1) * LANES)
        peak_ref[b : b + 1, :] = to_row(wide_peak[at, :])
        small[b : b + 1, :] = to_row(wide_lse[at, :])
    lse_ref[...] = jnp.broadcast_to(small[...][None], lse_ref.shape)


def common_order(b, n):
    _, _, core = place_on_cent()
    return lax.rem(b + core * (n // CORES), n)


def local_order(rows):
    _, _, core = place_on_cent()
    half = rows.shape[0] // CORES
    return jnp.where(core == 1, jnp.concatenate([rows[half:], rows[:half]], axis=0), rows)


def load_all(docs_hbm, cents_hbm, docs, cents):
    half = docs.shape[0] // 2
    pltpu.sync_copy(docs_hbm[0], docs.at[:half, :])
    pltpu.sync_copy(docs_hbm[1], docs.at[half:, :])
    pltpu.sync_copy(cents_hbm, cents)


def row_slow(docs_hbm, cents_hbm, col_wide, small):
    n_doc, n_cent = 2 * docs_hbm[0].shape[0], cents_hbm.shape[0]

    def body(docs, cents, x_ref, peak, total):
        load_all(docs_hbm, cents_hbm, docs, cents)
        peak[...] = jnp.full(peak.shape, -jnp.inf, f32)
        total[...] = jnp.zeros(total.shape, f32)

        def sweep(last):
            def block(t, _):
                start = pl.multiple_of(t * BLOCK, BLOCK)
                rows = pl.ds(start, BLOCK)
                logits_block(cents[rows, :], docs, x_ref, pl.ds(0, BLOCK))
                for at in range(0, n_doc, LANES):
                    y = x_ref[:, at : at + LANES] * SCALE + col_wide[rows, :]
                    here = peak[:, at : at + LANES]
                    if last:
                        total[:, at : at + LANES] += jnp.sum(jnp.exp(y - here), axis=0, keepdims=True)
                    else:
                        peak[:, at : at + LANES] = jnp.maximum(here, jnp.max(y, axis=0, keepdims=True))
                return 0

            lax.fori_loop(0, n_cent // BLOCK, block, 0)

        sweep(False)
        sweep(True)
        for b in range(n_doc // LANES):
            at = slice(b * LANES, (b + 1) * LANES)
            small[pl.ds(common_order(b, n_doc // LANES), 1), :] = peak[:, at] + jnp.log(total[:, at])

    pl.run_scoped(
        body,
        pltpu.VMEM((n_doc, cents_hbm.shape[1]), bf16),
        pltpu.VMEM(cents_hbm.shape, bf16),
        pltpu.VMEM((BLOCK, n_doc), f32),
        pltpu.VMEM((1, n_doc), f32),
        pltpu.VMEM((1, n_doc), f32),
    )


def row_kernel(log_ratio, t_ref, peak_ref, parts_ref, own_hbm, other_hbm, cents_hbm, lse_ref, col_ref, wide, acc, small):
    n_cent, n_doc = t_ref.shape
    col = log_ratio - merge(parts_ref[...])
    col_ref[...] = col
    factor = jnp.exp(peak_ref[...] + col)
    for b in range(n_cent // LANES):
        column = to_column(factor[b : b + 1, :])
        wide[b * LANES : (b + 1) * LANES, :] = jnp.broadcast_to(column, (LANES, LANES))
    acc[...] = jnp.zeros(acc.shape, f32)
    step = 64

    def block(t, _):
        start = pl.multiple_of(t * step, step)
        scale = wide[pl.ds(start, step), :]
        for at in range(0, n_doc, LANES):
            x = t_ref[pl.ds(start, step), at : at + LANES] * scale
            part = x[:8, :]
            for r in range(8, step, 8):
                part = part + x[r : r + 8, :]
            acc[:, at : at + LANES] += part
        return 0

    lax.fori_loop(0, n_cent // step, block, 0)
    least = jnp.full((1, LANES), jnp.inf, f32)
    for b in range(n_doc // LANES):
        total = jnp.sum(acc[:, b * LANES : (b + 1) * LANES], axis=0, keepdims=True)
        least = jnp.minimum(least, total)
        small[pl.ds(common_order(b, n_doc // LANES), 1), :] = jnp.log(total)

    @pl.when(jnp.logical_not(jnp.min(least) >= SMALL_SUM))
    def _():
        for b in range(n_cent // LANES):
            column = to_column(col[b : b + 1, :])
            wide[b * LANES : (b + 1) * LANES, :] = jnp.broadcast_to(column, (LANES, LANES))
        row_slow((own_hbm, other_hbm), cents_hbm, wide, small)

    lse_ref[...] = jnp.broadcast_to(small[...][None], lse_ref.shape)


def col_slow(docs_hbm, cents_hbm, row_pot, wide_lse):
    n_doc, n_cent = 2 * docs_hbm[0].shape[0], cents_hbm.shape[0]

    def body(docs, cents, x_ref):
        load_all(docs_hbm, cents_hbm, docs, cents)

        def block(t, _):
            start = pl.multiple_of(t * BLOCK, BLOCK)
            logits_block(cents[pl.ds(start, BLOCK), :], docs, x_ref, pl.ds(0, BLOCK))

            def chunk(c, _):
                at = pl.multiple_of(c * CHUNK, CHUNK)
                y = [
                    x_ref[pl.ds(at, CHUNK), b * LANES : (b + 1) * LANES] * SCALE + row_pot[b : b + 1, :]
                    for b in range(n_doc // LANES)
                ]
                peak = jnp.max(functools.reduce(jnp.maximum, y), axis=1, keepdims=True)
                total = jnp.sum(sum(jnp.exp(part - peak) for part in y), axis=1, keepdims=True)
                value = peak + jnp.log(total)
                wide_lse[pl.ds(start + at, CHUNK), :] = jnp.broadcast_to(value, (CHUNK, LANES))
                return 0

            return lax.fori_loop(0, BLOCK // CHUNK, chunk, 0)

        lax.fori_loop(0, n_cent // BLOCK, block, 0)

    pl.run_scoped(
        body,
        pltpu.VMEM((n_doc, cents_hbm.shape[1]), bf16),
        pltpu.VMEM(cents_hbm.shape, bf16),
        pltpu.VMEM((BLOCK, n_doc), f32),
    )


def col_kernel(t_ref, peak_ref, parts_ref, own_hbm, other_hbm, cents_hbm, lse_ref, wide_lse, small):
    n_cent, n_doc = t_ref.shape
    row_pot = local_order(-merge(parts_ref[...]))
    factor = jnp.exp(row_pot)
    step = 64

    def block(t, _):
        start = pl.multiple_of(t * step, step)
        total = jnp.zeros((step, LANES), f32)
        for b in range(n_doc // LANES):
            total = total + t_ref[pl.ds(start, step), b * LANES : (b + 1) * LANES] * factor[b : b + 1, :]
        wide_lse[pl.ds(start, step), :] = total
        return 0

    lax.fori_loop(0, n_cent // step, block, 0)
    good = jnp.max(row_pot) <= LARGE_POT
    for b in range(n_cent // LANES):
        at = slice(b * LANES, (b + 1) * LANES)
        total = jnp.sum(wide_lse[at, :], axis=1, keepdims=True)
        small[b : b + 1, :] = jnp.log(to_row(jnp.broadcast_to(total, (LANES, LANES)))) + peak_ref[b : b + 1, :]

    @pl.when(jnp.logical_not(good))
    def _():
        def body(pot):
            pot[...] = row_pot
            col_slow((own_hbm, other_hbm), cents_hbm, pot, wide_lse)

        pl.run_scoped(body, pltpu.VMEM(row_pot.shape, f32))
        for b in range(n_cent // LANES):
            small[b : b + 1, :] = to_row(wide_lse[b * LANES : (b + 1) * LANES, :])

    lse_ref[...] = jnp.broadcast_to(small[...][None], lse_ref.shape)


def prepare_kernel(peak_ref, col_ref, parts_ref, wide, pot_ref, row_ref):
    row_pot = local_order(-merge(parts_ref[...]))
    good = jnp.max(row_pot) <= LARGE_POT
    row_ref[...] = row_pot
    pot_ref[...] = jnp.where(good, jnp.exp(row_pot), row_pot)
    by_col = jnp.where(good, jnp.exp(peak_ref[...] + col_ref[...]), col_ref[...])
    for b in range(by_col.shape[0]):
        column = to_column(by_col[b : b + 1, :])
        wide[b * LANES : (b + 1) * LANES, :] = jnp.broadcast_to(column, (LANES, LANES))


def split(value):
    high = value.astype(bf16).astype(f32)
    middle = (value - high).astype(bf16).astype(f32)
    low = value - high - middle
    row = lax.broadcasted_iota(jnp.int32, (PAD, LANES), 0)
    rows = jnp.where(row == 0, high, jnp.where(row == 1, middle, jnp.where(row == 2, low, 0.0)))
    return rows.astype(bf16)


def joined(rows):
    rows = rows.astype(f32)
    return rows[0:1] + rows[1:2] + rows[2:3]


def product_kernel(shifts, ready, *refs):
    t_ref, wide, pot_ref, row_ref, own_ref, other_ref, cents_hbm = refs[:7]
    outs, mass_ref, plan = refs[7:-2], refs[-2], refs[-1]
    groups, me = lax.axis_size("dp"), lax.axis_index("dp")
    n_own = own_ref.shape[0]
    n_doc = 2 * n_own
    half = own_ref.shape[1] // 2
    good = jnp.max(row_ref[...]) <= LARGE_POT
    starts = [pl.multiple_of(lax.rem(me + shift, groups) * BLOCK, BLOCK) for shift in shifts]

    def build(k):
        for r in range(0, BLOCK, LANES):
            rows = pl.ds(starts[k] + r, LANES)
            scale = wide[rows, :]
            for b in range(n_doc // LANES):
                at = slice(b * LANES, (b + 1) * LANES)
                plan[k, r : r + LANES, at] = (t_ref[rows, at] * scale * pot_ref[b : b + 1, :]).astype(bf16)

    def build_slow(k):
        def body(cents, x_ref):
            pltpu.sync_copy(cents_hbm.at[pl.ds(starts[k], BLOCK), :], cents)
            logits_block(cents[...], own_ref, x_ref, pl.ds(0, BLOCK))
            logits_block(cents[...], other_ref, x_ref, pl.ds(0, BLOCK), n_own)
            col = wide[pl.ds(starts[k], BLOCK), :]
            for b in range(n_doc // LANES):
                at = slice(b * LANES, (b + 1) * LANES)
                plan[k, :, at] = jnp.exp(x_ref[:, at] * SCALE + pot_ref[b : b + 1, :] + col).astype(bf16)

        pl.run_scoped(body, pltpu.VMEM((BLOCK, cents_hbm.shape[1]), bf16), pltpu.VMEM((BLOCK, n_doc), f32))

    def multiply(k):
        sums = jnp.dot(plan[k, :, :n_own], own_ref[...], preferred_element_type=f32)
        sums = sums + jnp.dot(plan[k, :, n_own:], other_ref[...], preferred_element_type=f32)
        masses = []
        for r in range(0, BLOCK, LANES):
            mass = fold(plan[k, r : r + LANES, :].astype(f32), jnp.add)
            masses.append(to_row(jnp.broadcast_to(jnp.sum(mass, axis=1, keepdims=True), (LANES, LANES))))
        if not ready:
            for j, mass in enumerate(masses):
                mass_ref[2 * k + j : 2 * k + j + 1, :] = mass
            outs[0][k * BLOCK : (k + 1) * BLOCK, :] = sums[:, :half]
            outs[1][k * BLOCK : (k + 1) * BLOCK, :] = sums[:, half:]
        else:
            send(outs[0], sums[:, :half], masses)
            outs[1][...] = sums[:, half:].astype(bf16)
            mass_ref[...] = jnp.concatenate(masses, axis=0)

    def all_of(build):
        build(0)
        for k in range(len(shifts)):
            if k + 1 < len(shifts):
                build(k + 1)
            multiply(k)

    @pl.when(good)
    def _():
        all_of(build)

    @pl.when(jnp.logical_not(good))
    def _():
        all_of(build_slow)


def send(out, sums, masses):
    n = sums.shape[0]
    out[:n, :] = sums.astype(bf16)
    out[n:, :] = jnp.zeros((PAD, sums.shape[1]), bf16)
    for j, mass in enumerate(masses):
        out[n:, j * LANES : (j + 1) * LANES] = split(mass)


def mass_of(came, j):
    return joined(came[came.shape[0] - PAD :, j * LANES : (j + 1) * LANES])


def add_kernel(k, sums_ref, mass_ref, *refs):
    sums = sums_ref[k * BLOCK : (k + 1) * BLOCK, :]
    masses = [mass_ref[2 * k + j : 2 * k + j + 1, :] for j in range(2)]
    for came in refs[:-1]:
        sums = sums + came[:BLOCK, :].astype(f32)
        masses = [mass + mass_of(came, j) for j, mass in enumerate(masses)]
    send(refs[-1], sums, masses)


def add_rest_kernel(k, sums_ref, *refs):
    sums = sums_ref[k * BLOCK : (k + 1) * BLOCK, :]
    for came in refs[:-1]:
        sums = sums + came[...].astype(f32)
    refs[-1][...] = sums.astype(bf16)


def divide_kernel(sums_ref, mass_ref, right_ref, left_ref, out_ref, total_ref):
    for b in range(BLOCK // LANES):
        at = slice(b * LANES, (b + 1) * LANES)
        mass = mass_ref[b : b + 1, :] + (mass_of(right_ref, b) + mass_of(left_ref, b))
        total_ref[b : b + 1, :] = mass
        sums = sums_ref[at, :] + (right_ref[at, :].astype(f32) + left_ref[at, :].astype(f32))
        out_ref[at, :] = (sums / to_column(mass)).astype(bf16)


def divide_rest_kernel(sums_ref, mass_ref, right_ref, left_ref, out_ref):
    for b in range(BLOCK // LANES):
        at = slice(b * LANES, (b + 1) * LANES)
        sums = sums_ref[at, :] + (right_ref[at, :].astype(f32) + left_ref[at, :].astype(f32))
        out_ref[at, :] = (sums / to_column(mass_ref[b : b + 1, :])).astype(bf16)


def place_kernel(places, *refs):
    blocks, out, sems = refs[: len(places)], refs[-2], refs[-1]
    groups, me = lax.axis_size("dp"), lax.axis_index("dp")
    half = out.shape[1] // 2
    copies = []
    for at, (shift, row, column) in enumerate(places):
        start = pl.multiple_of(lax.rem(me + shift, groups) * BLOCK + row, LANES)
        to = out.at[pl.ds(start, blocks[at].shape[0]), pl.ds(column * half, half)]
        copy = pltpu.make_async_copy(blocks[at], to, sems.at[at])
        copy.start()
        copies.append(copy)
    for copy in copies:
        copy.wait()


IN_VMEM = pl.BlockSpec(memory_space=pltpu.VMEM)
IN_HBM = pl.BlockSpec(memory_space=pl.ANY)


def params(mib):
    return pltpu.CompilerParams(vmem_limit_bytes=mib * 2**20)


def shards(embeddings, centroids):
    groups, blocks = lax.axis_size("dp"), lax.axis_size("cent")
    own = gather(embeddings)
    other = on_cent(own, lambda y, x_at, core: (y, x_at, core + 1))
    n_doc, depth = CORES * own.shape[0], own.shape[1]
    n_cent = centroids.shape[0]
    log_ratio = math.log(n_doc * groups / (n_cent * blocks))
    row_shape = (n_doc // LANES, LANES)
    col_shape = (n_cent // LANES, LANES)
    shaped = jax.ShapeDtypeStruct
    by_group = shaped((groups, *col_shape), f32)
    by_block = shaped((blocks, *row_shape), f32)
    wide = pltpu.VMEM((n_cent, LANES), f32)

    raw = pl.pallas_call(
        own_kernel,
        out_shape=pltpu.VMEM((n_cent, own.shape[0]), f32),
        in_specs=[IN_VMEM] * 2,
        out_specs=IN_VMEM,
        compiler_params=params(10),
        cost_estimate=pl.CostEstimate(flops=2 * n_cent * own.shape[0] * depth, bytes_accessed=12 * 2**20, transcendentals=0),
    )(own, centroids)
    t, peak, lse = pl.pallas_call(
        first_kernel,
        out_shape=(pltpu.VMEM((n_cent, n_doc), f32), shaped(col_shape, f32), by_group),
        in_specs=[IN_VMEM] * 3,
        out_specs=(IN_VMEM,) * 3,
        scratch_shapes=[pltpu.VMEM((BLOCK, own.shape[0]), f32)] * 2 + [wide, wide, pltpu.VMEM(col_shape, f32)],
        compiler_params=params(16),
    )(raw, other, centroids)

    def rows(lse):
        parts = lax.all_to_all(lse, "dp", 0, 0)
        return pl.pallas_call(
            functools.partial(row_kernel, log_ratio),
            out_shape=(by_block, shaped(col_shape, f32)),
            in_specs=[IN_VMEM] * 3 + [IN_HBM] * 3,
            out_specs=(IN_VMEM, IN_VMEM),
            scratch_shapes=[wide, pltpu.VMEM((8, n_doc), f32), pltpu.VMEM(row_shape, f32)],
            compiler_params=params(20),
        )(t, peak, parts, own, other, centroids)

    def cols(lse):
        parts = lax.all_to_all(lse, "cent", 0, 0)
        return pl.pallas_call(
            col_kernel,
            out_shape=by_group,
            in_specs=[IN_VMEM] * 3 + [IN_HBM] * 3,
            out_specs=IN_VMEM,
            scratch_shapes=[wide, pltpu.VMEM(col_shape, f32)],
            compiler_params=params(20),
        )(t, peak, parts, own, other, centroids)

    lse, _ = rows(lse)
    lse = cols(lse)
    lse, col = rows(lse)
    parts = lax.all_to_all(lse, "cent", 0, 0)
    wide_col, pot, row = pl.pallas_call(
        prepare_kernel,
        out_shape=(pltpu.VMEM((n_cent, LANES), f32), shaped(row_shape, f32), shaped(row_shape, f32)),
        in_specs=[IN_VMEM] * 3,
        out_specs=(IN_VMEM,) * 3,
        compiler_params=params(4),
    )(peak, col, parts)

    far = groups // 2
    half = depth // 2
    free = pl.CostEstimate(flops=1, bytes_accessed=1, transcendentals=0)

    def message(rows):
        return shaped((rows, half), bf16)

    def move(x, by):
        return lax.ppermute(x, "dp", [(i, (i + by) % groups) for i in range(groups)])

    def products(shifts, outs, n_mass, ready=False):
        return pl.pallas_call(
            functools.partial(product_kernel, shifts, ready),
            out_shape=(*outs, shaped((n_mass, LANES), f32)),
            in_specs=[IN_VMEM] * 6 + [IN_HBM],
            out_specs=(IN_VMEM,) * (len(outs) + 1),
            scratch_shapes=[pltpu.VMEM((len(shifts), BLOCK, n_doc), bf16)],
            compiler_params=params(20),
            cost_estimate=free,
        )(t, wide_col, pot, row, own, other, centroids)

    def small_call(kernel, outs, *args):
        return pl.pallas_call(
            kernel,
            out_shape=outs,
            in_specs=[IN_VMEM] * len(args),
            out_specs=(IN_VMEM,) * len(outs) if isinstance(outs, tuple) else IN_VMEM,
            compiler_params=params(6),
            cost_estimate=free,
        )(*args)

    right, rest_left, _ = products([far], (message(BLOCK + PAD), message(BLOCK)), 2, ready=True)
    came, rest_came = {0: move(right, 1)}, {1: move(rest_left, -1)}
    for s in range(1, far):
        outs = (shaped((2 * BLOCK, half), f32),) * 2
        sums, rest, mass = products([far - s, far + s], outs, 4)
        for k, by in enumerate((1, -1)):
            arrived = [came[k]] if k in came else []
            out = small_call(functools.partial(add_kernel, k), message(BLOCK + PAD), sums, mass, *arrived)
            came[k] = move(out, by)
            arrived = [rest_came[k]] if k in rest_came else []
            out = small_call(functools.partial(add_rest_kernel, k), message(BLOCK), rest, *arrived)
            rest_came[k] = move(out, by)
    sums, rest, mass = products([0], (shaped((BLOCK, half), f32),) * 2, 2)
    new, total = small_call(
        divide_kernel, (message(BLOCK), shaped((2, LANES), f32)), sums, mass, came[0], came[1]
    )
    rest_new = small_call(divide_rest_kernel, message(BLOCK), rest, total, rest_came[0], rest_came[1])

    near, last = [], []
    for column, block in enumerate((new, rest_new)):
        near.append((block, (0, 0, column)))
        held = {1: block, -1: block}
        for hop in range(1, far + 1):
            for by in (1, -1):
                if hop == far and by != (-1, 1)[column]:
                    continue
                held[by] = move(held[by], by)
                (last if hop == far else near).append((held[by], (-by * hop % groups, 0, column)))

    def put(blocks, *into):
        arrays, places = zip(*blocks)
        return pl.pallas_call(
            functools.partial(place_kernel, places),
            out_shape=shaped((n_cent, depth), bf16),
            in_specs=[IN_HBM] * (len(arrays) + len(into)),
            out_specs=IN_HBM,
            scratch_shapes=[pltpu.SemaphoreType.DMA((len(arrays),))],
            input_output_aliases={len(arrays): 0} if into else {},
            compiler_params=params(4),
            cost_estimate=free,
        )(*arrays, *into)

    return put(last, put(near))


def solution(mesh):
    placed = (P(("dp", "cent"), None), P("cent", None))
    return jax.shard_map(
        shards, mesh=mesh, in_specs=placed, out_specs=P("cent", None), check_vma=False
    )
```
